256 devices in a mesh: gx: 8 (over y, core), gy: 4 (over z_lo), grp: 8 (over x, z_hi).
Axes of the slice: x: 4, y: 4, z: 8 (z_hi: 2, z_lo: 4; z = z_hi * 4 + z_lo), core: 2. Of those that a mesh axis runs over, the one named last changes fastest.
Arguments:
- pressure: float32 [128, 64, 8192], P('gx', 'gy', 'grp'), may hold values from -6 to 6
- pressure_old: float32 [128, 64, 8192], P('gx', 'gy', 'grp'), may hold values from -6 to 6
- accumulation: float32 [128, 64, 8192], P('gx', 'gy', 'grp'), may hold values from 0.05 to 1
- permeability: float32 [3, 128, 64, 8192], P(None, 'gx', 'gy', 'grp'), may hold values from 0.05 to 20
- comp_block: int32 [8, 4, 8, 128], P('gx', 'gy', 'grp'), may hold values from 0 to 2047, as said below
- comp_owner: int32 [8, 4, 8, 128, 1], P('gx', 'gy', 'grp'), may hold values from 0 to 63; in each aligned block of 128 rows (0 to 127, 128 to 255, ..., all dimensions but the last counted through in order) at most 4 rows name the same one
- comp_well: int32 [8, 4, 8, 128], P('gx', 'gy', 'grp'), may hold values from 0 to 7
- comp_wi: float32 [8, 4, 8, 128, 128], P('gx', 'gy', 'grp'), may hold values from 0.5 to 4
- well_rate: float32 [8, 4, 8, 8], P('gx', 'gy', 'grp'), may hold values from -4096 to 4096
- well_storage: float32 [8, 4, 8, 8], P('gx', 'gy', 'grp'), may hold values from 256 to 4096
- well_bhp_old: float32 [8, 4, 8, 8], P('gx', 'gy', 'grp'), may hold values from -6 to 6
Outputs:
- pressure_new: float32 [128, 64, 8192], P('gx', 'gy', 'grp')
- well_bhp: float32 [8, 4, 8, 8], P('gx', 'gy', 'grp')
The draws below stay inside these ranges and needn't reach their ends.
Inputs may be any that keep to these rules, and one draw needn't show every extreme that they name: `comp_block`: the 128 block numbers of one device are distinct. `comp_owner`: owner index o along gx and grp together (gx slowest), in the completion's own gy row; among the completions of one device at most 4 name one owner, a bound that some block reaches.
All inputs are finite; a program needn't handle non-finite values.
Results may differ from the reference program's by a relative error of at most 0.00022.
Values sent between devices are 32-bit elements; how exact they have to be, the bound alone decides.
A program may use at most 128 MiB of HBM per device.

```python
import math
import jax
import jax.numpy as jnp
import numpy as np

CX = 16
CY = 16
CZ = 1024
COMP_DEV = 128
WELLS_DEV = 8
CCX = 4
CCY = 4
CCZ = 8
SWEEPS = 4
COARSE_ITERS = 8
NX = 128
NY = 64
NZ = 8192
BLK_DEV = 2048
CAP = 4
N_GX = 8
N_GY = 4
N_GRP = 8


def draw_comp_block(key, part):
    key = jax.random.fold_in(key, 7)
    scores = jax.random.randint(key, (N_GX, N_GY, N_GRP, BLK_DEV), 0, 4096)
    scores = scores * BLK_DEV + jnp.arange(BLK_DEV, dtype=jnp.int32)
    return jnp.argsort(scores, axis=-1)[..., :COMP_DEV].astype(jnp.int32)


def with_ends(drawn, rng, low, high):
    shape = drawn.shape
    place = [jax.random.randint(jax.random.fold_in(rng, axis), (), 0, shape[axis]) for axis in range(len(shape))]
    drawn = drawn.at[tuple(place)].set(low)
    longest = shape.index(max(shape))
    place[longest] = (place[longest] + 1) % shape[longest]
    return drawn.at[tuple(place)].set(high)


def level_of(key, dims, split, least, high):
    level = 1.0
    for dim, shards_of in split:
        steps = jax.random.uniform(jax.random.fold_in(jax.random.fold_in(key, 6), dim), (shards_of,), jnp.float32, least / len(split), high / len(split))
        level = level * jnp.repeat(jnp.exp(steps), dims[dim] // shards_of).reshape((-1,) + (1,) * (len(dims) - 1 - dim))
    return level


def routed_block(own_key, own, number, rows, amount, top, limit, skew):
    sequence = jax.random.permutation(own_key, amount)
    crowded, usual = shares(amount, rows * top, limit, skew, True), shares(amount, rows * top, limit, skew, False)
    places = jnp.arange(amount)

    def named(sizes, turn):
        used = int((sizes > 0).sum())
        fixed = max(1, used // 4)
        passed = fixed + (places - fixed + turn * (used - fixed)) % max(1, amount - fixed)
        return jnp.zeros((amount,), jnp.int32).at[sequence[jnp.where(places < fixed, places, passed)]].set(jnp.asarray(sizes, jnp.int32))

    sizes = jnp.where(number % 4 == 0, named(crowded, number // 4), named(usual, number - number // 4 - 1))
    mixed = jax.random.permutation(jax.random.fold_in(own, 3), amount)
    source_of, receiver = mixed[0:amount // 2 * 2:2], mixed[1:amount // 2 * 2:2]
    slack = jnp.minimum(sizes[source_of] - 1, limit - sizes[receiver]) // 2
    slack = jnp.where((source_of == sequence[0]) | (receiver == sequence[0]) | (sizes[receiver] == 0), 0, jnp.maximum(slack, 0))
    passed = jax.random.randint(jax.random.fold_in(own, 4), (amount // 2,), 0, 1 << 20) % (slack + 1)
    sizes = sizes.at[source_of].add(-passed).at[receiver].add(passed)
    items = jnp.searchsorted(jnp.cumsum(sizes), jnp.arange(rows * top), side="right").astype(jnp.int32)
    grid = items.reshape(top, rows).T
    grid = grid[jax.random.permutation(jax.random.fold_in(own, 1), rows)]
    turn = jax.random.randint(jax.random.fold_in(own, 2), (rows, 1), 0, top)
    return jnp.take_along_axis(grid, (jnp.arange(top)[None, :] + turn) % top, axis=1)


def shares(number_of, total, reach, lean, full):
    loads = [(1 << 20) // math.isqrt(grade ** lean) + 1 for grade in range(1, number_of + 1)]
    largest = reach if full else min(reach, max(-(-total // number_of), total * loads[0] // sum(loads)))
    least = 1 if total - largest >= number_of - 1 else 0
    holding, rest = [largest] + [least] * (number_of - 1), total - largest - least * (number_of - 1)
    while rest > 0:
        free = [i for i in range(1, number_of) if holding[i] < largest] or [i for i in range(1, number_of) if holding[i] < reach]
        mass, budget = sum([loads[i] for i in free]), rest
        for i in free:
            more = min(reach - holding[i], max(1, budget * loads[i] // mass), rest)
            holding[i] = holding[i] + more
            rest = rest - more
    return np.array(holding)


def noise(own_key, extent, spread, most, split=(), kind=jnp.bfloat16):
    values = spread * jax.random.normal(own_key, extent, jnp.float32)
    if split:
        values = values * level_of(own_key, extent, split, -0.22, 0.18)
    return jnp.clip(values, -most, most).astype(kind)


def setup_inputs(seed: int = 0) -> dict:
    arg_keys = jax.random.split(jax.random.key(seed), 12)
    pressure = noise(arg_keys[0], (NX, NY, NZ), 1.0, 6.0, ((0, 8), (1, 4), (2, 8)), jnp.float32)
    pressure_old = noise(arg_keys[1], (NX, NY, NZ), 1.0, 6.0, ((0, 8), (1, 4), (2, 8)), jnp.float32)
    accumulation = jnp.clip(jnp.exp(math.log(1.0) - 2.9957323 * jax.random.uniform(arg_keys[2], (NX, NY, NZ), jnp.float32) ** level_of(arg_keys[2], (NX, NY, NZ), ((0, 8), (1, 4), (2, 8)), -0.2, 0.2)), 0.05, 1.0)
    permeability = jnp.clip(jnp.exp(math.log(20.0) - 5.9914645 * jax.random.uniform(arg_keys[3], (3, NX, NY, NZ), jnp.float32) ** level_of(arg_keys[3], (3, NX, NY, NZ), ((1, 8), (2, 4), (3, 8)), -0.2, 0.2)), 0.05, 20.0)
    comp_block = draw_comp_block(jax.random.fold_in(arg_keys[11], 71), 0)
    comp_owner_keys = jax.random.split(jax.random.fold_in(arg_keys[5], 1), N_GX * N_GY * N_GRP * COMP_DEV // COMP_DEV)
    comp_owner_turns = jax.random.permutation(jax.random.fold_in(arg_keys[5], 3), N_GX * N_GY * N_GRP * COMP_DEV // COMP_DEV)
    comp_owner = jax.vmap(lambda own, number: routed_block(jax.random.fold_in(arg_keys[5], 2), own, number, COMP_DEV, N_GX * N_GRP, 1, CAP, 2))(comp_owner_keys, comp_owner_turns).reshape((N_GX, N_GY, N_GRP, COMP_DEV, 1))
    comp_well = with_ends(jax.random.randint(arg_keys[6], (N_GX, N_GY, N_GRP, COMP_DEV), 0, WELLS_DEV), jax.random.fold_in(arg_keys[6], 1), 0, WELLS_DEV - 1).astype(jnp.int32)
    comp_wi = jnp.clip(jnp.exp(math.log(4.0) - 2.0794415 * jax.random.uniform(arg_keys[7], (N_GX, N_GY, N_GRP, COMP_DEV, 128), jnp.float32) ** level_of(arg_keys[7], (N_GX, N_GY, N_GRP, COMP_DEV, 128), ((0, 8), (1, 4), (2, 8)), -0.2, 0.2)), 0.5, 4.0)
    well_rate = jnp.clip(jax.random.uniform(arg_keys[8], (N_GX, N_GY, N_GRP, WELLS_DEV), jnp.float32, -4096.0, 4096.0) * level_of(arg_keys[8], (N_GX, N_GY, N_GRP, WELLS_DEV), ((0, 8), (1, 4), (2, 8)), -0.4, 0.0), -4096.0, 4096.0)
    well_storage = jnp.clip(jnp.exp(math.log(4096.0) - 2.7725887 * jax.random.uniform(arg_keys[9], (N_GX, N_GY, N_GRP, WELLS_DEV), jnp.float32) ** level_of(arg_keys[9], (N_GX, N_GY, N_GRP, WELLS_DEV), ((0, 8), (1, 4), (2, 8)), -0.2, 0.2)), 256.0, 4096.0)
    well_bhp_old = noise(arg_keys[10], (N_GX, N_GY, N_GRP, WELLS_DEV), 1.0, 6.0, ((0, 8), (1, 4), (2, 8)), jnp.float32)
    return {"pressure": pressure, "pressure_old": pressure_old, "accumulation": accumulation, "permeability": permeability, "comp_block": comp_block, "comp_owner": comp_owner, "comp_well": comp_well, "comp_wi": comp_wi, "well_rate": well_rate, "well_storage": well_storage, "well_bhp_old": well_bhp_old}


RELAXATION = 0.7


def harmonic(lower_k, upper_k):
    return 2.0 * lower_k * upper_k / (lower_k + upper_k)


def face_transmissibility(padded_perm):
    face_x = harmonic(padded_perm[0, :-1, 1:-1, 1:-1], padded_perm[0, 1:, 1:-1, 1:-1])
    face_y = harmonic(padded_perm[1, 1:-1, :-1, 1:-1], padded_perm[1, 1:-1, 1:, 1:-1])
    face_z = harmonic(padded_perm[2, 1:-1, 1:-1, :-1], padded_perm[2, 1:-1, 1:-1, 1:])
    return face_x, face_y, face_z


def neighbour_sum(padded, face_x, face_y, face_z):
    summed = face_x[1:] * padded[2:, 1:-1, 1:-1] + face_x[:-1] * padded[:-2, 1:-1, 1:-1]
    summed = summed + face_y[:, 1:] * padded[1:-1, 2:, 1:-1] + face_y[:, :-1] * padded[1:-1, :-2, 1:-1]
    summed = summed + face_z[:, :, 1:] * padded[1:-1, 1:-1, 2:] + face_z[:, :, :-1] * padded[1:-1, 1:-1, :-2]
    return summed


def face_total(face_x, face_y, face_z):
    return face_x[1:] + face_x[:-1] + face_y[:, 1:] + face_y[:, :-1] + face_z[:, :, 1:] + face_z[:, :, :-1]


def aggregate(values, agg_x, agg_y, agg_z):
    extent_x, extent_y, extent_z = values.shape
    shaped = values.reshape(extent_x // agg_x, agg_x, extent_y // agg_y, agg_y, extent_z // agg_z, agg_z)
    return shaped.sum(axis=(1, 3, 5))


def coarse_faces(face_x, face_y, face_z, agg_x, agg_y, agg_z):
    cells_x = (face_x.shape[0] - 1) // agg_x
    cells_y = (face_y.shape[1] - 1) // agg_y
    cells_z = (face_z.shape[2] - 1) // agg_z

    def plane_x(faces):
        return faces.reshape(cells_x, cells_y, agg_y, cells_z, agg_z).sum(axis=(2, 4))

    def plane_y(faces):
        return faces.reshape(cells_x, agg_x, cells_y, cells_z, agg_z).sum(axis=(1, 4))

    def plane_z(faces):
        return faces.reshape(cells_x, agg_x, cells_y, agg_y, cells_z).sum(axis=(1, 3))

    x_high = plane_x(face_x[agg_x::agg_x])
    x_low = plane_x(face_x[:-1:agg_x])
    y_high = plane_y(face_y[:, agg_y::agg_y])
    y_low = plane_y(face_y[:, :-1:agg_y])
    z_high = plane_z(face_z[:, :, agg_z::agg_z])
    z_low = plane_z(face_z[:, :, :-1:agg_z])
    return x_high, x_low, y_high, y_low, z_high, z_low


def coarse_sweep(current, padded, coarse_rhs, coarse_diag, faces):
    x_high, x_low, y_high, y_low, z_high, z_low = faces
    summed = x_high * padded[2:, 1:-1, 1:-1] + x_low * padded[:-2, 1:-1, 1:-1]
    summed = summed + y_high * padded[1:-1, 2:, 1:-1] + y_low * padded[1:-1, :-2, 1:-1]
    summed = summed + z_high * padded[1:-1, 1:-1, 2:] + z_low * padded[1:-1, 1:-1, :-2]
    return current + RELAXATION * (coarse_rhs - (coarse_diag * current - summed)) / coarse_diag


def to_blocks(values):
    shaped = values.reshape(N_GX, CX, N_GY, CY, N_GRP, CZ).transpose(0, 2, 4, 1, 3, 5)
    return shaped.reshape(N_GX * N_GY * N_GRP * (CX * CY * CZ // 128), 128)


def from_blocks(blocks):
    shaped = blocks.reshape(N_GX, N_GY, N_GRP, CX, CY, CZ).transpose(0, 3, 1, 4, 2, 5)
    return shaped.reshape(N_GX * CX, N_GY * CY, N_GRP * CZ)


def reference(pressure, pressure_old, accumulation, permeability, comp_block, comp_owner, comp_well, comp_wi, well_rate, well_storage, well_bhp_old):
    padded_perm = jnp.pad(permeability, ((0, 0), (1, 1), (1, 1), (1, 1)))
    face_x, face_y, face_z = face_transmissibility(padded_perm)
    summed_faces = face_total(face_x, face_y, face_z)
    device_count = N_GX * N_GY * N_GRP
    block_count = CX * CY * CZ // 128
    peers = N_GX * N_GRP
    well_count = WELLS_DEV
    device_ids = jnp.arange(device_count, dtype=jnp.int32).reshape(N_GX, N_GY, N_GRP, 1)
    block_index = device_ids * block_count + comp_block
    pressure_rows = to_blocks(pressure)[block_index]
    row_ids = jnp.arange(N_GY, dtype=jnp.int32).reshape(1, N_GY, 1, 1)
    well_slot = (row_ids * peers + comp_owner[..., 0]) * well_count + comp_well
    weighted = jnp.sum(comp_wi * pressure_rows, axis=-1)
    total_wi = jnp.sum(comp_wi, axis=-1)
    numerator = jax.ops.segment_sum(weighted.reshape(-1), well_slot.reshape(-1), num_segments=N_GY * peers * well_count)
    denominator = jax.ops.segment_sum(total_wi.reshape(-1), well_slot.reshape(-1), num_segments=N_GY * peers * well_count)

    def by_owner(values):
        return values.reshape(N_GY, N_GX, N_GRP, well_count).transpose(1, 0, 2, 3)

    well_bhp = (by_owner(numerator) + well_storage * well_bhp_old - well_rate) / (by_owner(denominator) + well_storage)
    flat_bhp = well_bhp.transpose(1, 0, 2, 3).reshape(-1)
    well_terms = comp_wi * (pressure_rows - flat_bhp[well_slot][..., None])
    empty = jnp.zeros((device_count * block_count, 128), jnp.float32)
    q_grid = from_blocks(empty.at[block_index.reshape(-1)].add(well_terms.reshape(-1, 128)))
    w_grid = from_blocks(empty.at[block_index.reshape(-1)].add(comp_wi.reshape(-1, 128)))
    padded_p = jnp.pad(pressure, 1)
    resid = accumulation * (pressure - pressure_old) + summed_faces * pressure - neighbour_sum(padded_p, face_x, face_y, face_z) + q_grid
    diagonal = accumulation + w_grid + summed_faces
    agg_x, agg_y, agg_z = CX // CCX, CY // CCY, CZ // CCZ
    coarse_rhs = aggregate(-resid, agg_x, agg_y, agg_z)
    x_high, x_low, y_high, y_low, z_high, z_low = coarse_faces(face_x, face_y, face_z, agg_x, agg_y, agg_z)
    coarse_diag = aggregate(accumulation + w_grid, agg_x, agg_y, agg_z) + x_high + x_low + y_high + y_low + z_high + z_low
    position = jnp.arange(N_GX * CCX, dtype=jnp.int32) % CCX
    high_mask = (position != CCX - 1).astype(jnp.float32)[:, None, None]
    low_mask = (position != 0).astype(jnp.float32)[:, None, None]
    faces = (x_high * high_mask, x_low * low_mask, y_high, y_low, z_high, z_low)
    coarse = jnp.zeros_like(coarse_rhs)
    for step_index in range(COARSE_ITERS):
        coarse = coarse_sweep(coarse, jnp.pad(coarse, 1), coarse_rhs, coarse_diag, faces)
    delta = jnp.repeat(jnp.repeat(jnp.repeat(coarse, agg_x, axis=0), agg_y, axis=1), agg_z, axis=2)
    for sweep_index in range(SWEEPS):
        applied = diagonal * delta - neighbour_sum(jnp.pad(delta, 1), face_x, face_y, face_z)
        delta = delta + RELAXATION * (-resid - applied) / diagonal
    return pressure + delta, well_bhp
```

```python
import jax
import jax.numpy as jnp
from jax import lax
from jax.experimental import pallas as pl
from jax.experimental.pallas import tpu as pltpu
from jax.sharding import PartitionSpec as P

MESH = pl.DeviceIdType.MESH
F32 = jnp.float32
RELAX = 0.7
KEEP = 1.0 - RELAX
NGX, NGY, NGRP = 8, 4, 8
HIGH = lax.Precision.HIGHEST


def iota(shape, dim):
    return lax.broadcasted_iota(jnp.int32, shape, dim)


def nt(a, b):
    return lax.dot_general(
        a, b, (((1,), (1,)), ((), ())), precision=HIGH, preferred_element_type=F32
    )


def nn(a, b):
    return jnp.dot(a, b, precision=HIGH, preferred_element_type=F32)


def rcp(x):
    r = pl.reciprocal(x, approx=True)
    return r * (2.0 - x * r)


def harm(a, b):
    return 2.0 * a * b * rcp(a + b)


def z_below(v):
    r = pltpu.roll(v, 1, 2)
    return jnp.where(iota(v.shape, 2) == 0, pltpu.roll(r, 1, 1), r)


def z_above(v):
    r = pltpu.roll(v, 127, 2)
    return jnp.where(iota(v.shape, 2) == 127, pltpu.roll(r, 7, 1), r)


def kernel(
    cb_s,
    p_hbm,
    po_hbm,
    ac_hbm,
    k_hbm,
    cb_v,
    ow_v,
    cw_v,
    wi_v,
    rate_v,
    stor_v,
    old_v,
    out_hbm,
    bhp_out,
    PG,
    PP,
    PO,
    AC,
    KX,
    KY,
    KZ,
    AXL,
    AXH,
    AYL,
    AYH,
    AZL,
    AZH,
    CC,
    BB,
    D,
    OUT,
    OH,
    PR,
    OWN,
    W1,
    W2,
    HZP,
    HZK,
    ZS0,
    ZI,
    ZSD,
    ZR,
    CQ,
    CSO,
    CBO,
    CS,
    CB,
    VO,
    VX,
    lsem,
    a1s,
    a1r,
    a2s,
    a2r,
    ihs,
    ihr,
    css,
    csr,
    cbs,
    cbr,
    vxs,
    vxr,
    sws,
    swr,
):
    i = lax.axis_index("gx")
    j = lax.axis_index("gy")
    l = lax.axis_index("grp")
    i_lo, i_hi = lax.rem(i + NGX - 1, NGX), lax.rem(i + 1, NGX)
    l_lo, l_hi = lax.rem(l + NGRP - 1, NGRP), lax.rem(l + 1, NGRP)

    def rdma(src, dst, ss, rs, dev):
        return pltpu.make_async_remote_copy(
            src_ref=src, dst_ref=dst, send_sem=ss, recv_sem=rs, device_id=dev, device_id_type=MESH
        )

    load_g = pltpu.make_async_copy(p_hbm, PG, lsem.at[0])
    load_g.start()

    def load(ys, _):
        for yt in range(2):
            y = yt * 8 + ys
            pltpu.make_async_copy(
                p_hbm.at[:, yt, :, ys, :], PP.at[pl.ds(1, 16), 1 + y], lsem.at[1]
            ).start()
            pltpu.make_async_copy(
                k_hbm.at[0, :, yt, :, ys, :], KX.at[pl.ds(1, 16), y], lsem.at[2]
            ).start()
            pltpu.make_async_copy(
                k_hbm.at[1, :, yt, :, ys, :], KY.at[:, 1 + y], lsem.at[3]
            ).start()
            pltpu.make_async_copy(k_hbm.at[2, :, yt, :, ys, :], KZ.at[:, y], lsem.at[4]).start()
            pltpu.make_async_copy(po_hbm.at[:, yt, :, ys, :], PO.at[:, y], lsem.at[5]).start()
            pltpu.make_async_copy(ac_hbm.at[:, yt, :, ys, :], AC.at[:, y], lsem.at[6]).start()
        return 0

    lax.fori_loop(0, 8, load, 0)

    zplane = jnp.zeros((16, 8, 128), F32)

    @pl.when(j == 0)
    def _():
        PP[pl.ds(1, 16), 0] = zplane
        for s in range(1, 4):
            D[s, pl.ds(1, 16), 0] = zplane

    @pl.when(j == NGY - 1)
    def _():
        PP[pl.ds(1, 16), 17] = zplane
        for s in range(1, 4):
            D[s, pl.ds(1, 16), 17] = zplane

    bar = pltpu.get_barrier_semaphore()

    def greet(dev):
        pl.semaphore_signal(bar, inc=1, device_id=dev, device_id_type=MESH)

    for d in range(1, NGX):
        greet({"gx": lax.rem(i + d, NGX)})
    for d in range(1, NGRP):
        greet({"grp": lax.rem(l + d, NGRP)})
    for dj in range(1, NGY):
        for dz in range(3):
            greet({"gy": lax.rem(j + dj, NGY), "grp": lax.rem(l + dz + NGRP - 1, NGRP)})

    load_g.wait()

    def gather(g, _):
        for u in range(8):
            b = cb_s[0, g * 8 + u]
            x, y, k = b // 128, lax.rem(b // 8, 16), lax.rem(b, 8)
            PR[pl.ds(g * 8 + u, 1), :] = PG[x, y // 8, k, pl.ds(lax.rem(y, 8), 1), :]
        return 0

    lax.fori_loop(0, 16, gather, 0)
    wi = wi_v[...]
    sub = iota((8, 128), 0)
    lane = iota((8, 128), 1)
    sub128 = iota((128, 128), 0)
    lane128 = iota((128, 128), 1)
    ones8 = jnp.ones((8, 128), F32)
    weighted = nt(ones8, wi * PR[...])
    total = nt(ones8, wi)
    cb = cb_v[...]
    q = ow_v[...] * 8 + cw_v[...]
    q_hi, q_lo = q // 128, lax.rem(q, 128)
    pick = (sub128 == q_lo).astype(F32)
    share = nt(
        jnp.where(sub == q_hi, weighted, 0.0) + jnp.where(sub == q_hi + 4, total, 0.0), pick
    )
    own = i * NGRP + l
    own_row, shift = own // 16, lax.rem(own, 16) * 8
    OWN[...] = jnp.zeros((8, 128), F32)
    OWN[0:1, 0:8] = stor_v[...] * old_v[...] - rate_v[...]
    OWN[1:2, 0:8] = stor_v[...]
    placed = pltpu.roll(OWN[...], shift, 1)
    share = (
        share
        + jnp.where(sub == own_row, placed[0:1], 0.0)
        + jnp.where(sub == own_row + 4, placed[1:2], 0.0)
    )
    W1[i] = share

    def face_matrix(lo_ref, hi_ref, half, base, width):
        los, his = [], []
        for xx in range(8):
            row = base + (half * 8 + xx) * width * 8
            los.append(lo_ref[pl.ds(row, 16, stride=8), :])
            his.append(hi_ref[pl.ds(row + 7, 16, stride=8), :])
        return jnp.where(
            lane128 < 64, jnp.concatenate(los, axis=0), jnp.concatenate(his, axis=0)
        )

    def face_rows(lo_ref, hi_ref, half, base, width):
        t = jnp.transpose(face_matrix(lo_ref, hi_ref, half, base, width))
        return t[0:8], t[120:128]

    def spread(lo, hi):
        return jnp.transpose(
            jnp.where(sub128 == 0, lo, jnp.where(sub128 == 127, hi, 0.0))
        )

    PP2 = PP.reshape(18 * 18 * 8, 128)
    KZ2 = KZ.reshape(2048, 128)
    for ref, hbm, sem in ((PP.at[pl.ds(1, 16), pl.ds(1, 16)], KZ, 1), (KZ, KZ, 4)):
        pltpu.make_async_copy(KZ, ref, lsem.at[sem]).wait()
    for half in range(2):
        a, b = face_rows(PP2, PP2, half, 19 * 8, 18)
        ZS0[0, 0, half] = a
        ZS0[1, 0, half] = b
        a, b = face_rows(KZ2, KZ2, half, 0, 16)
        ZS0[0, 1, half] = a
        ZS0[1, 1, half] = b
    pltpu.make_async_copy(KZ, KX.at[pl.ds(1, 16)], lsem.at[2]).wait()
    pltpu.make_async_copy(KZ, KY.at[:, pl.ds(1, 16)], lsem.at[3]).wait()

    pl.semaphore_wait(bar, 23)

    sends = []
    for d in range(1, NGX):
        c = rdma(W1.at[i], W1.at[i], a1s.at[d], a1r.at[i], {"gx": lax.rem(i + d, NGX)})
        c.start()
        sends.append(c)

    inner = pl.ds(1, 16)
    zc_lo = rdma(ZS0.at[0], ZI.at[1], ihs.at[0], ihr.at[0], {"grp": l_lo})
    zc_hi = rdma(ZS0.at[1], ZI.at[0], ihs.at[1], ihr.at[1], {"grp": l_hi})
    zc_lo.start()
    zc_hi.start()
    xs = [
        rdma(KX.at[1], KX.at[17], ihs.at[2], ihr.at[2], {"gx": i_lo}),
        rdma(KX.at[16], KX.at[0], ihs.at[3], ihr.at[3], {"gx": i_hi}),
        rdma(PP.at[1, inner], PP.at[17, inner], ihs.at[4], ihr.at[4], {"gx": i_lo}),
        rdma(PP.at[16, inner], PP.at[0, inner], ihs.at[5], ihr.at[5], {"gx": i_hi}),
    ]
    for c in xs:
        c.start()
    y_down = [
        rdma(KY.at[:, 1], KY.at[:, 17], ihs.at[6], ihr.at[6], {"gy": lax.max(j - 1, 0)}),
        rdma(PP.at[inner, 1], PP.at[inner, 17], ihs.at[7], ihr.at[7], {"gy": lax.max(j - 1, 0)}),
    ]
    y_up = [
        rdma(KY.at[:, 16], KY.at[:, 0], ihs.at[8], ihr.at[8], {"gy": lax.min(j + 1, 3)}),
        rdma(PP.at[inner, 16], PP.at[inner, 0], ihs.at[9], ihr.at[9], {"gy": lax.min(j + 1, 3)}),
    ]

    @pl.when(j > 0)
    def _():
        for c in y_down:
            c.start()

    @pl.when(j < NGY - 1)
    def _():
        for c in y_up:
            c.start()

    def onehot(x, _):
        OH[x] = (sub128 + x * 128 == cb).astype(F32).astype(jnp.bfloat16)
        return 0

    lax.fori_loop(0, 16, onehot, 0)

    def halves(v):
        hi = v.astype(jnp.bfloat16)
        lo = (v - hi.astype(F32)).astype(jnp.bfloat16)
        return jnp.concatenate([hi, lo], axis=1)

    def blocks(x, parts):
        r = jnp.dot(OH[x], parts, preferred_element_type=F32)
        return (r[:, :128] + r[:, 128:]).reshape(16, 8, 128)

    wi_parts = halves(wi)

    for d in range(1, NGX):
        s = lax.rem(i + d, NGX)
        rdma(W1.at[i], W1.at[s], a1s.at[d], a1r.at[s], {"gx": s}).wait_recv()
    acc8 = W1[0]
    for s in range(1, NGX):
        acc8 = acc8 + W1[s]
    W2[l] = acc8
    for d in range(1, NGRP):
        c = rdma(W2.at[l], W2.at[l], a2s.at[d], a2r.at[l], {"grp": lax.rem(l + d, NGRP)})
        c.start()
        sends.append(c)

    CQ[...] = jnp.zeros((8, 16, 8, 128), F32)
    pltpu.make_async_copy(KZ, PO, lsem.at[5]).wait()
    pltpu.make_async_copy(KZ, AC, lsem.at[6]).wait()
    for c in xs:
        c.wait_recv()

    @pl.when(j > 0)
    def _():
        for c in y_up:
            c.wait_recv()

    @pl.when(j < NGY - 1)
    def _():
        for c in y_down:
            c.wait_recv()

    zc_lo.wait_recv()
    zc_hi.wait_recv()

    @pl.when(i == 0)
    def _():
        KX[0] = zplane

    @pl.when(i == NGX - 1)
    def _():
        KX[17] = zplane

    @pl.when(j == 0)
    def _():
        KY[:, 0] = zplane

    @pl.when(j == NGY - 1)
    def _():
        KY[:, 17] = zplane

    has_lo = (l > 0).astype(F32)
    has_hi = (l < NGRP - 1).astype(F32)
    for half in range(2):
        rows = pl.ds(half * 128, 128)
        HZP[rows] = spread(ZI[0, 0, half][7:8], ZI[1, 0, half][0:1])
        HZK[rows] = spread(ZI[0, 1, half][7:8] * has_lo, ZI[1, 1, half][0:1] * has_hi)

    sh3 = (8, 8, 128)
    first = (iota(sh3, 2) == 0) & (iota(sh3, 1) == 0)
    last = (iota(sh3, 2) == 127) & (iota(sh3, 1) == 7)

    def column(ref, n):
        return jnp.concatenate(
            [jnp.broadcast_to(ref[pl.ds(n + u, 1), :], (8, 128))[None] for u in range(8)], axis=0
        )

    def operator(x, _):
        w16 = blocks(x, wi_parts)
        big = x // 4
        f_lo = (lax.rem(x, 4) == 0).astype(F32)
        f_hi = (lax.rem(x, 4) == 3).astype(F32)
        for yt in range(2):
            y0 = yt * 8
            c8 = pl.ds(y0, 8)
            kx = KX[x + 1, c8]
            txl, txh = harm(KX[x, c8], kx), harm(kx, KX[x + 2, c8])
            ky = KY[x, pl.ds(y0 + 1, 8)]
            tyl, tyh = harm(KY[x, c8], ky), harm(ky, KY[x, pl.ds(y0 + 2, 8)])
            kz = KZ[x, c8]
            hk = column(HZK, x * 16 + y0)
            tzl = harm(jnp.where(first, hk, z_below(kz)), kz)
            tzh = harm(kz, jnp.where(last, hk, z_above(kz)))
            tsum = ((txl + txh) + (tyl + tyh)) + (tzl + tzh)
            p = PP[x + 1, pl.ds(y0 + 1, 8)]
            hp = column(HZP, x * 16 + y0)
            nb = (
                (txl * PP[x, pl.ds(y0 + 1, 8)] + txh * PP[x + 2, pl.ds(y0 + 1, 8)])
                + (tyl * PP[x + 1, c8] + tyh * PP[x + 1, pl.ds(y0 + 2, 8)])
                + (
                    tzl * jnp.where(first, hp, z_below(p))
                    + tzh * jnp.where(last, hp, z_above(p))
                )
            )
            acc = AC[x, c8]
            w = w16[y0 : y0 + 8]
            r0 = acc * (p - PO[x, c8]) + tsum * p - nb + w * p
            accw = acc + w
            c = RELAX * rcp(accw + tsum)
            AXL[x, c8] = c * txl
            AXH[x, c8] = c * txh
            AYL[x, c8] = c * tyl
            AYH[x, c8] = c * tyh
            AZL[x, c8] = c * tzl
            AZH[x, c8] = c * tzh
            CC[x, c8] = c
            BB[x, c8] = -c * r0
            for yl in range(2):
                n = big * 4 + yt * 2 + yl
                part = slice(yl * 4, yl * 4 + 4)
                CQ[0, n] += r0[part].sum(0)
                CQ[1, n] += accw[part].sum(0)
                CQ[2, n] += txl[part].sum(0) * f_lo
                CQ[3, n] += txh[part].sum(0) * f_hi
                CQ[4, n] += tyl[yl * 4]
                CQ[5, n] += tyh[yl * 4 + 3]
                CQ[6, n] += tzl[part].sum(0)
                CQ[7, n] += tzh[part].sum(0)
        return 0

    lax.fori_loop(0, 16, operator, 0)

    sh4 = (16, 8, 128)
    lane4 = iota(sh4, 2)
    place4 = lane4 == (iota(sh4, 0) // 4) * 32 + iota(sh4, 1)

    def coarse_of(n):
        v = CQ[n]
        if n == 6:
            v = jnp.where(lane4 == 0, v, 0.0)
        if n == 7:
            v = jnp.where(lane4 == 127, v, 0.0)
        v = jnp.where(place4, jnp.sum(v, axis=2, keepdims=True), 0.0)
        v = ((v[0:4] + v[4:8]) + (v[8:12] + v[12:16])).sum(1, keepdims=True)
        out = jnp.zeros((8, 128), F32)
        for y in range(4):
            out = jnp.where(lax.rem(sub, 4) == y, v[y], out)
        return out

    r_c, a_c, xl, xh, yl, yh, zl, zh = [coarse_of(n) for n in range(8)]
    used = lax.rem(lane, 32) < 8
    diag_c = jnp.where(used, a_c + ((xl + xh) + (yl + yh)) + (zl + zh), 1.0)
    scale = jnp.where(used, RELAX / diag_c, 0.0)
    CSO[0] = jnp.where(lane >= 32, scale * xl, 0.0)
    CSO[1] = jnp.where(lane < 96, scale * xh, 0.0)
    CSO[2] = scale * yl
    CSO[3] = scale * yh
    CSO[4] = scale * zl
    CSO[5] = scale * zh
    peers = [(dj, dz) for dj in range(NGY) for dz in range(3) if (dj, dz) != (0, 1)]

    def to_peers(own_ref, all_ref, ss, rs):
        for n, (dj, dz) in enumerate(peers):
            dev = {"gy": lax.rem(j + dj, NGY), "grp": lax.rem(l + dz + NGRP - 1, NGRP)}
            c = rdma(own_ref, all_ref.at[2 - dz, j], ss.at[n], rs.at[2 - dz, j], dev)
            c.start()
            sends.append(c)

    def from_peers(own_ref, all_ref, ss, rs):
        for n, (dj, dz) in enumerate(peers):
            s = lax.rem(j + dj, NGY)
            dev = {"gy": s, "grp": lax.rem(l + dz + NGRP - 1, NGRP)}
            rdma(own_ref, all_ref.at[dz, s], ss.at[n], rs.at[dz, s], dev).wait_recv()

    to_peers(CSO, CS, css, csr)
    CS[1, j] = CSO[...]

    AZL2 = AZL.reshape(2048, 128)
    AZH2 = AZH.reshape(2048, 128)
    end_coef = []
    for half in range(2):
        a, b = face_rows(AZL2, AZH2, half, 0, 16)
        end_coef.append((a[0:1], b[7:8]))

    for d in range(1, NGRP):
        s = lax.rem(l + d, NGRP)
        rdma(W2.at[l], W2.at[s], a2s.at[d], a2r.at[s], {"grp": s}).wait_recv()
    acc8 = W2[0]
    for s in range(1, NGRP):
        acc8 = acc8 + W2[s]
    bhp = jnp.where(sub < 4, acc8 / jnp.where(sub < 4, pltpu.roll(acc8, 4, 0), 1.0), 0.0)
    mine = pltpu.roll(jnp.where(sub == own_row, bhp, 0.0), lax.rem(128 - shift, 128), 1)
    bhp_out[...] = jnp.sum(mine, axis=0, keepdims=True)[:, 0:8]
    bhp_c = jnp.sum(
        jnp.where(sub == q_hi, nn(bhp, pick), 0.0), axis=0, keepdims=True
    )

    cx, cy, ck = cb // 128, lax.rem(cb // 8, 16), lax.rem(cb, 8)
    spot = (sub128 == (cx // 4) * 32 + ck).astype(F32)
    flow = jnp.where(lax.rem(sub, 4) == cy // 4, total * bhp_c, 0.0)
    CBO[...] = scale * (nt(flow, spot) - r_c)
    to_peers(CBO, CB, cbs, cbr)
    CB[1, j] = CBO[...]

    bhp_col = jnp.sum(jnp.where(sub128 == lane128, bhp_c, 0.0), axis=1, keepdims=True)
    wb_parts = halves(wi * bhp_col)

    def finish(x, _):
        BB[x] = BB[x] + CC[x] * blocks(x, wb_parts)
        return 0

    lax.fori_loop(0, 16, finish, 0)

    def joined(tile):
        out = []
        for t in range(2):
            v = None
            for dz in range(3):
                u = jnp.where(sub < 4, tile(dz, 2 * t), tile(dz, 2 * t + 1))
                if dz:
                    u = pltpu.roll(u, 8 * dz, 1)
                v = u if v is None else v + u
            out.append(v)
        return jnp.concatenate(out, axis=0)

    from_peers(CSO, CS, css, csr)
    coef = [joined(lambda dz, g, n=n: CS[dz, g, n]) for n in range(6)]
    from_peers(CBO, CB, cbs, cbr)
    rhs = joined(lambda dz, g: CB[dz, g])

    def coarse_step(_, v):
        return (
            (KEEP * v + rhs)
            + (coef[0] * pltpu.roll(v, 32, 1) + coef[1] * pltpu.roll(v, 96, 1))
            + (coef[2] * pltpu.roll(v, 1, 0) + coef[3] * pltpu.roll(v, 15, 0))
            + (coef[4] * pltpu.roll(v, 1, 1) + coef[5] * pltpu.roll(v, 127, 1))
        )

    v = lax.fori_loop(0, 7, coarse_step, rhs)
    mine = jnp.zeros((8, 128), F32)
    for g in range(NGY):
        mine = jnp.where(j == g, pltpu.roll(v, (17 - 4 * g) % 16, 0)[0:8], mine)
    VO[...] = mine
    vx_lo = rdma(VO, VX.at[1], vxs.at[0], vxr.at[0], {"gx": i_lo})
    vx_hi = rdma(VO, VX.at[0], vxs.at[1], vxr.at[1], {"gx": i_hi})
    vx_lo.start()
    vx_hi.start()

    def upright(tile):
        return jnp.transpose(jnp.concatenate([tile] * 16, axis=0))

    def cell(up, big, row):
        t = jnp.where(lane == row, up[big * 32 + 8 : big * 32 + 16], 0.0)
        return jnp.broadcast_to(jnp.sum(t, axis=1, keepdims=True), (8, 128))

    up = upright(mine)
    for big in range(4):
        for row in range(6):
            t = cell(up, big, row)
            ys = (0,) if row == 0 else (17,) if row == 5 else range(row * 4 - 3, row * 4 + 1)
            for x in range(4):
                for y in ys:
                    D[0, 1 + big * 4 + x, y] = t
    for half in range(2):
        big = half * 2 + lane128 // 64
        row = 1 + lax.rem(lane, 16) // 4
        for n, at in ((0, 7), (1, 16)):
            u = nn(mine, (sub128 == big * 32 + at).astype(F32))
            u = jnp.sum(jnp.where(sub == row, u, 0.0), axis=0, keepdims=True)
            ZR[0, n, half] = jnp.broadcast_to(u, (8, 128))
    vx_lo.wait_recv()
    vx_hi.wait_recv()
    for n, big, at in ((0, 3, 0), (1, 0, 17)):
        up = upright(VX[n])
        for row in range(1, 5):
            t = cell(up, big, row)
            for y in range(row * 4 - 3, row * 4 + 1):
                D[0, at, y] = t

    def sweep(s, put):
        def body(x, _):
            for yt in range(2):
                y0 = yt * 8
                c8 = pl.ds(y0, 8)
                v = D[s, x + 1, pl.ds(y0 + 1, 8)]
                new = (
                    (KEEP * v + BB[x, c8])
                    + (
                        AXL[x, c8] * D[s, x, pl.ds(y0 + 1, 8)]
                        + AXH[x, c8] * D[s, x + 2, pl.ds(y0 + 1, 8)]
                    )
                    + (
                        AYL[x, c8] * D[s, x + 1, c8]
                        + AYH[x, c8] * D[s, x + 1, pl.ds(y0 + 2, 8)]
                    )
                    + (AZL[x, c8] * z_below(v) + AZH[x, c8] * z_above(v))
                )
                put(x, y0, new)
            return 0

        lax.fori_loop(0, 16, body, 0)

    D2 = D.reshape(4 * 18 * 18 * 8, 128)

    def base_of(s):
        return (s * 18 * 18 + 19) * 8

    def fix_ends(s, ref, base, width):
        for half in range(2):
            a, b = face_rows(D2, D2, half, base_of(s), 18)
            fix = spread(
                end_coef[half][0] * (ZR[s, 0, half][7:8] - b[7:8]),
                end_coef[half][1] * (ZR[s, 1, half][0:1] - a[0:1]),
            )
            lo = jnp.where(lane128 < 64, fix, 0.0)
            hi = fix - lo
            for xx in range(8):
                row = base + (half * 8 + xx) * width * 8
                at = pl.ds(row, 16, stride=8)
                ref[at, :] = ref[at, :] + lo[xx * 16 : xx * 16 + 16]
                at = pl.ds(row + 7, 16, stride=8)
                ref[at, :] = ref[at, :] + hi[xx * 16 : xx * 16 + 16]

    def exchange(s):
        out = [
            rdma(ZSD.at[s, 0], ZR.at[s, 1], sws.at[s, 0], swr.at[s, 0], {"grp": l_lo}),
            rdma(ZSD.at[s, 1], ZR.at[s, 0], sws.at[s, 1], swr.at[s, 1], {"grp": l_hi}),
            rdma(D.at[s, 1, inner], D.at[s, 17, inner], sws.at[s, 2], swr.at[s, 2], {"gx": i_lo}),
            rdma(D.at[s, 16, inner], D.at[s, 0, inner], sws.at[s, 3], swr.at[s, 3], {"gx": i_hi}),
        ]
        down = rdma(
            D.at[s, inner, 1],
            D.at[s, inner, 17],
            sws.at[s, 4],
            swr.at[s, 4],
            {"gy": lax.max(j - 1, 0)},
        )
        up = rdma(
            D.at[s, inner, 16],
            D.at[s, inner, 0],
            sws.at[s, 5],
            swr.at[s, 5],
            {"gy": lax.min(j + 1, 3)},
        )
        return out, down, up

    def step(s, _):
        def put(x, y0, new):
            D[s + 1, x + 1, pl.ds(y0 + 1, 8)] = new

        sweep(s, put)
        fix_ends(s, D2, base_of(s + 1), 18)
        for half in range(2):
            a, b = face_rows(D2, D2, half, base_of(s + 1), 18)
            ZSD[s + 1, 0, half] = a
            ZSD[s + 1, 1, half] = b
        out, down, up = exchange(s + 1)
        for c in out:
            c.start()

        @pl.when(j > 0)
        def _():
            down.start()

        @pl.when(j < NGY - 1)
        def _():
            up.start()

        for c in out:
            c.wait()

        @pl.when(j > 0)
        def _():
            down.wait_send()
            up.wait_recv()

        @pl.when(j < NGY - 1)
        def _():
            up.wait_send()
            down.wait_recv()

        return 0

    lax.fori_loop(0, 3, step, 0)

    def put_last(x, y0, new):
        OUT[x, y0 // 8] = PP[x + 1, pl.ds(y0 + 1, 8)] + new

    sweep(3, put_last)
    OUT2 = OUT.reshape(2048, 128)
    fix_ends(3, OUT2, 0, 16)

    def store(ys, _):
        pltpu.make_async_copy(OUT.at[:, :, ys], out_hbm.at[:, :, :, ys, :], lsem.at[0]).start()
        return 0

    lax.fori_loop(0, 8, store, 0)

    for c in sends + xs + [zc_lo, zc_hi, vx_lo, vx_hi]:
        c.wait_send()

    @pl.when(j > 0)
    def _():
        for c in y_down:
            c.wait_send()

    @pl.when(j < NGY - 1)
    def _():
        for c in y_up:
            c.wait_send()

    pltpu.make_async_copy(OUT, out_hbm, lsem.at[0]).wait()


def tiles(a):
    return a.reshape(16, 2, 8, 8, 128).transpose(0, 1, 3, 2, 4)


def per_device(
    pressure,
    pressure_old,
    accumulation,
    permeability,
    comp_block,
    comp_owner,
    comp_well,
    comp_wi,
    well_rate,
    well_storage,
    well_bhp_old,
):
    perm = permeability.reshape(3, 16, 2, 8, 8, 128).transpose(0, 1, 2, 4, 3, 5)
    hbm = pl.BlockSpec(memory_space=pl.ANY)
    vmem = pl.BlockSpec(memory_space=pltpu.VMEM)
    smem = pl.BlockSpec(memory_space=pltpu.SMEM)
    grid = (16, 16, 8, 128)
    dma = pltpu.SemaphoreType.DMA
    cb = comp_block.reshape(1, 128)

    def vm(*shape):
        return pltpu.VMEM(shape, F32)

    out, bhp = pl.pallas_call(
        kernel,
        out_shape=(
            jax.ShapeDtypeStruct((16, 2, 8, 8, 128), F32),
            jax.ShapeDtypeStruct((1, 8), F32),
        ),
        in_specs=[smem] + [hbm] * 4 + [vmem] * 7,
        out_specs=(hbm, vmem),
        scratch_shapes=[
            vm(16, 2, 8, 8, 128),
            vm(18, 18, 8, 128),
            vm(*grid),
            vm(*grid),
            vm(18, 16, 8, 128),
            vm(16, 18, 8, 128),
            vm(*grid),
            vm(*grid),
            vm(*grid),
            vm(*grid),
            vm(*grid),
            vm(*grid),
            vm(*grid),
            vm(*grid),
            vm(*grid),
            vm(4, 18, 18, 8, 128),
            vm(16, 2, 8, 8, 128),
            pltpu.VMEM((16, 128, 128), jnp.bfloat16),
            vm(128, 128),
            vm(8, 128),
            vm(8, 8, 128),
            vm(8, 8, 128),
            vm(256, 128),
            vm(256, 128),
            vm(2, 2, 2, 8, 128),
            vm(2, 2, 2, 8, 128),
            vm(4, 2, 2, 8, 128),
            vm(4, 2, 2, 8, 128),
            vm(8, 16, 8, 128),
            vm(6, 8, 128),
            vm(8, 128),
            vm(3, 4, 6, 8, 128),
            vm(3, 4, 8, 128),
            vm(8, 128),
            vm(2, 8, 128),
            dma((7,)),
            dma((8,)),
            dma((8,)),
            dma((8,)),
            dma((8,)),
            dma((10,)),
            dma((10,)),
            dma((11,)),
            dma((3, 4)),
            dma((11,)),
            dma((3, 4)),
            dma((2,)),
            dma((2,)),
            dma((4, 6)),
            dma((4, 6)),
        ],
        compiler_params=pltpu.CompilerParams(
            collective_id=0, has_side_effects=True, vmem_limit_bytes=60 * 1024 * 1024
        ),
    )(
        cb,
        tiles(pressure),
        tiles(pressure_old),
        tiles(accumulation),
        perm,
        cb,
        comp_owner.reshape(1, 128),
        comp_well.reshape(1, 128),
        comp_wi.reshape(128, 128),
        well_rate.reshape(1, 8),
        well_storage.reshape(1, 8),
        well_bhp_old.reshape(1, 8),
    )
    new = out.transpose(0, 1, 3, 2, 4).reshape(16, 16, 1024)
    return new, bhp.reshape(1, 1, 1, 8)


def solution(mesh):
    return jax.shard_map(
        per_device,
        mesh=mesh,
        in_specs=(
            P("gx", "gy", "grp"),
            P("gx", "gy", "grp"),
            P("gx", "gy", "grp"),
            P(None, "gx", "gy", "grp"),
            P("gx", "gy", "grp", None),
            P("gx", "gy", "grp", None, None),
            P("gx", "gy", "grp", None),
            P("gx", "gy", "grp", None, None),
            P("gx", "gy", "grp", None),
            P("gx", "gy", "grp", None),
            P("gx", "gy", "grp", None),
        ),
        out_specs=(P("gx", "gy", "grp"), P("gx", "gy", "grp", None)),
        check_vma=False,
    )
```

```python
import jax
import jax.numpy as jnp
from jax import lax
from jax.experimental import pallas as pl
from jax.experimental.pallas import tpu as pltpu
from jax.sharding import PartitionSpec as P

MESH = pl.DeviceIdType.MESH
F32 = jnp.float32
RELAX = 0.7
KEEP = 1.0 - RELAX
NGX, NGY, NGRP = 8, 4, 8
HIGH = lax.Precision.HIGHEST


def iota(shape, dim):
    return lax.broadcasted_iota(jnp.int32, shape, dim)


def nt(a, b):
    return lax.dot_general(
        a, b, (((1,), (1,)), ((), ())), precision=HIGH, preferred_element_type=F32
    )


def nn(a, b):
    return jnp.dot(a, b, precision=HIGH, preferred_element_type=F32)


def rcp(x):
    r = pl.reciprocal(x, approx=True)
    return r * (2.0 - x * r)


def harm(a, b):
    return 2.0 * a * b * rcp(a + b)


def z_below(v):
    r = pltpu.roll(v, 1, 2)
    return jnp.where(iota(v.shape, 2) == 0, pltpu.roll(r, 1, 1), r)


def z_above(v):
    r = pltpu.roll(v, 127, 2)
    return jnp.where(iota(v.shape, 2) == 127, pltpu.roll(r, 7, 1), r)


def kernel(
    cb_s,
    p_hbm,
    po_hbm,
    ac_hbm,
    k_hbm,
    cb_v,
    ow_v,
    cw_v,
    wi_v,
    rate_v,
    stor_v,
    old_v,
    out_hbm,
    bhp_out,
    PG,
    PP,
    PO,
    AC,
    KX,
    KY,
    KZ,
    AXL,
    AXH,
    AYL,
    AYH,
    AZL,
    AZH,
    CC,
    BB,
    D,
    OUT,
    OH,
    PR,
    OWN,
    W1,
    W2,
    HZP,
    HZK,
    ZS0,
    ZI,
    SA,
    RA,
    SB,
    RB,
    AE,
    E,
    EX,
    EY,
    EYS,
    FA,
    AR,
    FR,
    UU,
    CQ,
    CSO,
    CBO,
    CS,
    CB,
    VO,
    VX,
    lsem,
    a1s,
    a1r,
    a2s,
    a2r,
    ihs,
    ihr,
    css,
    csr,
    cbs,
    cbr,
    vxs,
    vxr,
    ras,
    rar,
    sws,
    swr,
):
    i = lax.axis_index("gx")
    j = lax.axis_index("gy")
    l = lax.axis_index("grp")
    i_lo, i_hi = lax.rem(i + NGX - 1, NGX), lax.rem(i + 1, NGX)
    l_lo, l_hi = lax.rem(l + NGRP - 1, NGRP), lax.rem(l + 1, NGRP)

    def rdma(src, dst, ss, rs, dev):
        return pltpu.make_async_remote_copy(
            src_ref=src, dst_ref=dst, send_sem=ss, recv_sem=rs, device_id=dev, device_id_type=MESH
        )

    bar = pltpu.get_barrier_semaphore()

    def greet(dev):
        pl.semaphore_signal(bar, inc=1, device_id=dev, device_id_type=MESH)

    for d in range(1, NGX):
        greet({"gx": lax.rem(i + d, NGX)})
    for d in range(1, NGRP):
        greet({"grp": lax.rem(l + d, NGRP)})
    for dj in range(1, NGY):
        for dz in range(3):
            greet({"gy": lax.rem(j + dj, NGY), "grp": lax.rem(l + dz + NGRP - 1, NGRP)})

    load_g = pltpu.make_async_copy(p_hbm, PG, lsem.at[0])
    load_g.start()

    def load(ys, _):
        for yt in range(2):
            y = yt * 8 + ys
            pltpu.make_async_copy(
                p_hbm.at[:, yt, :, ys, :], PP.at[pl.ds(1, 16), 1 + y], lsem.at[1]
            ).start()
            pltpu.make_async_copy(
                k_hbm.at[0, :, yt, :, ys, :], KX.at[pl.ds(1, 16), y], lsem.at[2]
            ).start()
            pltpu.make_async_copy(
                k_hbm.at[1, :, yt, :, ys, :], KY.at[:, 1 + y], lsem.at[3]
            ).start()
            pltpu.make_async_copy(k_hbm.at[2, :, yt, :, ys, :], KZ.at[:, y], lsem.at[4]).start()
            pltpu.make_async_copy(po_hbm.at[:, yt, :, ys, :], PO.at[:, y], lsem.at[5]).start()
            pltpu.make_async_copy(ac_hbm.at[:, yt, :, ys, :], AC.at[:, y], lsem.at[6]).start()
        return 0

    lax.fori_loop(0, 8, load, 0)

    load_g.wait()

    def gather(g, _):
        for u in range(8):
            b = cb_s[0, g * 8 + u]
            x, y, k = b // 128, lax.rem(b // 8, 16), lax.rem(b, 8)
            PR[pl.ds(g * 8 + u, 1), :] = PG[x, y // 8, k, pl.ds(lax.rem(y, 8), 1), :]
        return 0

    lax.fori_loop(0, 16, gather, 0)
    wi = wi_v[...]
    sub = iota((8, 128), 0)
    lane = iota((8, 128), 1)
    sub128 = iota((128, 128), 0)
    lane128 = iota((128, 128), 1)
    ones8 = jnp.ones((8, 128), F32)
    weighted = nt(ones8, wi * PR[...])
    total = nt(ones8, wi)
    cb = cb_v[...]
    q = ow_v[...] * 8 + cw_v[...]
    q_hi, q_lo = q // 128, lax.rem(q, 128)
    pick = (sub128 == q_lo).astype(F32)
    share = nt(
        jnp.where(sub == q_hi, weighted, 0.0) + jnp.where(sub == q_hi + 4, total, 0.0), pick
    )
    own = i * NGRP + l
    own_row, shift = own // 16, lax.rem(own, 16) * 8
    OWN[...] = jnp.zeros((8, 128), F32)
    OWN[0:1, 0:8] = stor_v[...] * old_v[...] - rate_v[...]
    OWN[1:2, 0:8] = stor_v[...]
    placed = pltpu.roll(OWN[...], shift, 1)
    share = (
        share
        + jnp.where(sub == own_row, placed[0:1], 0.0)
        + jnp.where(sub == own_row + 4, placed[1:2], 0.0)
    )
    W1[i] = share

    pl.semaphore_wait(bar, 23)

    sends = []
    for d in range(1, NGX):
        c = rdma(W1.at[i], W1.at[i], a1s.at[d], a1r.at[i], {"gx": lax.rem(i + d, NGX)})
        c.start()
        sends.append(c)

    zplane = jnp.zeros((16, 8, 128), F32)

    @pl.when(j == 0)
    def _():
        PP[pl.ds(1, 16), 0] = zplane
        for s in range(1, 4):
            D[s, pl.ds(1, 16), 0] = zplane
            EY[s, 0] = jnp.zeros((16, 128), F32)

    @pl.when(j == NGY - 1)
    def _():
        PP[pl.ds(1, 16), 17] = zplane
        for s in range(1, 4):
            D[s, pl.ds(1, 16), 17] = zplane
            EY[s, 1] = jnp.zeros((16, 128), F32)

    lane64 = iota((64, 128), 1)

    def end_rows(ref, part, k, base, width):
        return jnp.concatenate(
            [
                ref[pl.ds(base + (part * 4 + u) * width * 8 + k, 16, stride=8), :]
                for u in range(4)
            ],
            axis=0,
        )

    def pack_ends(refs, lo_ref, hi_ref):
        lo = hi = jnp.zeros((64, 128), F32)
        for part in range(4):
            for n, (ref, base, width) in enumerate(refs):
                to = part * 32 + n * 4
                a = jnp.where(lane64 < 4, end_rows(ref, part, 0, base, width), 0.0)
                b = jnp.where(lane64 >= 124, end_rows(ref, part, 7, base, width), 0.0)
                lo = lo + (pltpu.roll(a, to, 1) if to else a)
                hi = hi + pltpu.roll(b, to + 4, 1)
        lo_ref[...] = lo
        hi_ref[...] = hi

    PP2 = PP.reshape(18 * 18 * 8, 128)
    KZ2 = KZ.reshape(2048, 128)
    for ref, hbm, sem in ((PP.at[pl.ds(1, 16), pl.ds(1, 16)], KZ, 1), (KZ, KZ, 4)):
        pltpu.make_async_copy(KZ, ref, lsem.at[sem]).wait()
    pack_ends(((PP2, 19 * 8, 18), (KZ2, 0, 16)), ZS0.at[0], ZS0.at[1])
    pltpu.make_async_copy(KZ, KX.at[pl.ds(1, 16)], lsem.at[2]).wait()
    pltpu.make_async_copy(KZ, KY.at[:, pl.ds(1, 16)], lsem.at[3]).wait()

    inner = pl.ds(1, 16)
    zc_lo = rdma(ZS0.at[0], ZI.at[1], ihs.at[0], ihr.at[0], {"grp": l_lo})
    zc_hi = rdma(ZS0.at[1], ZI.at[0], ihs.at[1], ihr.at[1], {"grp": l_hi})
    zc_lo.start()
    zc_hi.start()
    xs = [
        rdma(KX.at[1], KX.at[17], ihs.at[2], ihr.at[2], {"gx": i_lo}),
        rdma(KX.at[16], KX.at[0], ihs.at[3], ihr.at[3], {"gx": i_hi}),
        rdma(PP.at[1, inner], PP.at[17, inner], ihs.at[4], ihr.at[4], {"gx": i_lo}),
        rdma(PP.at[16, inner], PP.at[0, inner], ihs.at[5], ihr.at[5], {"gx": i_hi}),
    ]
    for c in xs:
        c.start()
    y_down = [
        rdma(KY.at[:, 1], KY.at[:, 17], ihs.at[6], ihr.at[6], {"gy": lax.max(j - 1, 0)}),
        rdma(PP.at[inner, 1], PP.at[inner, 17], ihs.at[7], ihr.at[7], {"gy": lax.max(j - 1, 0)}),
    ]
    y_up = [
        rdma(KY.at[:, 16], KY.at[:, 0], ihs.at[8], ihr.at[8], {"gy": lax.min(j + 1, 3)}),
        rdma(PP.at[inner, 16], PP.at[inner, 0], ihs.at[9], ihr.at[9], {"gy": lax.min(j + 1, 3)}),
    ]

    @pl.when(j > 0)
    def _():
        for c in y_down:
            c.start()

    @pl.when(j < NGY - 1)
    def _():
        for c in y_up:
            c.start()

    def onehot(x, _):
        OH[x] = (sub128 + x * 128 == cb).astype(F32).astype(jnp.bfloat16)
        return 0

    lax.fori_loop(0, 16, onehot, 0)

    def halves(v):
        hi = v.astype(jnp.bfloat16)
        lo = (v - hi.astype(F32)).astype(jnp.bfloat16)
        return jnp.concatenate([hi, lo], axis=1)

    def blocks(x, parts):
        r = jnp.dot(OH[x], parts, preferred_element_type=F32)
        return (r[:, :128] + r[:, 128:]).reshape(16, 8, 128)

    wi_parts = halves(wi)

    for d in range(1, NGX):
        s = lax.rem(i + d, NGX)
        rdma(W1.at[i], W1.at[s], a1s.at[d], a1r.at[s], {"gx": s}).wait_recv()
    acc8 = W1[0]
    for s in range(1, NGX):
        acc8 = acc8 + W1[s]
    W2[l] = acc8
    for d in range(1, NGRP):
        c = rdma(W2.at[l], W2.at[l], a2s.at[d], a2r.at[l], {"grp": lax.rem(l + d, NGRP)})
        c.start()
        sends.append(c)

    CQ[...] = jnp.zeros((8, 16, 8, 128), F32)
    pltpu.make_async_copy(KZ, PO, lsem.at[5]).wait()
    pltpu.make_async_copy(KZ, AC, lsem.at[6]).wait()
    for c in xs:
        c.wait_recv()

    @pl.when(j > 0)
    def _():
        for c in y_up:
            c.wait_recv()

    @pl.when(j < NGY - 1)
    def _():
        for c in y_down:
            c.wait_recv()

    zc_lo.wait_recv()
    zc_hi.wait_recv()

    @pl.when(i == 0)
    def _():
        KX[0] = zplane

    @pl.when(i == NGX - 1)
    def _():
        KX[17] = zplane

    @pl.when(j == 0)
    def _():
        KY[:, 0] = zplane

    @pl.when(j == NGY - 1)
    def _():
        KY[:, 17] = zplane

    has_lo = (l > 0).astype(F32)
    has_hi = (l < NGRP - 1).astype(F32)
    for part in range(4):
        rows = pl.ds(part * 64, 64)
        for n, ref in enumerate((HZP, HZK)):
            at = part * 32 + n * 4
            lo = pltpu.roll(ZI[0], (128 - at - 3) % 128, 1)
            hi = pltpu.roll(ZI[1], 127 - at, 1)
            if n:
                lo, hi = lo * has_lo, hi * has_hi
            ref[rows] = jnp.where(lane64 == 0, lo, hi)

    sh3 = (8, 8, 128)
    first = (iota(sh3, 2) == 0) & (iota(sh3, 1) == 0)
    last = (iota(sh3, 2) == 127) & (iota(sh3, 1) == 7)

    def column(ref, n):
        return jnp.concatenate(
            [jnp.broadcast_to(ref[pl.ds(n + u, 1), :], (8, 128))[None] for u in range(8)], axis=0
        )

    def operator(x, _):
        w16 = blocks(x, wi_parts)
        big = x // 4
        f_lo = (lax.rem(x, 4) == 0).astype(F32)
        f_hi = (lax.rem(x, 4) == 3).astype(F32)
        for yt in range(2):
            y0 = yt * 8
            c8 = pl.ds(y0, 8)
            kx = KX[x + 1, c8]
            txl, txh = harm(KX[x, c8], kx), harm(kx, KX[x + 2, c8])
            ky = KY[x, pl.ds(y0 + 1, 8)]
            tyl, tyh = harm(KY[x, c8], ky), harm(ky, KY[x, pl.ds(y0 + 2, 8)])
            kz = KZ[x, c8]
            hk = column(HZK, x * 16 + y0)
            tzl = harm(jnp.where(first, hk, z_below(kz)), kz)
            tzh = harm(kz, jnp.where(last, hk, z_above(kz)))
            tsum = ((txl + txh) + (tyl + tyh)) + (tzl + tzh)
            p = PP[x + 1, pl.ds(y0 + 1, 8)]
            hp = column(HZP, x * 16 + y0)
            nb = (
                (txl * PP[x, pl.ds(y0 + 1, 8)] + txh * PP[x + 2, pl.ds(y0 + 1, 8)])
                + (tyl * PP[x + 1, c8] + tyh * PP[x + 1, pl.ds(y0 + 2, 8)])
                + (
                    tzl * jnp.where(first, hp, z_below(p))
                    + tzh * jnp.where(last, hp, z_above(p))
                )
            )
            acc = AC[x, c8]
            w = w16[y0 : y0 + 8]
            r0 = acc * (p - PO[x, c8]) + tsum * p - nb + w * p
            accw = acc + w
            c = RELAX * rcp(accw + tsum)
            AXL[x, c8] = c * txl
            AXH[x, c8] = c * txh
            AYL[x, c8] = c * tyl
            AYH[x, c8] = c * tyh
            AZL[x, c8] = c * tzl
            AZH[x, c8] = c * tzh
            CC[x, c8] = c
            BB[x, c8] = -c * r0
            for yl in range(2):
                n = big * 4 + yt * 2 + yl
                part = slice(yl * 4, yl * 4 + 4)
                CQ[0, n] += r0[part].sum(0)
                CQ[1, n] += accw[part].sum(0)
                CQ[2, n] += txl[part].sum(0) * f_lo
                CQ[3, n] += txh[part].sum(0) * f_hi
                CQ[4, n] += tyl[yl * 4]
                CQ[5, n] += tyh[yl * 4 + 3]
                CQ[6, n] += tzl[part].sum(0)
                CQ[7, n] += tzh[part].sum(0)
        return 0

    lax.fori_loop(0, 16, operator, 0)

    sh4 = (16, 8, 128)
    lane4 = iota(sh4, 2)
    place4 = lane4 == iota(sh4, 0) * 8 + iota(sh4, 1)

    def coarse_of(n):
        v = CQ[n]
        if n == 6:
            v = jnp.where(lane4 == 0, v, 0.0)
        if n == 7:
            v = jnp.where(lane4 == 127, v, 0.0)
        v = jnp.where(place4, jnp.sum(v, axis=2, keepdims=True), 0.0)
        return jnp.sum(v.sum(0), axis=0, keepdims=True)

    r_c, a_c, xl, xh, yl, yh, zl, zh = [coarse_of(n) for n in range(8)]
    scale = RELAX / (a_c + ((xl + xh) + (yl + yh)) + (zl + zh))
    lane1 = iota((1, 128), 1)
    CSO[...] = jnp.concatenate(
        [
            jnp.where(lane1 >= 32, scale * xl, 0.0),
            jnp.where(lane1 < 96, scale * xh, 0.0),
            scale * yl,
            scale * yh,
            scale * zl,
            scale * zh,
            scale,
            scale,
        ],
        axis=0,
    )
    peers = [(dj, dz) for dj in range(NGY) for dz in range(3) if (dj, dz) != (0, 1)]

    def to_peers(own_ref, all_ref, ss, rs):
        for n, (dj, dz) in enumerate(peers):
            dev = {"gy": lax.rem(j + dj, NGY), "grp": lax.rem(l + dz + NGRP - 1, NGRP)}
            c = rdma(own_ref, all_ref.at[2 - dz, j], ss.at[n], rs.at[2 - dz, j], dev)
            c.start()
            sends.append(c)

    def from_peers(own_ref, all_ref, ss, rs):
        for n, (dj, dz) in enumerate(peers):
            s = lax.rem(j + dj, NGY)
            dev = {"gy": s, "grp": lax.rem(l + dz + NGRP - 1, NGRP)}
            rdma(own_ref, all_ref.at[dz, s], ss.at[n], rs.at[dz, s], dev).wait_recv()

    to_peers(CSO, CS, css, csr)
    CS[1, j] = CSO[...]

    def flat(ref):
        return (ref.reshape(2048, 128), 0, 16)

    ends_s = [
        rdma(SA.at[0], RA.at[1], ras.at[0], rar.at[0], {"grp": l_lo}),
        rdma(SA.at[1], RA.at[0], ras.at[1], rar.at[1], {"grp": l_hi}),
        rdma(SB.at[0], RB.at[1], ras.at[2], rar.at[2], {"grp": l_lo}),
        rdma(SB.at[1], RB.at[0], ras.at[3], rar.at[3], {"grp": l_hi}),
    ]
    pack_ends([flat(r) for r in (AXL, AXH, AYL, AYH, AZL, AZH)], SA.at[0], SA.at[1])
    ends_s[0].start()
    ends_s[1].start()
    AZL2, AZH2 = AZL.reshape(2048, 128), AZH.reshape(2048, 128)
    for part in range(4):
        AR[pl.ds(part * 64, 64)] = jnp.where(
            lane64 < 64, end_rows(AZL2, part, 0, 0, 16), end_rows(AZH2, part, 7, 0, 16)
        )

    for d in range(1, NGRP):
        s = lax.rem(l + d, NGRP)
        rdma(W2.at[l], W2.at[s], a2s.at[d], a2r.at[s], {"grp": s}).wait_recv()
    acc8 = W2[0]
    for s in range(1, NGRP):
        acc8 = acc8 + W2[s]
    bhp = jnp.where(sub < 4, acc8 / jnp.where(sub < 4, pltpu.roll(acc8, 4, 0), 1.0), 0.0)
    mine = pltpu.roll(jnp.where(sub == own_row, bhp, 0.0), lax.rem(128 - shift, 128), 1)
    bhp_out[...] = jnp.sum(mine, axis=0, keepdims=True)[:, 0:8]
    bhp_c = jnp.sum(
        jnp.where(sub == q_hi, nn(bhp, pick), 0.0), axis=0, keepdims=True
    )

    cx, cy, ck = cb // 128, lax.rem(cb // 8, 16), lax.rem(cb, 8)
    spot = (sub128 == (cx // 4) * 32 + (cy // 4) * 8 + ck).astype(F32)
    CBO[...] = scale * (nt(total * bhp_c, spot) - r_c)
    to_peers(CBO, CB, cbs, cbr)
    CB[1, j] = CBO[...]

    bhp_col = jnp.sum(jnp.where(sub128 == lane128, bhp_c, 0.0), axis=1, keepdims=True)
    wb_parts = halves(wi * bhp_col)

    def finish(x, _):
        BB[x] = BB[x] + CC[x] * blocks(x, wb_parts)
        return 0

    lax.fori_loop(0, 16, finish, 0)
    pack_ends([flat(BB)], SB.at[0], SB.at[1])
    ends_s[2].start()
    ends_s[3].start()

    def joined(all_ref):
        block = lax.rem(lane, 32) // 8
        for g in range(NGY):
            for y in range(4):
                u = None
                for dz in range(3):
                    t = all_ref[dz, g]
                    to = (8 * (dz - y)) % 128
                    t = pltpu.roll(t, to, 1) if to else t
                    u = jnp.where(block == dz, t, 0.0 if u is None else u)
                UU[g * 4 + y] = u

    UU2 = UU.reshape(128, 128)
    from_peers(CSO, CS, css, csr)
    joined(CS)
    coef = [UU2[pl.ds(n, 16, stride=8), :] for n in range(6)]
    from_peers(CBO, CB, cbs, cbr)
    joined(CB)
    rhs = UU2[pl.ds(0, 16, stride=8), :]

    def coarse_step(_, v):
        return (
            (KEEP * v + rhs)
            + (coef[0] * pltpu.roll(v, 32, 1) + coef[1] * pltpu.roll(v, 96, 1))
            + (coef[2] * pltpu.roll(v, 1, 0) + coef[3] * pltpu.roll(v, 15, 0))
            + (coef[4] * pltpu.roll(v, 1, 1) + coef[5] * pltpu.roll(v, 127, 1))
        )

    v = lax.fori_loop(0, 7, coarse_step, rhs)
    mine = jnp.zeros((8, 128), F32)
    for g in range(NGY):
        mine = jnp.where(j == g, pltpu.roll(v, (17 - 4 * g) % 16, 0)[0:8], mine)
    VO[...] = mine
    vx_lo = rdma(VO, VX.at[1], vxs.at[0], vxr.at[0], {"gx": i_lo})
    vx_hi = rdma(VO, VX.at[0], vxs.at[1], vxr.at[1], {"gx": i_hi})
    vx_lo.start()
    vx_hi.start()

    def upright(tile):
        return jnp.transpose(jnp.concatenate([tile] * 16, axis=0))

    def cell(up, big, row):
        t = jnp.where(lane == row, up[big * 32 + 8 : big * 32 + 16], 0.0)
        return jnp.broadcast_to(jnp.sum(t, axis=1, keepdims=True), (8, 128))

    up = upright(mine)
    for big in range(4):
        for row in range(6):
            t = cell(up, big, row)
            ys = (0,) if row == 0 else (17,) if row == 5 else range(row * 4 - 3, row * 4 + 1)
            for x in range(4):
                for y in ys:
                    D[0, 1 + big * 4 + x, y] = t
    sub16 = iota((16, 128), 0)
    y_lo = y_hi = jnp.zeros((16, 128), F32)
    for big in range(4):
        lo, hi = [
            jnp.sum(jnp.where(lane == big * 32 + at, mine, 0.0), axis=1, keepdims=True)
            for at in (7, 16)
        ]
        e = jnp.where(lane < 64, hi, lo)
        rows = jnp.zeros((16, 128), F32)
        for y in range(4):
            rows = jnp.where(sub16 // 4 == y, e[y + 1 : y + 2], rows)
        for u in range(4):
            E[0, pl.ds((big * 4 + u) * 16, 16)] = rows
        y_lo = jnp.where(sub16 // 4 == big, e[0:1], y_lo)
        y_hi = jnp.where(sub16 // 4 == big, e[5:6], y_hi)
    EY[0, 0] = y_lo
    EY[0, 1] = y_hi
    ex_lo = rdma(E.at[0, pl.ds(0, 16)], EX.at[0, 1], sws.at[0, 4], swr.at[0, 4], {"gx": i_lo})
    ex_hi = rdma(E.at[0, pl.ds(240, 16)], EX.at[0, 0], sws.at[0, 5], swr.at[0, 5], {"gx": i_hi})
    ex_lo.start()
    ex_hi.start()
    vx_lo.wait_recv()
    vx_hi.wait_recv()
    for n, big, at in ((0, 3, 0), (1, 0, 17)):
        up = upright(VX[n])
        for row in range(1, 5):
            t = cell(up, big, row)
            for y in range(row * 4 - 3, row * 4 + 1):
                D[0, at, y] = t

    D2 = D.reshape(4 * 18 * 18 * 8, 128)
    E2 = E.reshape(4 * 256, 128)

    def faces(s):
        for part in range(4):
            base = (s * 18 * 18 + 19) * 8
            rows = pl.ds(part * 64, 64)
            m = jnp.where(
                lane64 < 64, end_rows(D2, part, 0, base, 18), end_rows(D2, part, 7, base, 18)
            )
            FA[rows] = m
            d = E[s, rows] - m
            FR[rows] = AR[rows] * jnp.where(
                lane64 < 64, pltpu.roll(d, 1, 1), pltpu.roll(d, 127, 1)
            )

    def columns(s, x, y0, n):
        at = pl.ds(y0, n)
        v = D[s, x + 1, pl.ds(y0 + 1, n)]
        shape = (n, 8, 128)
        k, z = iota(shape, 1), iota(shape, 2)
        ends = ((k == 0) & (z == 0)) | ((k == 7) & (z == 127))
        fix = jnp.concatenate(
            [
                jnp.broadcast_to(FR[pl.ds(x * 16 + y0 + u, 1), :], (8, 128))[None]
                for u in range(n)
            ],
            axis=0,
        )
        return (
            (KEEP * v + BB[x, at])
            + (
                AXL[x, at] * D[s, x, pl.ds(y0 + 1, n)]
                + AXH[x, at] * D[s, x + 2, pl.ds(y0 + 1, n)]
            )
            + (AYL[x, at] * D[s, x + 1, at] + AYH[x, at] * D[s, x + 1, pl.ds(y0 + 2, n)])
            + (AZL[x, at] * z_below(v) + AZH[x, at] * z_above(v))
            + jnp.where(ends, fix, 0.0)
        )

    def beyond(s):
        shape = (4, 16, 128)
        y, z = iota(shape, 1), iota(shape, 2)

        def each_y(ref, part):
            return jnp.concatenate(
                [
                    jnp.broadcast_to(ref[pl.ds(part * 4 + u, 1), :], (16, 128))[None]
                    for u in range(4)
                ],
                axis=0,
            )

        for part in range(4):
            rows = pl.ds(part * 64, 64)
            e = E[s, rows].reshape(shape)
            if part == 0:
                left = jnp.concatenate([EX[s, 0], E[s, pl.ds(0, 48)]], axis=0)
            else:
                left = E[s, pl.ds(part * 64 - 16, 64)]
            if part == 3:
                right = jnp.concatenate([E[s, pl.ds(208, 48)], EX[s, 1]], axis=0)
            else:
                right = E[s, pl.ds(part * 64 + 16, 64)]
            a = [AE[n, rows].reshape(shape) for n in range(7)]
            m = FA[rows].reshape(shape)
            new = (
                (KEEP * e + a[6])
                + (a[0] * left.reshape(shape) + a[1] * right.reshape(shape))
                + (
                    a[2] * jnp.where(y == 0, each_y(EY.at[s, 0], part), pltpu.roll(e, 1, 1))
                    + a[3] * jnp.where(y == 15, each_y(EY.at[s, 1], part), pltpu.roll(e, 15, 1))
                )
                + (
                    a[4] * jnp.where(z == 0, pltpu.roll(m, 1, 2), pltpu.roll(e, 1, 2))
                    + a[5] * jnp.where(z == 127, pltpu.roll(m, 127, 2), pltpu.roll(e, 127, 2))
                )
            )
            E[s + 1, rows] = new.reshape(64, 128)
        EYS[s + 1, 0] = E2[pl.ds((s + 1) * 256, 16, stride=16), :]
        EYS[s + 1, 1] = E2[pl.ds((s + 1) * 256 + 15, 16, stride=16), :]

    def exchange(s):
        ss, rs = sws.at[s], swr.at[s]
        lo, hi = {"gy": lax.max(j - 1, 0)}, {"gy": lax.min(j + 1, 3)}
        x_d = [
            rdma(D.at[s, 1, inner], D.at[s, 17, inner], ss.at[2], rs.at[2], {"gx": i_lo}),
            rdma(D.at[s, 16, inner], D.at[s, 0, inner], ss.at[3], rs.at[3], {"gx": i_hi}),
        ]
        x_e = [
            rdma(E.at[s, pl.ds(0, 16)], EX.at[s, 1], ss.at[4], rs.at[4], {"gx": i_lo}),
            rdma(E.at[s, pl.ds(240, 16)], EX.at[s, 0], ss.at[5], rs.at[5], {"gx": i_hi}),
        ]
        down_d = rdma(D.at[s, inner, 1], D.at[s, inner, 17], ss.at[0], rs.at[0], lo)
        up_d = rdma(D.at[s, inner, 16], D.at[s, inner, 0], ss.at[1], rs.at[1], hi)
        down_e = rdma(EYS.at[s, 0], EY.at[s, 1], ss.at[6], rs.at[6], lo)
        up_e = rdma(EYS.at[s, 1], EY.at[s, 0], ss.at[7], rs.at[7], hi)
        return x_d, x_e, down_d, up_d, down_e, up_e

    faces(0)
    for c in (ex_lo, ex_hi):
        c.wait_recv()

    def step(s, _):
        x_d, x_e, down_d, up_d, down_e, up_e = exchange(s + 1)

        def y_planes(x, _):
            for y in (0, 15):
                D[s + 1, x + 1, pl.ds(y + 1, 1)] = columns(s, x, y, 1)
            return 0

        lax.fori_loop(0, 16, y_planes, 0)

        @pl.when(j > 0)
        def _():
            down_d.start()

        @pl.when(j < NGY - 1)
        def _():
            up_d.start()

        for x in (0, 15):
            for y0 in (1, 8):
                D[s + 1, x + 1, pl.ds(y0 + 1, 7)] = columns(s, x, y0, 7)
        for c in x_d:
            c.start()

        @pl.when(s == 0)
        def _():
            for c in ends_s:
                c.wait_recv()
            for part in range(4):
                for n in range(7):
                    at = part * 32 + (n * 4 if n < 6 else 0)
                    up, down = (RA[1], RA[0]) if n < 6 else (RB[1], RB[0])
                    AE[n, pl.ds(part * 64, 64)] = jnp.where(
                        lane64 < 4,
                        pltpu.roll(up, (128 - at) % 128, 1) if at else up,
                        jnp.where(lane64 >= 124, pltpu.roll(down, 124 - at, 1), 0.0),
                    )

        beyond(s)
        for c in x_e:
            c.start()

        @pl.when(j > 0)
        def _():
            down_e.start()

        @pl.when(j < NGY - 1)
        def _():
            up_e.start()

        def inside(x, _):
            for y0 in (1, 8):
                D[s + 1, x + 1, pl.ds(y0 + 1, 7)] = columns(s, x, y0, 7)
            return 0

        lax.fori_loop(1, 15, inside, 0)
        faces(s + 1)

        @pl.when(j > 0)
        def _():
            for c in (down_d, down_e):
                c.wait_send()
            for c in (up_d, up_e):
                c.wait_recv()

        @pl.when(j < NGY - 1)
        def _():
            for c in (up_d, up_e):
                c.wait_send()
            for c in (down_d, down_e):
                c.wait_recv()

        for c in x_d + x_e:
            c.wait()
        return 0

    lax.fori_loop(0, 3, step, 0)

    def last_sweep(x, _):
        for yt in range(2):
            OUT[x, yt] = columns(3, x, yt * 8, 8)
        return 0

    lax.fori_loop(0, 16, last_sweep, 0)

    def store(ys, _):
        pltpu.make_async_copy(OUT.at[:, :, ys], out_hbm.at[:, :, :, ys, :], lsem.at[0]).start()
        return 0

    lax.fori_loop(0, 8, store, 0)

    for c in sends + xs + ends_s + [zc_lo, zc_hi, vx_lo, vx_hi, ex_lo, ex_hi]:
        c.wait_send()

    @pl.when(j > 0)
    def _():
        for c in y_down:
            c.wait_send()

    @pl.when(j < NGY - 1)
    def _():
        for c in y_up:
            c.wait_send()

    pltpu.make_async_copy(OUT, out_hbm, lsem.at[0]).wait()


def tiles(a):
    return a.reshape(16, 2, 8, 8, 128).transpose(0, 1, 3, 2, 4)


def per_device(
    pressure,
    pressure_old,
    accumulation,
    permeability,
    comp_block,
    comp_owner,
    comp_well,
    comp_wi,
    well_rate,
    well_storage,
    well_bhp_old,
):
    perm = permeability.reshape(3, 16, 2, 8, 8, 128).transpose(0, 1, 2, 4, 3, 5)
    hbm = pl.BlockSpec(memory_space=pl.ANY)
    vmem = pl.BlockSpec(memory_space=pltpu.VMEM)
    smem = pl.BlockSpec(memory_space=pltpu.SMEM)
    grid = (16, 16, 8, 128)
    dma = pltpu.SemaphoreType.DMA
    cb = comp_block.reshape(1, 128)

    def vm(*shape):
        return pltpu.VMEM(shape, F32)

    out, bhp = pl.pallas_call(
        kernel,
        out_shape=(
            jax.ShapeDtypeStruct((16, 2, 8, 8, 128), F32),
            jax.ShapeDtypeStruct((1, 8), F32),
        ),
        in_specs=[smem] + [hbm] * 4 + [vmem] * 7,
        out_specs=(hbm, vmem),
        scratch_shapes=[
            vm(16, 2, 8, 8, 128),
            vm(18, 18, 8, 128),
            vm(*grid),
            vm(*grid),
            vm(18, 16, 8, 128),
            vm(16, 18, 8, 128),
            vm(*grid),
            vm(*grid),
            vm(*grid),
            vm(*grid),
            vm(*grid),
            vm(*grid),
            vm(*grid),
            vm(*grid),
            vm(*grid),
            vm(4, 18, 18, 8, 128),
            vm(16, 2, 8, 8, 128),
            pltpu.VMEM((16, 128, 128), jnp.bfloat16),
            vm(128, 128),
            vm(8, 128),
            vm(8, 8, 128),
            vm(8, 8, 128),
            vm(256, 128),
            vm(256, 128),
            vm(2, 64, 128),
            vm(2, 64, 128),
            vm(2, 64, 128),
            vm(2, 64, 128),
            vm(2, 64, 128),
            vm(2, 64, 128),
            vm(7, 256, 128),
            vm(4, 256, 128),
            vm(4, 2, 16, 128),
            vm(4, 2, 16, 128),
            vm(4, 2, 16, 128),
            vm(256, 128),
            vm(256, 128),
            vm(256, 128),
            vm(16, 8, 128),
            vm(8, 16, 8, 128),
            vm(8, 128),
            vm(8, 128),
            vm(3, 4, 8, 128),
            vm(3, 4, 8, 128),
            vm(8, 128),
            vm(2, 8, 128),
            dma((7,)),
            dma((8,)),
            dma((8,)),
            dma((8,)),
            dma((8,)),
            dma((10,)),
            dma((10,)),
            dma((11,)),
            dma((3, 4)),
            dma((11,)),
            dma((3, 4)),
            dma((2,)),
            dma((2,)),
            dma((4,)),
            dma((4,)),
            dma((4, 8)),
            dma((4, 8)),
        ],
        compiler_params=pltpu.CompilerParams(
            collective_id=0, has_side_effects=True, vmem_limit_bytes=60 * 1024 * 1024
        ),
    )(
        cb,
        tiles(pressure),
        tiles(pressure_old),
        tiles(accumulation),
        perm,
        cb,
        comp_owner.reshape(1, 128),
        comp_well.reshape(1, 128),
        comp_wi.reshape(128, 128),
        well_rate.reshape(1, 8),
        well_storage.reshape(1, 8),
        well_bhp_old.reshape(1, 8),
    )
    delta = out.transpose(0, 1, 3, 2, 4).reshape(16, 16, 1024)
    return pressure + delta, bhp.reshape(1, 1, 1, 8)


def solution(mesh):
    return jax.shard_map(
        per_device,
        mesh=mesh,
        in_specs=(
            P("gx", "gy", "grp"),
            P("gx", "gy", "grp"),
            P("gx", "gy", "grp"),
            P(None, "gx", "gy", "grp"),
            P("gx", "gy", "grp", None),
            P("gx", "gy", "grp", None, None),
            P("gx", "gy", "grp", None),
            P("gx", "gy", "grp", None, None),
            P("gx", "gy", "grp", None),
            P("gx", "gy", "grp", None),
            P("gx", "gy", "grp", None),
        ),
        out_specs=(P("gx", "gy", "grp"), P("gx", "gy", "grp", None)),
        check_vma=False,
    )
```

```python
import jax
import jax.numpy as jnp
from jax import lax
from jax.experimental import pallas as pl
from jax.experimental.pallas import tpu as pltpu
from jax.sharding import PartitionSpec as P

MESH = pl.DeviceIdType.MESH
F32 = jnp.float32
RELAX = 0.7
KEEP = 1.0 - RELAX
NGX, NGY, NGRP = 8, 4, 8
HIGH = lax.Precision.HIGHEST


def iota(shape, dim):
    return lax.broadcasted_iota(jnp.int32, shape, dim)


def nt(a, b):
    return lax.dot_general(
        a, b, (((1,), (1,)), ((), ())), precision=HIGH, preferred_element_type=F32
    )


def nn(a, b):
    return jnp.dot(a, b, precision=HIGH, preferred_element_type=F32)


def rcp(x):
    r = pl.reciprocal(x, approx=True)
    return r * (2.0 - x * r)


def harm(a, b):
    return 2.0 * a * b * rcp(a + b)


def z_below(v):
    r = pltpu.roll(v, 1, 2)
    return jnp.where(iota(v.shape, 2) == 0, pltpu.roll(r, 1, 1), r)


def z_above(v):
    r = pltpu.roll(v, 127, 2)
    return jnp.where(iota(v.shape, 2) == 127, pltpu.roll(r, 7, 1), r)


def kernel(
    cb_s,
    p_hbm,
    po_hbm,
    ac_hbm,
    k_hbm,
    cb_v,
    ow_v,
    cw_v,
    wi_v,
    rate_v,
    stor_v,
    old_v,
    out_ref,
    bhp_out,
    PG,
    PP,
    PO,
    AC,
    KX,
    KY,
    KZ,
    AXL,
    AXH,
    AYL,
    AYH,
    AZL,
    AZH,
    CC,
    BB,
    D,
    OH,
    PR,
    OWN,
    W1,
    W2,
    HZP,
    HZK,
    ZS0,
    ZI,
    SA,
    RA,
    SB,
    RB,
    AE,
    E,
    EX,
    EY,
    EYS,
    FA,
    AR,
    FR,
    UU,
    CQ,
    CSO,
    CBO,
    CS,
    CB,
    VO,
    VX,
    lsem,
    a1s,
    a1r,
    a2s,
    a2r,
    ihs,
    ihr,
    css,
    csr,
    cbs,
    cbr,
    vxs,
    vxr,
    ras,
    rar,
    sws,
    swr,
):
    i = lax.axis_index("gx")
    j = lax.axis_index("gy")
    l = lax.axis_index("grp")
    i_lo, i_hi = lax.rem(i + NGX - 1, NGX), lax.rem(i + 1, NGX)
    l_lo, l_hi = lax.rem(l + NGRP - 1, NGRP), lax.rem(l + 1, NGRP)

    def rdma(src, dst, ss, rs, dev):
        return pltpu.make_async_remote_copy(
            src_ref=src, dst_ref=dst, send_sem=ss, recv_sem=rs, device_id=dev, device_id_type=MESH
        )

    bar = pltpu.get_barrier_semaphore()

    def greet(dev):
        pl.semaphore_signal(bar, inc=1, device_id=dev, device_id_type=MESH)

    for d in range(1, NGX):
        greet({"gx": lax.rem(i + d, NGX)})
    for d in range(1, NGRP):
        greet({"grp": lax.rem(l + d, NGRP)})
    for dj in range(1, NGY):
        for dz in range(3):
            greet({"gy": lax.rem(j + dj, NGY), "grp": lax.rem(l + dz + NGRP - 1, NGRP)})

    load_g = pltpu.make_async_copy(p_hbm, PG, lsem.at[0])
    load_g.start()

    def load_kz(ys, _):
        for yt in range(2):
            pltpu.make_async_copy(
                k_hbm.at[2, :, yt, :, ys, :], KZ.at[:, yt * 8 + ys], lsem.at[4]
            ).start()
        return 0

    lax.fori_loop(0, 8, load_kz, 0)

    def load(ys, _):
        for yt in range(2):
            y = yt * 8 + ys
            pltpu.make_async_copy(
                p_hbm.at[:, yt, :, ys, :], PP.at[pl.ds(1, 16), 1 + y], lsem.at[1]
            ).start()
            pltpu.make_async_copy(
                k_hbm.at[0, :, yt, :, ys, :], KX.at[pl.ds(1, 16), y], lsem.at[2]
            ).start()
            pltpu.make_async_copy(
                k_hbm.at[1, :, yt, :, ys, :], KY.at[:, 1 + y], lsem.at[3]
            ).start()
            pltpu.make_async_copy(po_hbm.at[:, yt, :, ys, :], PO.at[:, y], lsem.at[5]).start()
            pltpu.make_async_copy(ac_hbm.at[:, yt, :, ys, :], AC.at[:, y], lsem.at[6]).start()
        return 0

    lax.fori_loop(0, 8, load, 0)

    load_g.wait()

    def gather(g, _):
        for u in range(8):
            b = cb_s[0, g * 8 + u]
            x, y, k = b // 128, lax.rem(b // 8, 16), lax.rem(b, 8)
            PR[pl.ds(g * 8 + u, 1), :] = PG[x, y // 8, k, pl.ds(lax.rem(y, 8), 1), :]
        return 0

    lax.fori_loop(0, 16, gather, 0)
    wi = wi_v[...]
    sub = iota((8, 128), 0)
    lane = iota((8, 128), 1)
    sub128 = iota((128, 128), 0)
    lane128 = iota((128, 128), 1)
    ones8 = jnp.ones((8, 128), F32)
    weighted = nt(ones8, wi * PR[...])
    total = nt(ones8, wi)
    cb = cb_v[...]
    q = ow_v[...] * 8 + cw_v[...]
    q_hi, q_lo = q // 128, lax.rem(q, 128)
    pick = (sub128 == q_lo).astype(F32)
    share = nt(
        jnp.where(sub == q_hi, weighted, 0.0) + jnp.where(sub == q_hi + 4, total, 0.0), pick
    )
    own = i * NGRP + l
    own_row, shift = own // 16, lax.rem(own, 16) * 8
    OWN[...] = jnp.zeros((8, 128), F32)
    OWN[0:1, 0:8] = stor_v[...] * old_v[...] - rate_v[...]
    OWN[1:2, 0:8] = stor_v[...]
    placed = pltpu.roll(OWN[...], shift, 1)
    share = (
        share
        + jnp.where(sub == own_row, placed[0:1], 0.0)
        + jnp.where(sub == own_row + 4, placed[1:2], 0.0)
    )
    W1[i] = share

    lane64 = iota((64, 128), 1)

    def end_rows(ref, part, k, base, width):
        return jnp.concatenate(
            [
                ref[pl.ds(base + (part * 4 + u) * width * 8 + k, 16, stride=8), :]
                for u in range(4)
            ],
            axis=0,
        )

    def flat(ref):
        ref2 = ref.reshape(2048, 128)
        return (
            lambda part: end_rows(ref2, part, 0, 0, 16),
            lambda part: end_rows(ref2, part, 7, 0, 16),
        )

    def raw_rows(k):
        def rows(part):
            return jnp.concatenate(
                [PG[part * 4 + u, yt, k] for u in range(4) for yt in range(2)], axis=0
            )

        return rows

    def pack_tile(refs, lo_ref, hi_ref):
        keep = 4 if len(refs) == 1 else 1
        lo = hi = jnp.zeros((8, 128), F32)
        for part in range(4):
            for n, ends in enumerate(refs):
                a, b = ends[0](part), ends[1](part)
                for u in range(8):
                    to = part * 32 + u * 4 + n
                    at = slice(u * 8, u * 8 + 8)
                    a8 = jnp.where(lane < keep, a[at], 0.0)
                    b8 = jnp.where(lane >= 128 - keep, b[at], 0.0)
                    lo = lo + (pltpu.roll(a8, to, 1) if to else a8)
                    hi = hi + pltpu.roll(b8, (to + keep) % 128, 1)
        lo_ref[...] = lo
        hi_ref[...] = hi

    def pack_ends(refs, lo_ref, hi_ref):
        lo = hi = jnp.zeros((64, 128), F32)
        for part in range(4):
            for n, ends in enumerate(refs):
                to = part * 32 + n * 4
                a = jnp.where(lane64 < 4, ends[0](part), 0.0)
                b = jnp.where(lane64 >= 124, ends[1](part), 0.0)
                lo = lo + (pltpu.roll(a, to, 1) if to else a)
                hi = hi + pltpu.roll(b, to + 4, 1)
        lo_ref[...] = lo
        hi_ref[...] = hi

    pltpu.make_async_copy(KZ, KZ, lsem.at[4]).wait()
    pack_tile([(raw_rows(0), raw_rows(7)), flat(KZ)], ZS0.at[0], ZS0.at[1])


    pl.semaphore_wait(bar, 23)

    sends = []
    for d in range(1, NGX):
        c = rdma(W1.at[i], W1.at[i], a1s.at[d], a1r.at[i], {"gx": lax.rem(i + d, NGX)})
        c.start()
        sends.append(c)

    zc_lo = rdma(ZS0.at[0], ZI.at[1], ihs.at[0], ihr.at[0], {"grp": l_lo})
    zc_hi = rdma(ZS0.at[1], ZI.at[0], ihs.at[1], ihr.at[1], {"grp": l_hi})
    zc_lo.start()
    zc_hi.start()

    zplane = jnp.zeros((16, 8, 128), F32)

    @pl.when(j == 0)
    def _():
        PP[pl.ds(1, 16), 0] = zplane
        for s in range(1, 4):
            D[s, pl.ds(1, 16), 0] = zplane
            EY[s, 0] = jnp.zeros((16, 128), F32)

    @pl.when(j == NGY - 1)
    def _():
        PP[pl.ds(1, 16), 17] = zplane
        for s in range(1, 4):
            D[s, pl.ds(1, 16), 17] = zplane
            EY[s, 1] = jnp.zeros((16, 128), F32)

    inner = pl.ds(1, 16)
    pltpu.make_async_copy(KZ, KX.at[pl.ds(1, 16)], lsem.at[2]).wait()
    pltpu.make_async_copy(KZ, KY.at[:, pl.ds(1, 16)], lsem.at[3]).wait()
    pltpu.make_async_copy(KZ, PP.at[pl.ds(1, 16), pl.ds(1, 16)], lsem.at[1]).wait()
    xs = [
        rdma(KX.at[1], KX.at[17], ihs.at[2], ihr.at[2], {"gx": i_lo}),
        rdma(KX.at[16], KX.at[0], ihs.at[3], ihr.at[3], {"gx": i_hi}),
        rdma(PP.at[1, inner], PP.at[17, inner], ihs.at[4], ihr.at[4], {"gx": i_lo}),
        rdma(PP.at[16, inner], PP.at[0, inner], ihs.at[5], ihr.at[5], {"gx": i_hi}),
    ]
    for c in xs:
        c.start()
    y_down = [
        rdma(KY.at[:, 1], KY.at[:, 17], ihs.at[6], ihr.at[6], {"gy": lax.max(j - 1, 0)}),
        rdma(PP.at[inner, 1], PP.at[inner, 17], ihs.at[7], ihr.at[7], {"gy": lax.max(j - 1, 0)}),
    ]
    y_up = [
        rdma(KY.at[:, 16], KY.at[:, 0], ihs.at[8], ihr.at[8], {"gy": lax.min(j + 1, 3)}),
        rdma(PP.at[inner, 16], PP.at[inner, 0], ihs.at[9], ihr.at[9], {"gy": lax.min(j + 1, 3)}),
    ]

    @pl.when(j > 0)
    def _():
        for c in y_down:
            c.start()

    @pl.when(j < NGY - 1)
    def _():
        for c in y_up:
            c.start()

    def onehot(x, _):
        OH[x] = (sub128 + x * 128 == cb).astype(F32).astype(jnp.bfloat16)
        return 0

    lax.fori_loop(0, 16, onehot, 0)

    def halves(v):
        hi = v.astype(jnp.bfloat16)
        lo = (v - hi.astype(F32)).astype(jnp.bfloat16)
        return jnp.concatenate([hi, lo], axis=1)

    def blocks(x, parts):
        r = jnp.dot(OH[x], parts, preferred_element_type=F32)
        return (r[:, :128] + r[:, 128:]).reshape(16, 8, 128)

    wi_parts = halves(wi)

    for d in range(1, NGX):
        s = lax.rem(i + d, NGX)
        rdma(W1.at[i], W1.at[s], a1s.at[d], a1r.at[s], {"gx": s}).wait_recv()
    acc8 = W1[0]
    for s in range(1, NGX):
        acc8 = acc8 + W1[s]
    W2[l] = acc8
    for d in range(1, NGRP):
        c = rdma(W2.at[l], W2.at[l], a2s.at[d], a2r.at[l], {"grp": lax.rem(l + d, NGRP)})
        c.start()
        sends.append(c)

    CQ[...] = jnp.zeros((8, 16, 8, 128), F32)
    pltpu.make_async_copy(KZ, PO, lsem.at[5]).wait()
    pltpu.make_async_copy(KZ, AC, lsem.at[6]).wait()
    for c in xs:
        c.wait_recv()

    @pl.when(j > 0)
    def _():
        for c in y_up:
            c.wait_recv()

    @pl.when(j < NGY - 1)
    def _():
        for c in y_down:
            c.wait_recv()

    zc_lo.wait_recv()
    zc_hi.wait_recv()

    @pl.when(i == 0)
    def _():
        KX[0] = zplane

    @pl.when(i == NGX - 1)
    def _():
        KX[17] = zplane

    @pl.when(j == 0)
    def _():
        KY[:, 0] = zplane

    @pl.when(j == NGY - 1)
    def _():
        KY[:, 17] = zplane

    has_lo = (l > 0).astype(F32)
    has_hi = (l < NGRP - 1).astype(F32)
    for g in range(32):
        for n, ref in enumerate((HZP, HZK)):
            lo = pltpu.roll(ZI[0], (128 - g * 4 - n) % 128, 1) if g + n else ZI[0]
            hi = pltpu.roll(ZI[1], 127 - g * 4 - n, 1)
            if n:
                lo, hi = lo * has_lo, hi * has_hi
            ref[pl.ds(g * 8, 8)] = jnp.where(lane == 0, lo, hi)

    sh3 = (8, 8, 128)
    first = (iota(sh3, 2) == 0) & (iota(sh3, 1) == 0)
    last = (iota(sh3, 2) == 127) & (iota(sh3, 1) == 7)

    def column(ref, n):
        return jnp.concatenate(
            [jnp.broadcast_to(ref[pl.ds(n + u, 1), :], (8, 128))[None] for u in range(8)], axis=0
        )

    def operator(x, _):
        w16 = blocks(x, wi_parts)
        big = x // 4
        f_lo = (lax.rem(x, 4) == 0).astype(F32)
        f_hi = (lax.rem(x, 4) == 3).astype(F32)
        for yt in range(2):
            y0 = yt * 8
            c8 = pl.ds(y0, 8)
            kx = KX[x + 1, c8]
            txl, txh = harm(KX[x, c8], kx), harm(kx, KX[x + 2, c8])
            ky = KY[x, pl.ds(y0 + 1, 8)]
            tyl, tyh = harm(KY[x, c8], ky), harm(ky, KY[x, pl.ds(y0 + 2, 8)])
            kz = KZ[x, c8]
            hk = column(HZK, x * 16 + y0)
            tzl = harm(jnp.where(first, hk, z_below(kz)), kz)
            tzh = harm(kz, jnp.where(last, hk, z_above(kz)))
            tsum = ((txl + txh) + (tyl + tyh)) + (tzl + tzh)
            p = PP[x + 1, pl.ds(y0 + 1, 8)]
            hp = column(HZP, x * 16 + y0)
            nb = (
                (txl * PP[x, pl.ds(y0 + 1, 8)] + txh * PP[x + 2, pl.ds(y0 + 1, 8)])
                + (tyl * PP[x + 1, c8] + tyh * PP[x + 1, pl.ds(y0 + 2, 8)])
                + (
                    tzl * jnp.where(first, hp, z_below(p))
                    + tzh * jnp.where(last, hp, z_above(p))
                )
            )
            acc = AC[x, c8]
            w = w16[y0 : y0 + 8]
            r0 = acc * (p - PO[x, c8]) + tsum * p - nb + w * p
            accw = acc + w
            c = RELAX * rcp(accw + tsum)
            AXL[x, c8] = c * txl
            AXH[x, c8] = c * txh
            AYL[x, c8] = c * tyl
            AYH[x, c8] = c * tyh
            AZL[x, c8] = c * tzl
            AZH[x, c8] = c * tzh
            CC[x, c8] = c
            BB[x, c8] = -c * r0
            for yl in range(2):
                n = big * 4 + yt * 2 + yl
                part = slice(yl * 4, yl * 4 + 4)
                CQ[0, n] += r0[part].sum(0)
                CQ[1, n] += accw[part].sum(0)
                CQ[2, n] += txl[part].sum(0) * f_lo
                CQ[3, n] += txh[part].sum(0) * f_hi
                CQ[4, n] += tyl[yl * 4]
                CQ[5, n] += tyh[yl * 4 + 3]
                CQ[6, n] += tzl[part].sum(0)
                CQ[7, n] += tzh[part].sum(0)
        return 0

    lax.fori_loop(0, 16, operator, 0)

    sh4 = (16, 8, 128)
    lane4 = iota(sh4, 2)
    place4 = lane4 == iota(sh4, 0) * 8 + iota(sh4, 1)

    def coarse_of(n):
        v = CQ[n]
        if n == 6:
            v = jnp.where(lane4 == 0, v, 0.0)
        if n == 7:
            v = jnp.where(lane4 == 127, v, 0.0)
        v = jnp.where(place4, jnp.sum(v, axis=2, keepdims=True), 0.0)
        return jnp.sum(v.sum(0), axis=0, keepdims=True)

    r_c, a_c, xl, xh, yl, yh, zl, zh = [coarse_of(n) for n in range(8)]
    scale = RELAX / (a_c + ((xl + xh) + (yl + yh)) + (zl + zh))
    lane1 = iota((1, 128), 1)
    CSO[...] = jnp.concatenate(
        [
            jnp.where(lane1 >= 32, scale * xl, 0.0),
            jnp.where(lane1 < 96, scale * xh, 0.0),
            scale * yl,
            scale * yh,
            scale * zl,
            scale * zh,
            scale,
            scale,
        ],
        axis=0,
    )
    peers = [(dj, dz) for dj in range(NGY) for dz in range(3) if (dj, dz) != (0, 1)]

    def to_peers(own_ref, all_ref, ss, rs):
        for n, (dj, dz) in enumerate(peers):
            dev = {"gy": lax.rem(j + dj, NGY), "grp": lax.rem(l + dz + NGRP - 1, NGRP)}
            c = rdma(own_ref, all_ref.at[2 - dz, j], ss.at[n], rs.at[2 - dz, j], dev)
            c.start()
            sends.append(c)

    def from_peers(own_ref, all_ref, ss, rs):
        for n, (dj, dz) in enumerate(peers):
            s = lax.rem(j + dj, NGY)
            dev = {"gy": s, "grp": lax.rem(l + dz + NGRP - 1, NGRP)}
            rdma(own_ref, all_ref.at[dz, s], ss.at[n], rs.at[dz, s], dev).wait_recv()

    to_peers(CSO, CS, css, csr)
    CS[1, j] = CSO[...]

    for d in range(1, NGRP):
        s = lax.rem(l + d, NGRP)
        rdma(W2.at[l], W2.at[s], a2s.at[d], a2r.at[s], {"grp": s}).wait_recv()
    acc8 = W2[0]
    for s in range(1, NGRP):
        acc8 = acc8 + W2[s]
    bhp = jnp.where(sub < 4, acc8 / jnp.where(sub < 4, pltpu.roll(acc8, 4, 0), 1.0), 0.0)
    mine = pltpu.roll(jnp.where(sub == own_row, bhp, 0.0), lax.rem(128 - shift, 128), 1)
    bhp_out[...] = jnp.sum(mine, axis=0, keepdims=True)[:, 0:8]
    bhp_c = jnp.sum(
        jnp.where(sub == q_hi, nn(bhp, pick), 0.0), axis=0, keepdims=True
    )

    cx, cy, ck = cb // 128, lax.rem(cb // 8, 16), lax.rem(cb, 8)
    spot = (sub128 == (cx // 4) * 32 + (cy // 4) * 8 + ck).astype(F32)
    CBO[...] = scale * (nt(total * bhp_c, spot) - r_c)
    to_peers(CBO, CB, cbs, cbr)
    CB[1, j] = CBO[...]

    ends_s = [
        rdma(SA.at[0], RA.at[1], ras.at[0], rar.at[0], {"grp": l_lo}),
        rdma(SA.at[1], RA.at[0], ras.at[1], rar.at[1], {"grp": l_hi}),
        rdma(SB.at[0], RB.at[1], ras.at[2], rar.at[2], {"grp": l_lo}),
        rdma(SB.at[1], RB.at[0], ras.at[3], rar.at[3], {"grp": l_hi}),
    ]
    pack_ends([flat(r) for r in (AXL, AXH, AYL, AYH, AZL, AZH)], SA.at[0], SA.at[1])
    ends_s[0].start()
    ends_s[1].start()
    AZL2, AZH2 = AZL.reshape(2048, 128), AZH.reshape(2048, 128)
    for part in range(4):
        AR[pl.ds(part * 64, 64)] = jnp.where(
            lane64 < 64, end_rows(AZL2, part, 0, 0, 16), end_rows(AZH2, part, 7, 0, 16)
        )

    bhp_col = jnp.sum(jnp.where(sub128 == lane128, bhp_c, 0.0), axis=1, keepdims=True)
    wb_parts = halves(wi * bhp_col)

    def finish(x, _):
        BB[x] = BB[x] + CC[x] * blocks(x, wb_parts)
        return 0

    lax.fori_loop(0, 16, finish, 0)
    pack_tile([flat(BB)], SB.at[0], SB.at[1])
    ends_s[2].start()
    ends_s[3].start()

    def joined(all_ref):
        block = lax.rem(lane, 32) // 8
        for g in range(NGY):
            for y in range(4):
                u = None
                for dz in range(3):
                    t = all_ref[dz, g]
                    to = (8 * (dz - y)) % 128
                    t = pltpu.roll(t, to, 1) if to else t
                    u = jnp.where(block == dz, t, 0.0 if u is None else u)
                UU[g * 4 + y] = u

    UU2 = UU.reshape(128, 128)
    from_peers(CSO, CS, css, csr)
    joined(CS)
    coef = [UU2[pl.ds(n, 16, stride=8), :] for n in range(6)]
    from_peers(CBO, CB, cbs, cbr)
    joined(CB)
    rhs = UU2[pl.ds(0, 16, stride=8), :]

    def coarse_step(_, v):
        return (
            (KEEP * v + rhs)
            + (coef[0] * pltpu.roll(v, 32, 1) + coef[1] * pltpu.roll(v, 96, 1))
            + (coef[2] * pltpu.roll(v, 1, 0) + coef[3] * pltpu.roll(v, 15, 0))
            + (coef[4] * pltpu.roll(v, 1, 1) + coef[5] * pltpu.roll(v, 127, 1))
        )

    v = lax.fori_loop(0, 7, coarse_step, rhs)
    mine = jnp.zeros((8, 128), F32)
    for g in range(NGY):
        mine = jnp.where(j == g, pltpu.roll(v, (17 - 4 * g) % 16, 0)[0:8], mine)
    VO[...] = mine
    vx_lo = rdma(VO, VX.at[1], vxs.at[0], vxr.at[0], {"gx": i_lo})
    vx_hi = rdma(VO, VX.at[0], vxs.at[1], vxr.at[1], {"gx": i_hi})
    vx_lo.start()
    vx_hi.start()

    def upright(tile):
        return jnp.transpose(jnp.concatenate([tile] * 16, axis=0))

    def cell(up, big, row):
        t = jnp.where(lane == row, up[big * 32 + 8 : big * 32 + 16], 0.0)
        return jnp.broadcast_to(jnp.sum(t, axis=1, keepdims=True), (8, 128))

    up = upright(mine)
    for big in range(4):
        for row in range(6):
            t = cell(up, big, row)
            ys = (0,) if row == 0 else (17,) if row == 5 else range(row * 4 - 3, row * 4 + 1)
            for x in range(4):
                for y in ys:
                    D[0, 1 + big * 4 + x, y] = t
    sub16 = iota((16, 128), 0)
    y_lo = y_hi = jnp.zeros((16, 128), F32)
    for big in range(4):
        lo, hi = [
            jnp.sum(jnp.where(lane == big * 32 + at, mine, 0.0), axis=1, keepdims=True)
            for at in (7, 16)
        ]
        e = jnp.where(lane < 64, hi, lo)
        rows = jnp.zeros((16, 128), F32)
        for y in range(4):
            rows = jnp.where(sub16 // 4 == y, e[y + 1 : y + 2], rows)
        for u in range(4):
            E[0, pl.ds((big * 4 + u) * 16, 16)] = rows
        y_lo = jnp.where(sub16 // 4 == big, e[0:1], y_lo)
        y_hi = jnp.where(sub16 // 4 == big, e[5:6], y_hi)
    EY[0, 0] = y_lo
    EY[0, 1] = y_hi
    ex_lo = rdma(E.at[0, pl.ds(0, 16)], EX.at[0, 1], sws.at[0, 4], swr.at[0, 4], {"gx": i_lo})
    ex_hi = rdma(E.at[0, pl.ds(240, 16)], EX.at[0, 0], sws.at[0, 5], swr.at[0, 5], {"gx": i_hi})
    ex_lo.start()
    ex_hi.start()
    D2 = D.reshape(4 * 18 * 18 * 8, 128)
    E2 = E.reshape(4 * 256, 128)

    def faces(s):
        for part in range(4):
            base = (s * 18 * 18 + 19) * 8
            rows = pl.ds(part * 64, 64)
            m = jnp.where(
                lane64 < 64, end_rows(D2, part, 0, base, 18), end_rows(D2, part, 7, base, 18)
            )
            FA[rows] = m
            d = E[s, rows] - m
            FR[rows] = AR[rows] * jnp.where(
                lane64 < 64, pltpu.roll(d, 1, 1), pltpu.roll(d, 127, 1)
            )

    def columns(s, x, y, n, along_x=False):
        at = (pl.ds(x, n), y) if along_x else (x, pl.ds(y, n))

        def near(dx, dy):
            if along_x:
                return D[s, pl.ds(x + 1 + dx, n), y + 1 + dy]
            return D[s, x + 1 + dx, pl.ds(y + 1 + dy, n)]

        v = near(0, 0)
        shape = (n, 8, 128)
        k, z = iota(shape, 1), iota(shape, 2)
        ends = ((k == 0) & (z == 0)) | ((k == 7) & (z == 127))
        fix = jnp.concatenate(
            [
                jnp.broadcast_to(
                    FR[pl.ds(x * 16 + y + u * (16 if along_x else 1), 1), :], (8, 128)
                )[None]
                for u in range(n)
            ],
            axis=0,
        )
        return (
            (KEEP * v + BB[at])
            + (AXL[at] * near(-1, 0) + AXH[at] * near(1, 0))
            + (AYL[at] * near(0, -1) + AYH[at] * near(0, 1))
            + (AZL[at] * z_below(v) + AZH[at] * z_above(v))
            + jnp.where(ends, fix, 0.0)
        )

    def beyond(s):
        shape = (4, 16, 128)
        y, z = iota(shape, 1), iota(shape, 2)

        def each_y(ref, part):
            return jnp.concatenate(
                [
                    jnp.broadcast_to(ref[pl.ds(part * 4 + u, 1), :], (16, 128))[None]
                    for u in range(4)
                ],
                axis=0,
            )

        for part in range(4):
            rows = pl.ds(part * 64, 64)
            e = E[s, rows].reshape(shape)
            if part == 0:
                left = jnp.concatenate([EX[s, 0], E[s, pl.ds(0, 48)]], axis=0)
            else:
                left = E[s, pl.ds(part * 64 - 16, 64)]
            if part == 3:
                right = jnp.concatenate([E[s, pl.ds(208, 48)], EX[s, 1]], axis=0)
            else:
                right = E[s, pl.ds(part * 64 + 16, 64)]
            a = [AE[n, rows].reshape(shape) for n in range(7)]
            m = FA[rows].reshape(shape)
            new = (
                (KEEP * e + a[6])
                + (a[0] * left.reshape(shape) + a[1] * right.reshape(shape))
                + (
                    a[2] * jnp.where(y == 0, each_y(EY.at[s, 0], part), pltpu.roll(e, 1, 1))
                    + a[3] * jnp.where(y == 15, each_y(EY.at[s, 1], part), pltpu.roll(e, 15, 1))
                )
                + (
                    a[4] * jnp.where(z == 0, pltpu.roll(m, 1, 2), pltpu.roll(e, 1, 2))
                    + a[5] * jnp.where(z == 127, pltpu.roll(m, 127, 2), pltpu.roll(e, 127, 2))
                )
            )
            E[s + 1, rows] = new.reshape(64, 128)
        EYS[s + 1, 0] = E2[pl.ds((s + 1) * 256, 16, stride=16), :]
        EYS[s + 1, 1] = E2[pl.ds((s + 1) * 256 + 15, 16, stride=16), :]

    def exchange(s):
        ss, rs = sws.at[s], swr.at[s]
        lo, hi = {"gy": lax.max(j - 1, 0)}, {"gy": lax.min(j + 1, 3)}
        x_d = [
            rdma(D.at[s, 1, inner], D.at[s, 17, inner], ss.at[2], rs.at[2], {"gx": i_lo}),
            rdma(D.at[s, 16, inner], D.at[s, 0, inner], ss.at[3], rs.at[3], {"gx": i_hi}),
        ]
        x_e = [
            rdma(E.at[s, pl.ds(0, 16)], EX.at[s, 1], ss.at[4], rs.at[4], {"gx": i_lo}),
            rdma(E.at[s, pl.ds(240, 16)], EX.at[s, 0], ss.at[5], rs.at[5], {"gx": i_hi}),
        ]
        down_d = rdma(D.at[s, inner, 1], D.at[s, inner, 17], ss.at[0], rs.at[0], lo)
        up_d = rdma(D.at[s, inner, 16], D.at[s, inner, 0], ss.at[1], rs.at[1], hi)
        down_e = rdma(EYS.at[s, 0], EY.at[s, 1], ss.at[6], rs.at[6], lo)
        up_e = rdma(EYS.at[s, 1], EY.at[s, 0], ss.at[7], rs.at[7], hi)
        return x_d, x_e, down_d, up_d, down_e, up_e

    def put_d(s):
        def put(x, y, new, along_x=False):
            n = new.shape[0]
            if along_x:
                D[s, pl.ds(x + 1, n), y + 1] = new
            else:
                D[s, x + 1, pl.ds(y + 1, n)] = new

        return put

    def put_out(x, y, new, along_x=False):
        for u in range(new.shape[0]):
            xu, yu = (x + u, y) if along_x else (x, y + u)
            row = xu * 128 + yu // 8 * 64 + yu % 8
            out_ref[pl.ds(row, 8, stride=8), :] = new[u]

    def inside(s, put):
        def body(x, _):
            for y in (1, 8):
                put(x, y, columns(s, x, y, 7))
            return 0

        lax.fori_loop(1, 15, body, 0)

    def y_planes(s, put):
        def body(g, _):
            for y in (0, 15):
                put(g * 4, y, columns(s, g * 4, y, 4, True), True)
            return 0

        lax.fori_loop(0, 4, body, 0)

    def x_planes(s, put):
        for x in (0, 15):
            for y in (1, 8):
                put(x, y, columns(s, x, y, 7))

    faces(0)
    inside(0, put_d(1))
    for c in (ex_lo, ex_hi):
        c.wait_recv()
    vx_lo.wait_recv()
    vx_hi.wait_recv()
    for n, big, at in ((0, 3, 0), (1, 0, 17)):
        up = upright(VX[n])
        for row in range(1, 5):
            t = cell(up, big, row)
            for y in range(row * 4 - 3, row * 4 + 1):
                D[0, at, y] = t

    def step(s, put):
        x_d, x_e, down_d, up_d, down_e, up_e = exchange(s + 1)
        y_planes(s, put_d(s + 1))

        @pl.when(j > 0)
        def _():
            down_d.start()

        @pl.when(j < NGY - 1)
        def _():
            up_d.start()

        x_planes(s, put_d(s + 1))
        for c in x_d:
            c.start()

        @pl.when(s == 0)
        def _():
            for c in ends_s:
                c.wait_recv()
            for part in range(4):
                for n in range(6):
                    at = part * 32 + n * 4
                    AE[n, pl.ds(part * 64, 64)] = jnp.where(
                        lane64 < 4,
                        pltpu.roll(RA[1], (128 - at) % 128, 1) if at else RA[1],
                        jnp.where(lane64 >= 124, pltpu.roll(RA[0], 124 - at, 1), 0.0),
                    )
            for g in range(32):
                AE[6, pl.ds(g * 8, 8)] = jnp.where(
                    lane < 4,
                    pltpu.roll(RB[1], (128 - g * 4) % 128, 1) if g else RB[1],
                    jnp.where(lane >= 124, pltpu.roll(RB[0], 124 - g * 4, 1) if g < 31 else RB[0], 0.0),
                )

        beyond(s)
        for c in x_e:
            c.start()

        @pl.when(j > 0)
        def _():
            down_e.start()

        @pl.when(j < NGY - 1)
        def _():
            up_e.start()

        faces(s + 1)
        inside(s + 1, put)

        @pl.when(j > 0)
        def _():
            for c in (down_d, down_e):
                c.wait_send()
            for c in (up_d, up_e):
                c.wait_recv()

        @pl.when(j < NGY - 1)
        def _():
            for c in (up_d, up_e):
                c.wait_send()
            for c in (down_d, down_e):
                c.wait_recv()

        for c in x_d + x_e:
            c.wait()

    def step_on(s, _):
        step(s, put_d(s + 2))
        return 0

    lax.fori_loop(0, 2, step_on, 0)
    step(2, put_out)
    y_planes(3, put_out)
    x_planes(3, put_out)

    for c in sends + xs + ends_s + [zc_lo, zc_hi, vx_lo, vx_hi, ex_lo, ex_hi]:
        c.wait_send()

    @pl.when(j > 0)
    def _():
        for c in y_down:
            c.wait_send()

    @pl.when(j < NGY - 1)
    def _():
        for c in y_up:
            c.wait_send()


def tiles(a):
    return a.reshape(16, 2, 8, 8, 128).transpose(0, 1, 3, 2, 4)


def per_device(
    pressure,
    pressure_old,
    accumulation,
    permeability,
    comp_block,
    comp_owner,
    comp_well,
    comp_wi,
    well_rate,
    well_storage,
    well_bhp_old,
):
    perm = permeability.reshape(3, 16, 2, 8, 8, 128).transpose(0, 1, 2, 4, 3, 5)
    hbm = pl.BlockSpec(memory_space=pltpu.HBM)
    vmem = pl.BlockSpec(memory_space=pltpu.VMEM)
    smem = pl.BlockSpec(memory_space=pltpu.SMEM)
    grid = (16, 16, 8, 128)
    dma = pltpu.SemaphoreType.DMA
    cb = comp_block.reshape(1, 128)

    def vm(*shape):
        return pltpu.VMEM(shape, F32)

    out, bhp = pl.pallas_call(
        kernel,
        out_shape=(
            jax.ShapeDtypeStruct((2048, 128), F32),
            jax.ShapeDtypeStruct((1, 8), F32),
        ),
        in_specs=[smem] + [hbm] * 4 + [vmem] * 7,
        out_specs=(vmem, vmem),
        scratch_shapes=[
            vm(16, 2, 8, 8, 128),
            vm(18, 18, 8, 128),
            vm(*grid),
            vm(*grid),
            vm(18, 16, 8, 128),
            vm(16, 18, 8, 128),
            vm(*grid),
            vm(*grid),
            vm(*grid),
            vm(*grid),
            vm(*grid),
            vm(*grid),
            vm(*grid),
            vm(*grid),
            vm(*grid),
            vm(4, 18, 18, 8, 128),
            pltpu.VMEM((16, 128, 128), jnp.bfloat16),
            vm(128, 128),
            vm(8, 128),
            vm(8, 8, 128),
            vm(8, 8, 128),
            vm(256, 128),
            vm(256, 128),
            vm(2, 8, 128),
            vm(2, 8, 128),
            vm(2, 64, 128),
            vm(2, 64, 128),
            vm(2, 8, 128),
            vm(2, 8, 128),
            vm(7, 256, 128),
            vm(4, 256, 128),
            vm(4, 2, 16, 128),
            vm(4, 2, 16, 128),
            vm(4, 2, 16, 128),
            vm(256, 128),
            vm(256, 128),
            vm(256, 128),
            vm(16, 8, 128),
            vm(8, 16, 8, 128),
            vm(8, 128),
            vm(8, 128),
            vm(3, 4, 8, 128),
            vm(3, 4, 8, 128),
            vm(8, 128),
            vm(2, 8, 128),
            dma((7,)),
            dma((8,)),
            dma((8,)),
            dma((8,)),
            dma((8,)),
            dma((10,)),
            dma((10,)),
            dma((11,)),
            dma((3, 4)),
            dma((11,)),
            dma((3, 4)),
            dma((2,)),
            dma((2,)),
            dma((4,)),
            dma((4,)),
            dma((4, 8)),
            dma((4, 8)),
        ],
        compiler_params=pltpu.CompilerParams(
            collective_id=0, has_side_effects=True, vmem_limit_bytes=60 * 1024 * 1024
        ),
    )(
        cb,
        tiles(pressure),
        tiles(pressure_old),
        tiles(accumulation),
        perm,
        cb,
        comp_owner.reshape(1, 128),
        comp_well.reshape(1, 128),
        comp_wi.reshape(128, 128),
        well_rate.reshape(1, 8),
        well_storage.reshape(1, 8),
        well_bhp_old.reshape(1, 8),
    )
    delta = out.reshape(16, 2, 8, 8, 128).transpose(0, 1, 3, 2, 4).reshape(16, 16, 1024)
    return pressure + delta, bhp.reshape(1, 1, 1, 8)


def solution(mesh):
    return jax.shard_map(
        per_device,
        mesh=mesh,
        in_specs=(
            P("gx", "gy", "grp"),
            P("gx", "gy", "grp"),
            P("gx", "gy", "grp"),
            P(None, "gx", "gy", "grp"),
            P("gx", "gy", "grp", None),
            P("gx", "gy", "grp", None, None),
            P("gx", "gy", "grp", None),
            P("gx", "gy", "grp", None, None),
            P("gx", "gy", "grp", None),
            P("gx", "gy", "grp", None),
            P("gx", "gy", "grp", None),
        ),
        out_specs=(P("gx", "gy", "grp"), P("gx", "gy", "grp", None)),
        check_vma=False,
    )
```

```python
import jax
import jax.numpy as jnp
from jax import lax
from jax.experimental import pallas as pl
from jax.experimental.pallas import tpu as pltpu
from jax.sharding import PartitionSpec as P

MESH = pl.DeviceIdType.MESH
F32 = jnp.float32
RELAX = 0.7
KEEP = 1.0 - RELAX
NGX, NGY, NGRP = 8, 4, 8
HIGH = lax.Precision.HIGHEST


def iota(shape, dim):
    return lax.broadcasted_iota(jnp.int32, shape, dim)


def nt(a, b):
    return lax.dot_general(
        a, b, (((1,), (1,)), ((), ())), precision=HIGH, preferred_element_type=F32
    )


def nn(a, b):
    return jnp.dot(a, b, precision=HIGH, preferred_element_type=F32)


def rcp(x):
    r = pl.reciprocal(x, approx=True)
    return r * (2.0 - x * r)


def harm(a, b):
    return 2.0 * a * b * rcp(a + b)


def z_below(v):
    r = pltpu.roll(v, 1, 2)
    return jnp.where(iota(v.shape, 2) == 0, pltpu.roll(r, 1, 1), r)


def z_above(v):
    r = pltpu.roll(v, 127, 2)
    return jnp.where(iota(v.shape, 2) == 127, pltpu.roll(r, 7, 1), r)


def kernel(
    cb_s,
    p_hbm,
    po_hbm,
    ac_hbm,
    k_hbm,
    cb_v,
    ow_v,
    cw_v,
    wi_v,
    rate_v,
    stor_v,
    old_v,
    out_ref,
    bhp_out,
    PG,
    PP,
    PO,
    AC,
    KX,
    KY,
    KZ,
    TX,
    TY,
    TZL,
    TZH,
    AXL,
    AXH,
    AYL,
    AYH,
    AZL,
    AZH,
    CC,
    BB,
    D,
    OH,
    PR,
    OWN,
    W1,
    W2,
    HZP,
    HZK,
    ZS0,
    ZI,
    SA,
    RA,
    SB,
    RB,
    AE,
    E,
    EX,
    EY,
    EYS,
    FA,
    AR,
    FR,
    UU,
    CQ,
    CSO,
    CBO,
    CS,
    CB,
    VO,
    VX,
    lsem,
    a1s,
    a1r,
    a2s,
    a2r,
    ihs,
    ihr,
    css,
    csr,
    cbs,
    cbr,
    vxs,
    vxr,
    ras,
    rar,
    sws,
    swr,
):
    i = lax.axis_index("gx")
    j = lax.axis_index("gy")
    l = lax.axis_index("grp")
    i_lo, i_hi = lax.rem(i + NGX - 1, NGX), lax.rem(i + 1, NGX)
    l_lo, l_hi = lax.rem(l + NGRP - 1, NGRP), lax.rem(l + 1, NGRP)

    def rdma(src, dst, ss, rs, dev):
        return pltpu.make_async_remote_copy(
            src_ref=src, dst_ref=dst, send_sem=ss, recv_sem=rs, device_id=dev, device_id_type=MESH
        )

    bar = pltpu.get_barrier_semaphore()

    def greet(dev):
        pl.semaphore_signal(bar, inc=1, device_id=dev, device_id_type=MESH)

    for d in range(1, NGX):
        greet({"gx": lax.rem(i + d, NGX)})
    for d in range(1, NGRP):
        greet({"grp": lax.rem(l + d, NGRP)})
    for dj in range(1, NGY):
        for dz in range(3):
            greet({"gy": lax.rem(j + dj, NGY), "grp": lax.rem(l + dz + NGRP - 1, NGRP)})

    load_g = pltpu.make_async_copy(p_hbm, PG, lsem.at[0])
    load_g.start()

    def load_kz(ys, _):
        for yt in range(2):
            pltpu.make_async_copy(
                k_hbm.at[2, :, yt, :, ys, :], KZ.at[:, yt * 8 + ys], lsem.at[4]
            ).start()
        return 0

    lax.fori_loop(0, 8, load_kz, 0)

    def load(ys, _):
        for yt in range(2):
            y = yt * 8 + ys
            pltpu.make_async_copy(
                p_hbm.at[:, yt, :, ys, :], PP.at[pl.ds(1, 16), 1 + y], lsem.at[1]
            ).start()
            pltpu.make_async_copy(
                k_hbm.at[0, :, yt, :, ys, :], KX.at[pl.ds(1, 16), y], lsem.at[2]
            ).start()
            pltpu.make_async_copy(
                k_hbm.at[1, :, yt, :, ys, :], KY.at[:, 1 + y], lsem.at[3]
            ).start()
            pltpu.make_async_copy(po_hbm.at[:, yt, :, ys, :], PO.at[:, y], lsem.at[5]).start()
            pltpu.make_async_copy(ac_hbm.at[:, yt, :, ys, :], AC.at[:, y], lsem.at[6]).start()
        return 0

    lax.fori_loop(0, 8, load, 0)

    load_g.wait()

    def gather(g, _):
        for u in range(8):
            b = cb_s[0, g * 8 + u]
            x, y, k = b // 128, lax.rem(b // 8, 16), lax.rem(b, 8)
            PR[pl.ds(g * 8 + u, 1), :] = PG[x, y // 8, k, pl.ds(lax.rem(y, 8), 1), :]
        return 0

    lax.fori_loop(0, 16, gather, 0)
    wi = wi_v[...]
    sub = iota((8, 128), 0)
    lane = iota((8, 128), 1)
    sub128 = iota((128, 128), 0)
    lane128 = iota((128, 128), 1)
    ones8 = jnp.ones((8, 128), F32)
    weighted = nt(ones8, wi * PR[...])
    total = nt(ones8, wi)
    cb = cb_v[...]
    q = ow_v[...] * 8 + cw_v[...]
    q_hi, q_lo = q // 128, lax.rem(q, 128)
    pick = (sub128 == q_lo).astype(F32)
    share = nt(
        jnp.where(sub == q_hi, weighted, 0.0) + jnp.where(sub == q_hi + 4, total, 0.0), pick
    )
    own = i * NGRP + l
    own_row, shift = own // 16, lax.rem(own, 16) * 8
    OWN[...] = jnp.zeros((8, 128), F32)
    OWN[0:1, 0:8] = stor_v[...] * old_v[...] - rate_v[...]
    OWN[1:2, 0:8] = stor_v[...]
    placed = pltpu.roll(OWN[...], shift, 1)
    share = (
        share
        + jnp.where(sub == own_row, placed[0:1], 0.0)
        + jnp.where(sub == own_row + 4, placed[1:2], 0.0)
    )
    W1[i] = share

    lane64 = iota((64, 128), 1)

    def end_rows(ref, part, k, base, width):
        return jnp.concatenate(
            [
                ref[pl.ds(base + (part * 4 + u) * width * 8 + k, 16, stride=8), :]
                for u in range(4)
            ],
            axis=0,
        )

    KZ2 = KZ.reshape(2048, 128)

    def flat(ref):
        ref2 = ref.reshape(2048, 128)
        return (
            lambda part: end_rows(ref2, part, 0, 0, 16),
            lambda part: end_rows(ref2, part, 7, 0, 16),
        )

    def raw_rows(k):
        def rows(part):
            return jnp.concatenate(
                [PG[part * 4 + u, yt, k] for u in range(4) for yt in range(2)], axis=0
            )

        return rows

    def pack_tile(refs, lo_ref, hi_ref):
        keep = 4 if len(refs) == 1 else 1
        lo = hi = jnp.zeros((8, 128), F32)
        for part in range(4):
            for n, ends in enumerate(refs):
                a, b = ends[0](part), ends[1](part)
                for u in range(8):
                    to = part * 32 + u * 4 + n
                    at = slice(u * 8, u * 8 + 8)
                    a8 = jnp.where(lane < keep, a[at], 0.0)
                    b8 = jnp.where(lane >= 128 - keep, b[at], 0.0)
                    lo = lo + (pltpu.roll(a8, to, 1) if to else a8)
                    hi = hi + pltpu.roll(b8, (to + keep) % 128, 1)
        lo_ref[...] = lo
        hi_ref[...] = hi

    def pack_ends(refs, lo_ref, hi_ref):
        lo = hi = jnp.zeros((64, 128), F32)
        for part in range(4):
            for n, ends in enumerate(refs):
                to = part * 32 + n * 4
                a = jnp.where(lane64 < 4, ends[0](part), 0.0)
                b = jnp.where(lane64 >= 124, ends[1](part), 0.0)
                lo = lo + (pltpu.roll(a, to, 1) if to else a)
                hi = hi + pltpu.roll(b, to + 4, 1)
        lo_ref[...] = lo
        hi_ref[...] = hi

    pltpu.make_async_copy(KZ, KZ, lsem.at[4]).wait()
    pack_tile([(raw_rows(0), raw_rows(7)), flat(KZ)], ZS0.at[0], ZS0.at[1])


    pl.semaphore_wait(bar, 23)

    sends = []
    for d in range(1, NGX):
        c = rdma(W1.at[i], W1.at[i], a1s.at[d], a1r.at[i], {"gx": lax.rem(i + d, NGX)})
        c.start()
        sends.append(c)

    zc_lo = rdma(ZS0.at[0], ZI.at[1], ihs.at[0], ihr.at[0], {"grp": l_lo})
    zc_hi = rdma(ZS0.at[1], ZI.at[0], ihs.at[1], ihr.at[1], {"grp": l_hi})
    zc_lo.start()
    zc_hi.start()

    zplane = jnp.zeros((16, 8, 128), F32)

    @pl.when(j == 0)
    def _():
        PP[pl.ds(1, 16), 0] = zplane
        for s in range(1, 4):
            D[s, pl.ds(1, 16), 0] = zplane
            EY[s, 0] = jnp.zeros((16, 128), F32)

    @pl.when(j == NGY - 1)
    def _():
        PP[pl.ds(1, 16), 17] = zplane
        for s in range(1, 4):
            D[s, pl.ds(1, 16), 17] = zplane
            EY[s, 1] = jnp.zeros((16, 128), F32)

    inner = pl.ds(1, 16)
    pltpu.make_async_copy(KZ, KX.at[pl.ds(1, 16)], lsem.at[2]).wait()
    pltpu.make_async_copy(KZ, KY.at[:, pl.ds(1, 16)], lsem.at[3]).wait()
    pltpu.make_async_copy(KZ, PP.at[pl.ds(1, 16), pl.ds(1, 16)], lsem.at[1]).wait()
    xs = [
        rdma(KX.at[1], KX.at[17], ihs.at[2], ihr.at[2], {"gx": i_lo}),
        rdma(KX.at[16], KX.at[0], ihs.at[3], ihr.at[3], {"gx": i_hi}),
        rdma(PP.at[1, inner], PP.at[17, inner], ihs.at[4], ihr.at[4], {"gx": i_lo}),
        rdma(PP.at[16, inner], PP.at[0, inner], ihs.at[5], ihr.at[5], {"gx": i_hi}),
    ]
    for c in xs:
        c.start()
    y_down = [
        rdma(KY.at[:, 1], KY.at[:, 17], ihs.at[6], ihr.at[6], {"gy": lax.max(j - 1, 0)}),
        rdma(PP.at[inner, 1], PP.at[inner, 17], ihs.at[7], ihr.at[7], {"gy": lax.max(j - 1, 0)}),
    ]
    y_up = [
        rdma(KY.at[:, 16], KY.at[:, 0], ihs.at[8], ihr.at[8], {"gy": lax.min(j + 1, 3)}),
        rdma(PP.at[inner, 16], PP.at[inner, 0], ihs.at[9], ihr.at[9], {"gy": lax.min(j + 1, 3)}),
    ]

    @pl.when(j > 0)
    def _():
        for c in y_down:
            c.start()

    @pl.when(j < NGY - 1)
    def _():
        for c in y_up:
            c.start()

    def onehot(x, _):
        OH[x] = (sub128 + x * 128 == cb).astype(F32).astype(jnp.bfloat16)
        return 0

    lax.fori_loop(0, 16, onehot, 0)

    def halves(v):
        hi = v.astype(jnp.bfloat16)
        lo = (v - hi.astype(F32)).astype(jnp.bfloat16)
        return jnp.concatenate([hi, lo], axis=1)

    def blocks(x, n, parts):
        rows = OH[pl.ds(x, n)].reshape(n * 128, 128)
        r = jnp.dot(rows, parts, preferred_element_type=F32)
        return (r[:, :128] + r[:, 128:]).reshape(n, 16, 8, 128)

    wi_parts = halves(wi)

    CQ[...] = jnp.zeros((8, 16, 8, 128), F32)
    pltpu.make_async_copy(KZ, PO, lsem.at[5]).wait()
    pltpu.make_async_copy(KZ, AC, lsem.at[6]).wait()

    def prepare(x, _):
        w16 = blocks(x, 1, wi_parts)[0]
        for yt in range(2):
            y0 = yt * 8
            c8 = pl.ds(y0, 8)
            p = PP[x + 1, pl.ds(y0 + 1, 8)]
            acc = AC[x, c8]
            w = w16[y0 : y0 + 8]
            PO[x, c8] = acc * (p - PO[x, c8]) + w * p
            accw = acc + w
            AC[x, c8] = accw
            for yl in range(2):
                CQ[1, x // 4 * 4 + yt * 2 + yl] += accw[yl * 4 : yl * 4 + 4].sum(0)
            kz = KZ[x, c8]
            tzl = harm(z_below(kz), kz)
            TZL[x, c8] = tzl
            TZH[x, c8] = z_above(tzl)
            n = 8 - yt
            lower, upper = KY[x, pl.ds(y0 + 1, n)], KY[x, pl.ds(y0 + 2, n)]
            TY[x, pl.ds(y0 + 1, n)] = harm(lower, upper)
        return 0

    lax.fori_loop(0, 16, prepare, 0)

    def faces_x(x, _):
        for yt in range(2):
            c8 = pl.ds(yt * 8, 8)
            TX[x, c8] = harm(KX[x, c8], KX[x + 1, c8])
        return 0

    lax.fori_loop(1, 16, faces_x, 0)

    for d in range(1, NGX):
        s = lax.rem(i + d, NGX)
        rdma(W1.at[i], W1.at[s], a1s.at[d], a1r.at[s], {"gx": s}).wait_recv()
    acc8 = W1[0]
    for s in range(1, NGX):
        acc8 = acc8 + W1[s]
    W2[l] = acc8
    for d in range(1, NGRP):
        c = rdma(W2.at[l], W2.at[l], a2s.at[d], a2r.at[l], {"grp": lax.rem(l + d, NGRP)})
        c.start()
        sends.append(c)

    for c in xs:
        c.wait_recv()

    @pl.when(j > 0)
    def _():
        for c in y_up:
            c.wait_recv()

    @pl.when(j < NGY - 1)
    def _():
        for c in y_down:
            c.wait_recv()

    @pl.when(i == 0)
    def _():
        KX[0] = zplane

    @pl.when(i == NGX - 1)
    def _():
        KX[17] = zplane

    @pl.when(j == 0)
    def _():
        KY[:, 0] = zplane

    @pl.when(j == NGY - 1)
    def _():
        KY[:, 17] = zplane

    for x in (0, 16):
        TX[x] = harm(KX[x], KX[x + 1])
    for y in (0, 16):
        TY[:, y] = harm(KY[:, y], KY[:, y + 1])
    zc_lo.wait_recv()
    zc_hi.wait_recv()
    has_lo = (l > 0).astype(F32)
    has_hi = (l < NGRP - 1).astype(F32)
    for g in range(32):
        for n, ref in enumerate((HZP, HZK)):
            lo = pltpu.roll(ZI[0], (128 - g * 4 - n) % 128, 1) if g + n else ZI[0]
            hi = pltpu.roll(ZI[1], 127 - g * 4 - n, 1)
            if n:
                lo, hi = lo * has_lo, hi * has_hi
            ref[pl.ds(g * 8, 8)] = jnp.where(lane == 0, lo, hi)

    for part in range(4):
        rows = pl.ds(part * 64, 64)
        k_end = jnp.where(
            lane64 < 64, end_rows(KZ2, part, 0, 0, 16), end_rows(KZ2, part, 7, 0, 16)
        )
        HZK[rows] = harm(k_end, HZK[rows])
    sh3 = (8, 8, 128)
    first = (iota(sh3, 2) == 0) & (iota(sh3, 1) == 0)
    last = (iota(sh3, 2) == 127) & (iota(sh3, 1) == 7)

    def column(ref, n):
        return jnp.concatenate(
            [jnp.broadcast_to(ref[pl.ds(n + u, 1), :], (8, 128))[None] for u in range(8)], axis=0
        )

    def operator(x, _):
        big = x // 4
        f_lo = (lax.rem(x, 4) == 0).astype(F32)
        f_hi = (lax.rem(x, 4) == 3).astype(F32)
        for yt in range(2):
            y0 = yt * 8
            c8 = pl.ds(y0, 8)
            txl, txh = TX[x, c8], TX[x + 1, c8]
            tyl, tyh = TY[x, c8], TY[x, pl.ds(y0 + 1, 8)]
            tk = column(HZK, x * 16 + y0)
            tzl = jnp.where(first, tk, TZL[x, c8])
            tzh = jnp.where(last, tk, TZH[x, c8])
            tsum = ((txl + txh) + (tyl + tyh)) + (tzl + tzh)
            p = PP[x + 1, pl.ds(y0 + 1, 8)]
            hp = column(HZP, x * 16 + y0)
            nb = (
                (txl * PP[x, pl.ds(y0 + 1, 8)] + txh * PP[x + 2, pl.ds(y0 + 1, 8)])
                + (tyl * PP[x + 1, c8] + tyh * PP[x + 1, pl.ds(y0 + 2, 8)])
                + (
                    tzl * jnp.where(first, hp, z_below(p))
                    + tzh * jnp.where(last, hp, z_above(p))
                )
            )
            r0 = PO[x, c8] + tsum * p - nb
            c = RELAX * rcp(AC[x, c8] + tsum)
            AXL[x, c8] = c * txl
            AXH[x, c8] = c * txh
            AYL[x, c8] = c * tyl
            AYH[x, c8] = c * tyh
            AZL[x, c8] = c * tzl
            AZH[x, c8] = c * tzh
            CC[x, c8] = c
            BB[x, c8] = -c * r0
            for yl in range(2):
                n = big * 4 + yt * 2 + yl
                part = slice(yl * 4, yl * 4 + 4)
                CQ[0, n] += r0[part].sum(0)
                CQ[2, n] += txl[part].sum(0) * f_lo
                CQ[3, n] += txh[part].sum(0) * f_hi
                CQ[4, n] += tyl[yl * 4]
                CQ[5, n] += tyh[yl * 4 + 3]
                CQ[6, n] += tzl[part].sum(0)
                CQ[7, n] += tzh[part].sum(0)
        return 0

    lax.fori_loop(0, 16, operator, 0)

    sh4 = (16, 8, 128)
    lane4 = iota(sh4, 2)
    place4 = lane4 == iota(sh4, 0) * 8 + iota(sh4, 1)

    def coarse_of(n):
        v = CQ[n]
        if n == 6:
            v = jnp.where(lane4 == 0, v, 0.0)
        if n == 7:
            v = jnp.where(lane4 == 127, v, 0.0)
        v = jnp.where(place4, jnp.sum(v, axis=2, keepdims=True), 0.0)
        return jnp.sum(v.sum(0), axis=0, keepdims=True)

    r_c, a_c, xl, xh, yl, yh, zl, zh = [coarse_of(n) for n in range(8)]
    scale = RELAX / (a_c + ((xl + xh) + (yl + yh)) + (zl + zh))
    lane1 = iota((1, 128), 1)
    CSO[...] = jnp.concatenate(
        [
            jnp.where(lane1 >= 32, scale * xl, 0.0),
            jnp.where(lane1 < 96, scale * xh, 0.0),
            scale * yl,
            scale * yh,
            scale * zl,
            scale * zh,
            scale,
            scale,
        ],
        axis=0,
    )
    peers = [(dj, dz) for dj in range(NGY) for dz in range(3) if (dj, dz) != (0, 1)]

    def to_peers(own_ref, all_ref, ss, rs, count):
        rows = pl.ds(0, count)
        for n, (dj, dz) in enumerate(peers):
            dev = {"gy": lax.rem(j + dj, NGY), "grp": lax.rem(l + dz + NGRP - 1, NGRP)}
            to = all_ref.at[2 - dz, j, rows]
            c = rdma(own_ref.at[rows], to, ss.at[n], rs.at[2 - dz, j], dev)
            c.start()
            sends.append(c)

    def from_peers(own_ref, all_ref, ss, rs, count):
        rows = pl.ds(0, count)
        for n, (dj, dz) in enumerate(peers):
            s = lax.rem(j + dj, NGY)
            dev = {"gy": s, "grp": lax.rem(l + dz + NGRP - 1, NGRP)}
            to = all_ref.at[dz, s, rows]
            rdma(own_ref.at[rows], to, ss.at[n], rs.at[dz, s], dev).wait_recv()

    to_peers(CSO, CS, css, csr, 8)
    CS[1, j] = CSO[...]

    for d in range(1, NGRP):
        s = lax.rem(l + d, NGRP)
        rdma(W2.at[l], W2.at[s], a2s.at[d], a2r.at[s], {"grp": s}).wait_recv()
    acc8 = W2[0]
    for s in range(1, NGRP):
        acc8 = acc8 + W2[s]
    bhp = jnp.where(sub < 4, acc8 / jnp.where(sub < 4, pltpu.roll(acc8, 4, 0), 1.0), 0.0)
    mine = pltpu.roll(jnp.where(sub == own_row, bhp, 0.0), lax.rem(128 - shift, 128), 1)
    bhp_out[...] = jnp.sum(mine, axis=0, keepdims=True)[:, 0:8]
    bhp_c = jnp.sum(
        jnp.where(sub == q_hi, nn(bhp, pick), 0.0), axis=0, keepdims=True
    )

    cx, cy, ck = cb // 128, lax.rem(cb // 8, 16), lax.rem(cb, 8)
    spot = (sub128 == (cx // 4) * 32 + (cy // 4) * 8 + ck).astype(F32)
    CBO[...] = scale * (nt(total * bhp_c, spot) - r_c)
    to_peers(CBO, CB, cbs, cbr, 1)
    CB[1, j] = CBO[...]

    ends_s = [
        rdma(SA.at[0], RA.at[1], ras.at[0], rar.at[0], {"grp": l_lo}),
        rdma(SA.at[1], RA.at[0], ras.at[1], rar.at[1], {"grp": l_hi}),
        rdma(SB.at[0], RB.at[1], ras.at[2], rar.at[2], {"grp": l_lo}),
        rdma(SB.at[1], RB.at[0], ras.at[3], rar.at[3], {"grp": l_hi}),
    ]
    pack_ends([flat(r) for r in (AXL, AXH, AYL, AYH, AZL, AZH)], SA.at[0], SA.at[1])
    ends_s[0].start()
    ends_s[1].start()
    AZL2, AZH2 = AZL.reshape(2048, 128), AZH.reshape(2048, 128)
    for part in range(4):
        AR[pl.ds(part * 64, 64)] = jnp.where(
            lane64 < 64, end_rows(AZL2, part, 0, 0, 16), end_rows(AZH2, part, 7, 0, 16)
        )

    bhp_col = jnp.sum(jnp.where(sub128 == lane128, bhp_c, 0.0), axis=1, keepdims=True)
    wb_parts = halves(wi * bhp_col)

    def finish(g, _):
        at = pl.ds(g * 4, 4)
        BB[at] = BB[at] + CC[at] * blocks(g * 4, 4, wb_parts)
        return 0

    lax.fori_loop(0, 4, finish, 0)
    pack_tile([flat(BB)], SB.at[0], SB.at[1])
    ends_s[2].start()
    ends_s[3].start()

    def joined(tile):
        block = lax.rem(lane, 32) // 8
        for g in range(NGY):
            for y in range(4):
                u = None
                for dz in range(3):
                    t = tile(dz, g)
                    to = (8 * (dz - y)) % 128
                    t = pltpu.roll(t, to, 1) if to else t
                    u = jnp.where(block == dz, t, 0.0 if u is None else u)
                UU[g * 4 + y] = u

    UU2 = UU.reshape(128, 128)
    from_peers(CSO, CS, css, csr, 8)
    joined(lambda dz, g: CS[dz, g])
    coef = [UU2[pl.ds(n, 16, stride=8), :] for n in range(6)]
    from_peers(CBO, CB, cbs, cbr, 1)
    joined(lambda dz, g: jnp.broadcast_to(CB[dz, g, 0:1], (8, 128)))
    rhs = UU2[pl.ds(0, 16, stride=8), :]

    def coarse_step(_, v):
        return (
            (KEEP * v + rhs)
            + (coef[0] * pltpu.roll(v, 32, 1) + coef[1] * pltpu.roll(v, 96, 1))
            + (coef[2] * pltpu.roll(v, 1, 0) + coef[3] * pltpu.roll(v, 15, 0))
            + (coef[4] * pltpu.roll(v, 1, 1) + coef[5] * pltpu.roll(v, 127, 1))
        )

    v = lax.fori_loop(0, 7, coarse_step, rhs)
    mine = jnp.zeros((8, 128), F32)
    for g in range(NGY):
        mine = jnp.where(j == g, pltpu.roll(v, (17 - 4 * g) % 16, 0)[0:8], mine)
    VO[...] = mine
    vx_lo = rdma(VO, VX.at[1], vxs.at[0], vxr.at[0], {"gx": i_lo})
    vx_hi = rdma(VO, VX.at[0], vxs.at[1], vxr.at[1], {"gx": i_hi})
    vx_lo.start()
    vx_hi.start()

    def upright(tile):
        return jnp.transpose(jnp.concatenate([tile] * 16, axis=0))

    def cell(up, big, row):
        t = jnp.where(lane == row, up[big * 32 + 8 : big * 32 + 16], 0.0)
        return jnp.broadcast_to(jnp.sum(t, axis=1, keepdims=True), (8, 128))

    up = upright(mine)
    for big in range(4):
        for row in range(6):
            t = cell(up, big, row)
            ys = (0,) if row == 0 else (17,) if row == 5 else range(row * 4 - 3, row * 4 + 1)
            for x in range(4):
                for y in ys:
                    D[0, 1 + big * 4 + x, y] = t
    sub16 = iota((16, 128), 0)
    y_lo = y_hi = jnp.zeros((16, 128), F32)
    for big in range(4):
        lo, hi = [
            jnp.sum(jnp.where(lane == big * 32 + at, mine, 0.0), axis=1, keepdims=True)
            for at in (7, 16)
        ]
        e = jnp.where(lane < 64, hi, lo)
        rows = jnp.zeros((16, 128), F32)
        for y in range(4):
            rows = jnp.where(sub16 // 4 == y, e[y + 1 : y + 2], rows)
        for u in range(4):
            E[0, pl.ds((big * 4 + u) * 16, 16)] = rows
        y_lo = jnp.where(sub16 // 4 == big, e[0:1], y_lo)
        y_hi = jnp.where(sub16 // 4 == big, e[5:6], y_hi)
    EY[0, 0] = y_lo
    EY[0, 1] = y_hi
    ex_lo = rdma(E.at[0, pl.ds(0, 16)], EX.at[0, 1], sws.at[0, 4], swr.at[0, 4], {"gx": i_lo})
    ex_hi = rdma(E.at[0, pl.ds(240, 16)], EX.at[0, 0], sws.at[0, 5], swr.at[0, 5], {"gx": i_hi})
    ex_lo.start()
    ex_hi.start()
    D2 = D.reshape(4 * 18 * 18 * 8, 128)
    E2 = E.reshape(4 * 256, 128)

    def faces(s):
        for part in range(4):
            base = (s * 18 * 18 + 19) * 8
            rows = pl.ds(part * 64, 64)
            m = jnp.where(
                lane64 < 64, end_rows(D2, part, 0, base, 18), end_rows(D2, part, 7, base, 18)
            )
            FA[rows] = m
            d = E[s, rows] - m
            FR[rows] = AR[rows] * jnp.where(
                lane64 < 64, pltpu.roll(d, 1, 1), pltpu.roll(d, 127, 1)
            )

    def columns(s, x, y, n, along_x=False):
        at = (pl.ds(x, n), y) if along_x else (x, pl.ds(y, n))

        def near(dx, dy):
            if along_x:
                return D[s, pl.ds(x + 1 + dx, n), y + 1 + dy]
            return D[s, x + 1 + dx, pl.ds(y + 1 + dy, n)]

        v = near(0, 0)
        shape = (n, 8, 128)
        k, z = iota(shape, 1), iota(shape, 2)
        ends = ((k == 0) & (z == 0)) | ((k == 7) & (z == 127))
        fix = jnp.concatenate(
            [
                jnp.broadcast_to(
                    FR[pl.ds(x * 16 + y + u * (16 if along_x else 1), 1), :], (8, 128)
                )[None]
                for u in range(n)
            ],
            axis=0,
        )
        return (
            (KEEP * v + BB[at])
            + (AXL[at] * near(-1, 0) + AXH[at] * near(1, 0))
            + (AYL[at] * near(0, -1) + AYH[at] * near(0, 1))
            + (AZL[at] * z_below(v) + AZH[at] * z_above(v))
            + jnp.where(ends, fix, 0.0)
        )

    def beyond(s):
        shape = (4, 16, 128)
        y, z = iota(shape, 1), iota(shape, 2)

        def each_y(ref, part):
            return jnp.concatenate(
                [
                    jnp.broadcast_to(ref[pl.ds(part * 4 + u, 1), :], (16, 128))[None]
                    for u in range(4)
                ],
                axis=0,
            )

        for part in range(4):
            rows = pl.ds(part * 64, 64)
            e = E[s, rows].reshape(shape)
            if part == 0:
                left = jnp.concatenate([EX[s, 0], E[s, pl.ds(0, 48)]], axis=0)
            else:
                left = E[s, pl.ds(part * 64 - 16, 64)]
            if part == 3:
                right = jnp.concatenate([E[s, pl.ds(208, 48)], EX[s, 1]], axis=0)
            else:
                right = E[s, pl.ds(part * 64 + 16, 64)]
            a = [AE[n, rows].reshape(shape) for n in range(7)]
            m = FA[rows].reshape(shape)
            new = (
                (KEEP * e + a[6])
                + (a[0] * left.reshape(shape) + a[1] * right.reshape(shape))
                + (
                    a[2] * jnp.where(y == 0, each_y(EY.at[s, 0], part), pltpu.roll(e, 1, 1))
                    + a[3] * jnp.where(y == 15, each_y(EY.at[s, 1], part), pltpu.roll(e, 15, 1))
                )
                + (
                    a[4] * jnp.where(z == 0, pltpu.roll(m, 1, 2), pltpu.roll(e, 1, 2))
                    + a[5] * jnp.where(z == 127, pltpu.roll(m, 127, 2), pltpu.roll(e, 127, 2))
                )
            )
            E[s + 1, rows] = new.reshape(64, 128)
        EYS[s + 1, 0] = E2[pl.ds((s + 1) * 256, 16, stride=16), :]
        EYS[s + 1, 1] = E2[pl.ds((s + 1) * 256 + 15, 16, stride=16), :]

    gy_lo, gy_hi = {"gy": lax.max(j - 1, 0)}, {"gy": lax.min(j + 1, 3)}

    def planes_of(s):
        ss, rs = sws.at[s], swr.at[s]
        return (
            [
                rdma(D.at[s, 1, inner], D.at[s, 17, inner], ss.at[2], rs.at[2], {"gx": i_lo}),
                rdma(D.at[s, 16, inner], D.at[s, 0, inner], ss.at[3], rs.at[3], {"gx": i_hi}),
            ],
            rdma(D.at[s, inner, 1], D.at[s, inner, 17], ss.at[0], rs.at[0], gy_lo),
            rdma(D.at[s, inner, 16], D.at[s, inner, 0], ss.at[1], rs.at[1], gy_hi),
        )

    def e_of(s):
        ss, rs = sws.at[s], swr.at[s]
        return (
            [
                rdma(E.at[s, pl.ds(0, 16)], EX.at[s, 1], ss.at[4], rs.at[4], {"gx": i_lo}),
                rdma(E.at[s, pl.ds(240, 16)], EX.at[s, 0], ss.at[5], rs.at[5], {"gx": i_hi}),
            ],
            rdma(EYS.at[s, 0], EY.at[s, 1], ss.at[6], rs.at[6], gy_lo),
            rdma(EYS.at[s, 1], EY.at[s, 0], ss.at[7], rs.at[7], gy_hi),
        )

    def put_d(s):
        def put(x, y, new, along_x=False):
            n = new.shape[0]
            if along_x:
                D[s, pl.ds(x + 1, n), y + 1] = new
            else:
                D[s, x + 1, pl.ds(y + 1, n)] = new

        return put

    def put_out(x, y, new, along_x=False):
        for u in range(new.shape[0]):
            xu, yu = (x + u, y) if along_x else (x, y + u)
            row = xu * 128 + yu // 8 * 64 + yu % 8
            out_ref[pl.ds(row, 8, stride=8), :] = new[u]

    def inside(s, put):
        def body(x, _):
            for y in (1, 8):
                put(x, y, columns(s, x, y, 7))
            return 0

        lax.fori_loop(1, 15, body, 0)

    def y_planes(s, put):
        def body(g, _):
            for y in (0, 15):
                put(g * 4, y, columns(s, g * 4, y, 4, True), True)
            return 0

        lax.fori_loop(0, 4, body, 0)

    def x_planes(s, put):
        for x in (0, 15):
            for y in (1, 8):
                put(x, y, columns(s, x, y, 7))

    faces(0)
    inside(0, put_d(1))
    vx_lo.wait_recv()
    vx_hi.wait_recv()
    for n, big, at in ((0, 3, 0), (1, 0, 17)):
        up = upright(VX[n])
        for row in range(1, 5):
            t = cell(up, big, row)
            for y in range(row * 4 - 3, row * 4 + 1):
                D[0, at, y] = t

    def e_send(s):
        x_e, down_e, up_e = e_of(s)
        for c in x_e:
            c.start()

        @pl.when(j > 0)
        def _():
            down_e.start()

        @pl.when(j < NGY - 1)
        def _():
            up_e.start()

    def e_wait(s):
        x_e, down_e, up_e = e_of(s)
        for c in x_e:
            c.wait()

        @pl.when(j > 0)
        def _():
            down_e.wait_send()
            up_e.wait_recv()

        @pl.when(j < NGY - 1)
        def _():
            up_e.wait_send()
            down_e.wait_recv()

    def planes(s):
        x_d, down_d, up_d = planes_of(s + 1)
        y_planes(s, put_d(s + 1))

        @pl.when(j > 0)
        def _():
            down_d.start()

        @pl.when(j < NGY - 1)
        def _():
            up_d.start()

        x_planes(s, put_d(s + 1))
        for c in x_d:
            c.start()

    def planes_wait(s):
        x_d, down_d, up_d = planes_of(s + 1)

        @pl.when(j > 0)
        def _():
            down_d.wait_send()
            up_d.wait_recv()

        @pl.when(j < NGY - 1)
        def _():
            up_d.wait_send()
            down_d.wait_recv()

        for c in x_d:
            c.wait()

    def ends_wait():
        for c in ends_s:
            c.wait_recv()
        for part in range(4):
            for n in range(6):
                at = part * 32 + n * 4
                AE[n, pl.ds(part * 64, 64)] = jnp.where(
                    lane64 < 4,
                    pltpu.roll(RA[1], (128 - at) % 128, 1) if at else RA[1],
                    jnp.where(lane64 >= 124, pltpu.roll(RA[0], 124 - at, 1), 0.0),
                )
        for g in range(32):
            up = pltpu.roll(RB[1], (128 - g * 4) % 128, 1) if g else RB[1]
            down = pltpu.roll(RB[0], 124 - g * 4, 1) if g < 31 else RB[0]
            AE[6, pl.ds(g * 8, 8)] = jnp.where(
                lane < 4, up, jnp.where(lane >= 124, down, 0.0)
            )

    planes(0)
    ends_wait()
    for c in (ex_lo, ex_hi):
        c.wait_recv()
    beyond(0)
    e_send(1)
    faces(1)
    inside(1, put_d(2))
    planes_wait(0)
    planes(1)
    e_wait(1)
    beyond(1)
    e_send(2)
    faces(2)
    inside(2, put_d(3))
    planes_wait(1)
    planes(2)
    e_wait(2)
    beyond(2)
    faces(3)
    inside(3, put_out)
    planes_wait(2)
    y_planes(3, put_out)
    x_planes(3, put_out)

    for c in sends + xs + ends_s + [zc_lo, zc_hi, vx_lo, vx_hi, ex_lo, ex_hi]:
        c.wait_send()

    @pl.when(j > 0)
    def _():
        for c in y_down:
            c.wait_send()

    @pl.when(j < NGY - 1)
    def _():
        for c in y_up:
            c.wait_send()


def tiles(a):
    return a.reshape(16, 2, 8, 8, 128).transpose(0, 1, 3, 2, 4)


def per_device(
    pressure,
    pressure_old,
    accumulation,
    permeability,
    comp_block,
    comp_owner,
    comp_well,
    comp_wi,
    well_rate,
    well_storage,
    well_bhp_old,
):
    perm = permeability.reshape(3, 16, 2, 8, 8, 128).transpose(0, 1, 2, 4, 3, 5)
    hbm = pl.BlockSpec(memory_space=pltpu.HBM)
    vmem = pl.BlockSpec(memory_space=pltpu.VMEM)
    smem = pl.BlockSpec(memory_space=pltpu.SMEM)
    grid = (16, 16, 8, 128)
    dma = pltpu.SemaphoreType.DMA
    cb = comp_block.reshape(1, 128)

    def vm(*shape):
        return pltpu.VMEM(shape, F32)

    out, bhp = pl.pallas_call(
        kernel,
        out_shape=(
            jax.ShapeDtypeStruct((2048, 128), F32),
            jax.ShapeDtypeStruct((1, 8), F32),
        ),
        in_specs=[smem] + [hbm] * 4 + [vmem] * 7,
        out_specs=(vmem, vmem),
        scratch_shapes=[
            vm(16, 2, 8, 8, 128),
            vm(18, 18, 8, 128),
            vm(*grid),
            vm(*grid),
            vm(18, 16, 8, 128),
            vm(16, 18, 8, 128),
            vm(*grid),
            vm(17, 16, 8, 128),
            vm(16, 17, 8, 128),
            vm(*grid),
            vm(*grid),
            vm(*grid),
            vm(*grid),
            vm(*grid),
            vm(*grid),
            vm(*grid),
            vm(*grid),
            vm(*grid),
            vm(*grid),
            vm(4, 18, 18, 8, 128),
            pltpu.VMEM((16, 128, 128), jnp.bfloat16),
            vm(128, 128),
            vm(8, 128),
            vm(8, 8, 128),
            vm(8, 8, 128),
            vm(256, 128),
            vm(256, 128),
            vm(2, 8, 128),
            vm(2, 8, 128),
            vm(2, 64, 128),
            vm(2, 64, 128),
            vm(2, 8, 128),
            vm(2, 8, 128),
            vm(7, 256, 128),
            vm(4, 256, 128),
            vm(4, 2, 16, 128),
            vm(4, 2, 16, 128),
            vm(4, 2, 16, 128),
            vm(256, 128),
            vm(256, 128),
            vm(256, 128),
            vm(16, 8, 128),
            vm(8, 16, 8, 128),
            vm(8, 128),
            vm(8, 128),
            vm(3, 4, 8, 128),
            vm(3, 4, 8, 128),
            vm(8, 128),
            vm(2, 8, 128),
            dma((7,)),
            dma((8,)),
            dma((8,)),
            dma((8,)),
            dma((8,)),
            dma((10,)),
            dma((10,)),
            dma((11,)),
            dma((3, 4)),
            dma((11,)),
            dma((3, 4)),
            dma((2,)),
            dma((2,)),
            dma((4,)),
            dma((4,)),
            dma((4, 8)),
            dma((4, 8)),
        ],
        compiler_params=pltpu.CompilerParams(
            collective_id=0, has_side_effects=True, vmem_limit_bytes=60 * 1024 * 1024
        ),
    )(
        cb,
        tiles(pressure),
        tiles(pressure_old),
        tiles(accumulation),
        perm,
        cb,
        comp_owner.reshape(1, 128),
        comp_well.reshape(1, 128),
        comp_wi.reshape(128, 128),
        well_rate.reshape(1, 8),
        well_storage.reshape(1, 8),
        well_bhp_old.reshape(1, 8),
    )
    delta = out.reshape(16, 2, 8, 8, 128).transpose(0, 1, 3, 2, 4).reshape(16, 16, 1024)
    return pressure + delta, bhp.reshape(1, 1, 1, 8)


def solution(mesh):
    return jax.shard_map(
        per_device,
        mesh=mesh,
        in_specs=(
            P("gx", "gy", "grp"),
            P("gx", "gy", "grp"),
            P("gx", "gy", "grp"),
            P(None, "gx", "gy", "grp"),
            P("gx", "gy", "grp", None),
            P("gx", "gy", "grp", None, None),
            P("gx", "gy", "grp", None),
            P("gx", "gy", "grp", None, None),
            P("gx", "gy", "grp", None),
            P("gx", "gy", "grp", None),
            P("gx", "gy", "grp", None),
        ),
        out_specs=(P("gx", "gy", "grp"), P("gx", "gy", "grp", None)),
        check_vma=False,
    )
```

```python
import jax
import jax.numpy as jnp
from jax import lax
from jax.experimental import pallas as pl
from jax.experimental.pallas import tpu as pltpu
from jax.sharding import PartitionSpec as P

MESH = pl.DeviceIdType.MESH
F32 = jnp.float32
RELAX = 0.7
KEEP = 1.0 - RELAX
NGX, NGY, NGRP = 8, 4, 8
FAR_FIRST = (3, 5, 1, 7, 4, 2, 6)
HIGH = lax.Precision.HIGHEST


def iota(shape, dim):
    return lax.broadcasted_iota(jnp.int32, shape, dim)


def nt(a, b):
    return lax.dot_general(
        a, b, (((1,), (1,)), ((), ())), precision=HIGH, preferred_element_type=F32
    )


def exact(a, onehot, dim):
    hi = a.astype(jnp.bfloat16).astype(F32)
    mid = (a - hi).astype(jnp.bfloat16).astype(F32)
    parts = jnp.concatenate([hi, mid, a - hi - mid], axis=0).astype(jnp.bfloat16)
    out = lax.dot_general(
        parts, onehot, (((1,), (dim,)), ((), ())), preferred_element_type=F32
    )
    return (out[0:8] + out[8:16]) + out[16:24]


def rcp(x):
    r = pl.reciprocal(x, approx=True)
    return r * (2.0 - x * r)


def harm(a, b):
    return 2.0 * a * b * rcp(a + b)


def z_below(v):
    r = pltpu.roll(v, 1, 2)
    return jnp.where(iota(v.shape, 2) == 0, pltpu.roll(r, 1, 1), r)


def z_above(v):
    r = pltpu.roll(v, 127, 2)
    return jnp.where(iota(v.shape, 2) == 127, pltpu.roll(r, 7, 1), r)


def kernel(
    p_hbm,
    po_hbm,
    ac_hbm,
    k_hbm,
    cb_hbm,
    ow_hbm,
    cw_hbm,
    wi_hbm,
    rate_hbm,
    stor_hbm,
    old_hbm,
    out_hbm,
    bhp_hbm,
    cb_s,
    cb_v,
    ow_v,
    cw_v,
    wi_v,
    rate_v,
    stor_v,
    old_v,
    bhp_out,
    PG,
    PP,
    PO,
    AC,
    KX,
    KY,
    KZ,
    TX,
    TY,
    TZL,
    TZH,
    AXL,
    AXH,
    AYL,
    AYH,
    AZL,
    AZH,
    CC,
    BB,
    D,
    OUT,
    OH,
    PR,
    OWN,
    W1,
    W2,
    HZP,
    HZK,
    ZS0,
    ZI,
    SA,
    RA,
    SB,
    RB,
    AE,
    E,
    EX,
    EY,
    EYS,
    FA,
    AR,
    FR,
    UU,
    CQ,
    CSO,
    CBO,
    CS,
    CB,
    VO,
    VX,
    lsem,
    a1s,
    a1r,
    a2s,
    a2r,
    ihs,
    ihr,
    css,
    csr,
    cbs,
    cbr,
    vxs,
    vxr,
    ras,
    rar,
    sws,
    swr,
):
    i = lax.axis_index("gx")
    j = lax.axis_index("gy")
    l = lax.axis_index("grp")
    i_lo, i_hi = lax.rem(i + NGX - 1, NGX), lax.rem(i + 1, NGX)
    l_lo, l_hi = lax.rem(l + NGRP - 1, NGRP), lax.rem(l + 1, NGRP)

    def rdma(src, dst, ss, rs, dev):
        return pltpu.make_async_remote_copy(
            src_ref=src, dst_ref=dst, send_sem=ss, recv_sem=rs, device_id=dev, device_id_type=MESH
        )

    bar = pltpu.get_barrier_semaphore()

    def greet(dev):
        pl.semaphore_signal(bar, inc=1, device_id=dev, device_id_type=MESH)

    for dz in (0, 2, 1):
        for dj in range(1, NGY):
            greet({"gy": lax.rem(j + dj, NGY), "grp": lax.rem(l + dz + NGRP - 1, NGRP)})
    for d in FAR_FIRST:
        greet({"grp": lax.rem(l + d, NGRP)})
    for d in range(1, NGX):
        greet({"gx": lax.rem(i + d, NGX)})

    load_g = pltpu.make_async_copy(p_hbm, PG, lsem.at[0])
    load_g.start()
    small = [
        pltpu.make_async_copy(src, dst, lsem.at[7 + n])
        for n, (src, dst) in enumerate(
            (
                (cb_hbm, cb_s),
                (wi_hbm, wi_v),
                (cb_hbm, cb_v),
                (ow_hbm, ow_v),
                (cw_hbm, cw_v),
                (rate_hbm, rate_v),
                (stor_hbm, stor_v),
                (old_hbm, old_v),
            )
        )
    ]
    for c in small:
        c.start()

    def load_kz(ys, _):
        for yt in range(2):
            pltpu.make_async_copy(
                k_hbm.at[2, :, yt, :, ys, :], KZ.at[:, yt * 8 + ys], lsem.at[4]
            ).start()
        return 0

    lax.fori_loop(0, 8, load_kz, 0)

    def load(ys, _):
        for yt in range(2):
            y = yt * 8 + ys
            pltpu.make_async_copy(
                p_hbm.at[:, yt, :, ys, :], PP.at[pl.ds(1, 16), 1 + y], lsem.at[1]
            ).start()
            pltpu.make_async_copy(
                k_hbm.at[0, :, yt, :, ys, :], KX.at[pl.ds(1, 16), y], lsem.at[2]
            ).start()
            pltpu.make_async_copy(
                k_hbm.at[1, :, yt, :, ys, :], KY.at[:, 1 + y], lsem.at[3]
            ).start()
            pltpu.make_async_copy(po_hbm.at[:, yt, :, ys, :], PO.at[:, y], lsem.at[5]).start()
            pltpu.make_async_copy(ac_hbm.at[:, yt, :, ys, :], AC.at[:, y], lsem.at[6]).start()
        return 0

    lax.fori_loop(0, 8, load, 0)

    for c in small:
        c.wait()
    load_g.wait()

    def gather(g, _):
        for u in range(8):
            b = cb_s[0, g * 8 + u]
            x, y, k = b // 128, lax.rem(b // 8, 16), lax.rem(b, 8)
            PR[pl.ds(g * 8 + u, 1), :] = PG[x, y // 8, k, pl.ds(lax.rem(y, 8), 1), :]
        return 0

    lax.fori_loop(0, 16, gather, 0)
    wi = wi_v[...]
    sub = iota((8, 128), 0)
    lane = iota((8, 128), 1)
    sub128 = iota((128, 128), 0)
    lane128 = iota((128, 128), 1)
    ones8 = jnp.ones((8, 128), F32)
    weighted = nt(ones8, wi * PR[...])
    total = nt(ones8, wi)
    cb = cb_v[...]
    q = ow_v[...] * 8 + cw_v[...]
    q_hi, q_lo = q // 128, lax.rem(q, 128)
    pick = (sub128 == q_lo).astype(F32).astype(jnp.bfloat16)
    share = exact(
        jnp.where(sub == q_hi, weighted, 0.0) + jnp.where(sub == q_hi + 4, total, 0.0), pick, 1
    )
    own = i * NGRP + l
    own_row, shift = own // 16, lax.rem(own, 16) * 8
    OWN[...] = jnp.zeros((8, 128), F32)
    OWN[0:1, 0:8] = stor_v[...] * old_v[...] - rate_v[...]
    OWN[1:2, 0:8] = stor_v[...]
    placed = pltpu.roll(OWN[...], shift, 1)
    share = (
        share
        + jnp.where(sub == own_row, placed[0:1], 0.0)
        + jnp.where(sub == own_row + 4, placed[1:2], 0.0)
    )
    W1[i] = share

    lane64 = iota((64, 128), 1)

    def end_rows(ref, part, k, base, width):
        return jnp.concatenate(
            [
                ref[pl.ds(base + (part * 4 + u) * width * 8 + k, 16, stride=8), :]
                for u in range(4)
            ],
            axis=0,
        )

    KZ2 = KZ.reshape(2048, 128)

    def flat(ref):
        ref2 = ref.reshape(2048, 128)
        return (
            lambda part: end_rows(ref2, part, 0, 0, 16),
            lambda part: end_rows(ref2, part, 7, 0, 16),
        )

    def raw_rows(k):
        def rows(part):
            return jnp.concatenate(
                [PG[part * 4 + u, yt, k] for u in range(4) for yt in range(2)], axis=0
            )

        return rows

    def pack_tile(refs, lo_ref, hi_ref):
        keep = 4 if len(refs) == 1 else 1
        lo = hi = jnp.zeros((8, 128), F32)
        for part in range(4):
            for n, ends in enumerate(refs):
                a, b = ends[0](part), ends[1](part)
                for u in range(8):
                    to = part * 32 + u * 4 + n
                    at = slice(u * 8, u * 8 + 8)
                    a8 = jnp.where(lane < keep, a[at], 0.0)
                    b8 = jnp.where(lane >= 128 - keep, b[at], 0.0)
                    lo = lo + (pltpu.roll(a8, to, 1) if to else a8)
                    hi = hi + pltpu.roll(b8, (to + keep) % 128, 1)
        lo_ref[...] = lo
        hi_ref[...] = hi

    def pack_ends(refs, lo_ref, hi_ref):
        lo = hi = jnp.zeros((64, 128), F32)
        for part in range(4):
            for n, ends in enumerate(refs):
                to = part * 32 + n * 4
                a = jnp.where(lane64 < 4, ends[0](part), 0.0)
                b = jnp.where(lane64 >= 124, ends[1](part), 0.0)
                lo = lo + (pltpu.roll(a, to, 1) if to else a)
                hi = hi + pltpu.roll(b, to + 4, 1)
        lo_ref[...] = lo
        hi_ref[...] = hi

    pltpu.make_async_copy(KZ, KZ, lsem.at[4]).wait()
    pack_tile([(raw_rows(0), raw_rows(7)), flat(KZ)], ZS0.at[0], ZS0.at[1])


    pl.semaphore_wait(bar, 23)

    sends = []
    for d in range(1, NGX):
        c = rdma(W1.at[i], W1.at[i], a1s.at[d], a1r.at[i], {"gx": lax.rem(i + d, NGX)})
        c.start()
        sends.append(c)

    zc_lo = rdma(ZS0.at[0], ZI.at[1], ihs.at[0], ihr.at[0], {"grp": l_lo})
    zc_hi = rdma(ZS0.at[1], ZI.at[0], ihs.at[1], ihr.at[1], {"grp": l_hi})
    zc_lo.start()
    zc_hi.start()

    zplane = jnp.zeros((16, 8, 128), F32)

    @pl.when(j == 0)
    def _():
        PP[pl.ds(1, 16), 0] = zplane
        for s in range(1, 4):
            D[s, pl.ds(1, 16), 0] = zplane
            EY[s, 0] = jnp.zeros((16, 128), F32)

    @pl.when(j == NGY - 1)
    def _():
        PP[pl.ds(1, 16), 17] = zplane
        for s in range(1, 4):
            D[s, pl.ds(1, 16), 17] = zplane
            EY[s, 1] = jnp.zeros((16, 128), F32)

    inner = pl.ds(1, 16)
    pltpu.make_async_copy(KZ, KX.at[pl.ds(1, 16)], lsem.at[2]).wait()
    pltpu.make_async_copy(KZ, KY.at[:, pl.ds(1, 16)], lsem.at[3]).wait()
    pltpu.make_async_copy(KZ, PP.at[pl.ds(1, 16), pl.ds(1, 16)], lsem.at[1]).wait()
    xs = [
        rdma(KX.at[1], KX.at[17], ihs.at[2], ihr.at[2], {"gx": i_lo}),
        rdma(KX.at[16], KX.at[0], ihs.at[3], ihr.at[3], {"gx": i_hi}),
        rdma(PP.at[1, inner], PP.at[17, inner], ihs.at[4], ihr.at[4], {"gx": i_lo}),
        rdma(PP.at[16, inner], PP.at[0, inner], ihs.at[5], ihr.at[5], {"gx": i_hi}),
    ]
    for c in xs:
        c.start()
    y_down = [
        rdma(KY.at[:, 1], KY.at[:, 17], ihs.at[6], ihr.at[6], {"gy": lax.max(j - 1, 0)}),
        rdma(PP.at[inner, 1], PP.at[inner, 17], ihs.at[7], ihr.at[7], {"gy": lax.max(j - 1, 0)}),
    ]
    y_up = [
        rdma(KY.at[:, 16], KY.at[:, 0], ihs.at[8], ihr.at[8], {"gy": lax.min(j + 1, 3)}),
        rdma(PP.at[inner, 16], PP.at[inner, 0], ihs.at[9], ihr.at[9], {"gy": lax.min(j + 1, 3)}),
    ]

    @pl.when(j > 0)
    def _():
        for c in y_down:
            c.start()

    @pl.when(j < NGY - 1)
    def _():
        for c in y_up:
            c.start()

    def onehot(x, _):
        OH[x] = (sub128 + x * 128 == cb).astype(F32).astype(jnp.bfloat16)
        return 0

    lax.fori_loop(0, 16, onehot, 0)

    def halves(v):
        hi = v.astype(jnp.bfloat16)
        lo = (v - hi.astype(F32)).astype(jnp.bfloat16)
        return jnp.concatenate([hi, lo], axis=1)

    def blocks(x, n, parts):
        rows = OH[pl.ds(x, n)].reshape(n * 128, 128)
        r = jnp.dot(rows, parts, preferred_element_type=F32)
        return (r[:, :128] + r[:, 128:]).reshape(n, 16, 8, 128)

    wi_parts = halves(wi)

    CQ[...] = jnp.zeros((8, 16, 8, 128), F32)
    pltpu.make_async_copy(KZ, PO, lsem.at[5]).wait()
    pltpu.make_async_copy(KZ, AC, lsem.at[6]).wait()

    def prepare(x, _):
        w16 = blocks(x, 1, wi_parts)[0]
        for yt in range(2):
            y0 = yt * 8
            c8 = pl.ds(y0, 8)
            p = PP[x + 1, pl.ds(y0 + 1, 8)]
            acc = AC[x, c8]
            w = w16[y0 : y0 + 8]
            PO[x, c8] = acc * (p - PO[x, c8]) + w * p
            accw = acc + w
            AC[x, c8] = accw
            for yl in range(2):
                CQ[1, x // 4 * 4 + yt * 2 + yl] += accw[yl * 4 : yl * 4 + 4].sum(0)
            kz = KZ[x, c8]
            tzl = harm(z_below(kz), kz)
            TZL[x, c8] = tzl
            TZH[x, c8] = z_above(tzl)
            n = 8 - yt
            lower, upper = KY[x, pl.ds(y0 + 1, n)], KY[x, pl.ds(y0 + 2, n)]
            TY[x, pl.ds(y0 + 1, n)] = harm(lower, upper)
        return 0

    lax.fori_loop(0, 16, prepare, 0)

    def faces_x(x, _):
        for yt in range(2):
            c8 = pl.ds(yt * 8, 8)
            TX[x, c8] = harm(KX[x, c8], KX[x + 1, c8])
        return 0

    lax.fori_loop(1, 16, faces_x, 0)

    for d in range(1, NGX):
        s = lax.rem(i + d, NGX)
        rdma(W1.at[i], W1.at[s], a1s.at[d], a1r.at[s], {"gx": s}).wait_recv()
    acc8 = W1[0]
    for s in range(1, NGX):
        acc8 = acc8 + W1[s]
    W2[l] = acc8
    for d in FAR_FIRST:
        c = rdma(W2.at[l], W2.at[l], a2s.at[d], a2r.at[l], {"grp": lax.rem(l + d, NGRP)})
        c.start()
        sends.append(c)

    for c in xs:
        c.wait_recv()

    @pl.when(j > 0)
    def _():
        for c in y_up:
            c.wait_recv()

    @pl.when(j < NGY - 1)
    def _():
        for c in y_down:
            c.wait_recv()

    @pl.when(i == 0)
    def _():
        KX[0] = zplane

    @pl.when(i == NGX - 1)
    def _():
        KX[17] = zplane

    @pl.when(j == 0)
    def _():
        KY[:, 0] = zplane

    @pl.when(j == NGY - 1)
    def _():
        KY[:, 17] = zplane

    for x in (0, 16):
        TX[x] = harm(KX[x], KX[x + 1])
    for y in (0, 16):
        TY[:, y] = harm(KY[:, y], KY[:, y + 1])
    zc_lo.wait_recv()
    zc_hi.wait_recv()
    has_lo = (l > 0).astype(F32)
    has_hi = (l < NGRP - 1).astype(F32)
    for g in range(32):
        for n, ref in enumerate((HZP, HZK)):
            lo = pltpu.roll(ZI[0], (128 - g * 4 - n) % 128, 1) if g + n else ZI[0]
            hi = pltpu.roll(ZI[1], 127 - g * 4 - n, 1)
            if n:
                lo, hi = lo * has_lo, hi * has_hi
            ref[pl.ds(g * 8, 8)] = jnp.where(lane == 0, lo, hi)

    for part in range(4):
        rows = pl.ds(part * 64, 64)
        k_end = jnp.where(
            lane64 < 64, end_rows(KZ2, part, 0, 0, 16), end_rows(KZ2, part, 7, 0, 16)
        )
        HZK[rows] = harm(k_end, HZK[rows])
    sh3 = (8, 8, 128)
    first = (iota(sh3, 2) == 0) & (iota(sh3, 1) == 0)
    last = (iota(sh3, 2) == 127) & (iota(sh3, 1) == 7)

    def column(ref, n):
        return jnp.concatenate(
            [jnp.broadcast_to(ref[pl.ds(n + u, 1), :], (8, 128))[None] for u in range(8)], axis=0
        )

    def operator(x, _):
        big = x // 4
        f_lo = (lax.rem(x, 4) == 0).astype(F32)
        f_hi = (lax.rem(x, 4) == 3).astype(F32)
        for yt in range(2):
            y0 = yt * 8
            c8 = pl.ds(y0, 8)
            txl, txh = TX[x, c8], TX[x + 1, c8]
            tyl, tyh = TY[x, c8], TY[x, pl.ds(y0 + 1, 8)]
            tk = column(HZK, x * 16 + y0)
            tzl = jnp.where(first, tk, TZL[x, c8])
            tzh = jnp.where(last, tk, TZH[x, c8])
            tsum = ((txl + txh) + (tyl + tyh)) + (tzl + tzh)
            p = PP[x + 1, pl.ds(y0 + 1, 8)]
            hp = column(HZP, x * 16 + y0)
            nb = (
                (txl * PP[x, pl.ds(y0 + 1, 8)] + txh * PP[x + 2, pl.ds(y0 + 1, 8)])
                + (tyl * PP[x + 1, c8] + tyh * PP[x + 1, pl.ds(y0 + 2, 8)])
                + (
                    tzl * jnp.where(first, hp, z_below(p))
                    + tzh * jnp.where(last, hp, z_above(p))
                )
            )
            r0 = PO[x, c8] + tsum * p - nb
            c = RELAX * rcp(AC[x, c8] + tsum)
            AXL[x, c8] = c * txl
            AXH[x, c8] = c * txh
            AYL[x, c8] = c * tyl
            AYH[x, c8] = c * tyh
            AZL[x, c8] = c * tzl
            AZH[x, c8] = c * tzh
            CC[x, c8] = c
            BB[x, c8] = -c * r0
            for yl in range(2):
                n = big * 4 + yt * 2 + yl
                part = slice(yl * 4, yl * 4 + 4)
                CQ[0, n] += r0[part].sum(0)
                CQ[2, n] += txl[part].sum(0) * f_lo
                CQ[3, n] += txh[part].sum(0) * f_hi
                CQ[4, n] += tyl[yl * 4]
                CQ[5, n] += tyh[yl * 4 + 3]
                CQ[6, n] += tzl[part].sum(0)
                CQ[7, n] += tzh[part].sum(0)
        return 0

    lax.fori_loop(0, 16, operator, 0)

    sh4 = (16, 8, 128)
    lane4 = iota(sh4, 2)
    place4 = lane4 == iota(sh4, 0) * 8 + iota(sh4, 1)

    def coarse_of(n):
        v = CQ[n]
        if n == 6:
            v = jnp.where(lane4 == 0, v, 0.0)
        if n == 7:
            v = jnp.where(lane4 == 127, v, 0.0)
        v = jnp.where(place4, jnp.sum(v, axis=2, keepdims=True), 0.0)
        return jnp.sum(v.sum(0), axis=0, keepdims=True)

    r_c, a_c, xl, xh, yl, yh, zl, zh = [coarse_of(n) for n in range(8)]
    scale = RELAX / (a_c + ((xl + xh) + (yl + yh)) + (zl + zh))
    lane1 = iota((1, 128), 1)
    CSO[...] = jnp.concatenate(
        [
            jnp.where(lane1 >= 32, scale * xl, 0.0),
            jnp.where(lane1 < 96, scale * xh, 0.0),
            scale * yl,
            scale * yh,
            scale * zl,
            scale * zh,
            scale,
            scale,
        ],
        axis=0,
    )
    peers = [(dj, dz) for dz in (0, 2, 1) for dj in range(NGY) if (dj, dz) != (0, 1)]

    def to_peers(own_ref, all_ref, ss, rs, count):
        rows = pl.ds(0, count)
        for n, (dj, dz) in enumerate(peers):
            dev = {"gy": lax.rem(j + dj, NGY), "grp": lax.rem(l + dz + NGRP - 1, NGRP)}
            to = all_ref.at[2 - dz, j, rows]
            c = rdma(own_ref.at[rows], to, ss.at[n], rs.at[2 - dz, j], dev)
            c.start()
            sends.append(c)

    def from_peers(own_ref, all_ref, ss, rs, count):
        rows = pl.ds(0, count)
        for n, (dj, dz) in enumerate(peers):
            s = lax.rem(j + dj, NGY)
            dev = {"gy": s, "grp": lax.rem(l + dz + NGRP - 1, NGRP)}
            to = all_ref.at[dz, s, rows]
            rdma(own_ref.at[rows], to, ss.at[n], rs.at[dz, s], dev).wait_recv()

    to_peers(CSO, CS, css, csr, 8)
    CS[1, j] = CSO[...]

    cx, cy, ck = cb // 128, lax.rem(cb // 8, 16), lax.rem(cb, 8)
    spot = (sub128 == (cx // 4) * 32 + (cy // 4) * 8 + ck).astype(F32).astype(jnp.bfloat16)

    for d in range(1, NGRP):
        s = lax.rem(l + d, NGRP)
        rdma(W2.at[l], W2.at[s], a2s.at[d], a2r.at[s], {"grp": s}).wait_recv()
    acc8 = W2[0]
    for s in range(1, NGRP):
        acc8 = acc8 + W2[s]
    bhp = jnp.where(sub < 4, acc8 / jnp.where(sub < 4, pltpu.roll(acc8, 4, 0), 1.0), 0.0)
    mine = pltpu.roll(jnp.where(sub == own_row, bhp, 0.0), lax.rem(128 - shift, 128), 1)
    bhp_out[...] = jnp.sum(mine, axis=0, keepdims=True)[:, 0:8]
    bhp_copy = pltpu.make_async_copy(bhp_out, bhp_hbm, lsem.at[15])
    bhp_copy.start()
    bhp_c = jnp.sum(
        jnp.where(sub == q_hi, exact(bhp, pick, 0), 0.0), axis=0, keepdims=True
    )

    CBO[...] = scale * (exact(total * bhp_c, spot, 1) - r_c)
    to_peers(CBO, CB, cbs, cbr, 1)
    CB[1, j] = CBO[...]

    ends_s = [
        rdma(SA.at[0], RA.at[1], ras.at[0], rar.at[0], {"grp": l_lo}),
        rdma(SA.at[1], RA.at[0], ras.at[1], rar.at[1], {"grp": l_hi}),
        rdma(SB.at[0], RB.at[1], ras.at[2], rar.at[2], {"grp": l_lo}),
        rdma(SB.at[1], RB.at[0], ras.at[3], rar.at[3], {"grp": l_hi}),
    ]
    pack_ends([flat(r) for r in (AXL, AXH, AYL, AYH, AZL, AZH)], SA.at[0], SA.at[1])
    ends_s[0].start()
    ends_s[1].start()
    AZL2, AZH2 = AZL.reshape(2048, 128), AZH.reshape(2048, 128)
    for part in range(4):
        AR[pl.ds(part * 64, 64)] = jnp.where(
            lane64 < 64, end_rows(AZL2, part, 0, 0, 16), end_rows(AZH2, part, 7, 0, 16)
        )

    bhp_col = jnp.sum(jnp.where(sub128 == lane128, bhp_c, 0.0), axis=1, keepdims=True)
    wb_parts = halves(wi * bhp_col)

    def finish(g, _):
        at = pl.ds(g * 4, 4)
        BB[at] = BB[at] + CC[at] * blocks(g * 4, 4, wb_parts)
        return 0

    lax.fori_loop(0, 4, finish, 0)
    pack_tile([flat(BB)], SB.at[0], SB.at[1])
    ends_s[2].start()
    ends_s[3].start()

    def joined(tile):
        block = lax.rem(lane, 32) // 8
        for g in range(NGY):
            for y in range(4):
                u = None
                for dz in range(3):
                    t = tile(dz, g)
                    to = (8 * (dz - y)) % 128
                    t = pltpu.roll(t, to, 1) if to else t
                    u = jnp.where(block == dz, t, 0.0 if u is None else u)
                UU[g * 4 + y] = u

    UU2 = UU.reshape(128, 128)
    from_peers(CSO, CS, css, csr, 8)
    joined(lambda dz, g: CS[dz, g])
    coef = [UU2[pl.ds(n, 16, stride=8), :] for n in range(6)]
    from_peers(CBO, CB, cbs, cbr, 1)
    joined(lambda dz, g: jnp.broadcast_to(CB[dz, g, 0:1], (8, 128)))
    rhs = UU2[pl.ds(0, 16, stride=8), :]

    def coarse_step(_, v):
        return (
            (KEEP * v + rhs)
            + (coef[0] * pltpu.roll(v, 32, 1) + coef[1] * pltpu.roll(v, 96, 1))
            + (coef[2] * pltpu.roll(v, 1, 0) + coef[3] * pltpu.roll(v, 15, 0))
            + (coef[4] * pltpu.roll(v, 1, 1) + coef[5] * pltpu.roll(v, 127, 1))
        )

    v = lax.fori_loop(0, 7, coarse_step, rhs)
    mine = jnp.zeros((8, 128), F32)
    for g in range(NGY):
        mine = jnp.where(j == g, pltpu.roll(v, (17 - 4 * g) % 16, 0)[0:8], mine)
    VO[...] = mine
    vx_lo = rdma(VO, VX.at[1], vxs.at[0], vxr.at[0], {"gx": i_lo})
    vx_hi = rdma(VO, VX.at[0], vxs.at[1], vxr.at[1], {"gx": i_hi})
    vx_lo.start()
    vx_hi.start()

    def cell(tile, big, row):
        t = jnp.where(lane == big * 32 + 8 + sub, tile[row : row + 1], 0.0)
        return jnp.broadcast_to(jnp.sum(t, axis=1, keepdims=True), (8, 128))

    for big in range(4):
        for row in range(6):
            t = cell(mine, big, row)
            ys = (0,) if row == 0 else (17,) if row == 5 else range(row * 4 - 3, row * 4 + 1)
            for x in range(4):
                for y in ys:
                    D[0, 1 + big * 4 + x, y] = t
    sub16 = iota((16, 128), 0)
    y_lo = y_hi = jnp.zeros((16, 128), F32)
    for big in range(4):
        lo, hi = [
            jnp.sum(jnp.where(lane == big * 32 + at, mine, 0.0), axis=1, keepdims=True)
            for at in (7, 16)
        ]
        e = jnp.where(lane < 64, hi, lo)
        rows = jnp.zeros((16, 128), F32)
        for y in range(4):
            rows = jnp.where(sub16 // 4 == y, e[y + 1 : y + 2], rows)
        for u in range(4):
            E[0, pl.ds((big * 4 + u) * 16, 16)] = rows
        y_lo = jnp.where(sub16 // 4 == big, e[0:1], y_lo)
        y_hi = jnp.where(sub16 // 4 == big, e[5:6], y_hi)
    EY[0, 0] = y_lo
    EY[0, 1] = y_hi
    ex_lo = rdma(E.at[0, pl.ds(0, 16)], EX.at[0, 1], sws.at[0, 4], swr.at[0, 4], {"gx": i_lo})
    ex_hi = rdma(E.at[0, pl.ds(240, 16)], EX.at[0, 0], sws.at[0, 5], swr.at[0, 5], {"gx": i_hi})
    ex_lo.start()
    ex_hi.start()
    D2 = D.reshape(4 * 18 * 18 * 8, 128)
    E2 = E.reshape(4 * 256, 128)

    def faces(s):
        for part in range(4):
            base = (s * 18 * 18 + 19) * 8
            rows = pl.ds(part * 64, 64)
            m = jnp.where(
                lane64 < 64, end_rows(D2, part, 0, base, 18), end_rows(D2, part, 7, base, 18)
            )
            FA[rows] = m
            d = E[s, rows] - m
            FR[rows] = AR[rows] * jnp.where(
                lane64 < 64, pltpu.roll(d, 1, 1), pltpu.roll(d, 127, 1)
            )

    def columns(s, x, y, n, along_x=False):
        at = (pl.ds(x, n), y) if along_x else (x, pl.ds(y, n))

        def near(dx, dy):
            if along_x:
                return D[s, pl.ds(x + 1 + dx, n), y + 1 + dy]
            return D[s, x + 1 + dx, pl.ds(y + 1 + dy, n)]

        v = near(0, 0)
        shape = (n, 8, 128)
        k, z = iota(shape, 1), iota(shape, 2)
        ends = ((k == 0) & (z == 0)) | ((k == 7) & (z == 127))
        fix = jnp.concatenate(
            [
                jnp.broadcast_to(
                    FR[pl.ds(x * 16 + y + u * (16 if along_x else 1), 1), :], (8, 128)
                )[None]
                for u in range(n)
            ],
            axis=0,
        )
        return (
            (KEEP * v + BB[at])
            + (AXL[at] * near(-1, 0) + AXH[at] * near(1, 0))
            + (AYL[at] * near(0, -1) + AYH[at] * near(0, 1))
            + (AZL[at] * z_below(v) + AZH[at] * z_above(v))
            + jnp.where(ends, fix, 0.0)
        )

    def beyond(s):
        shape = (4, 16, 128)
        y, z = iota(shape, 1), iota(shape, 2)

        def each_y(ref, part):
            return jnp.concatenate(
                [
                    jnp.broadcast_to(ref[pl.ds(part * 4 + u, 1), :], (16, 128))[None]
                    for u in range(4)
                ],
                axis=0,
            )

        for part in range(4):
            rows = pl.ds(part * 64, 64)
            e = E[s, rows].reshape(shape)
            if part == 0:
                left = jnp.concatenate([EX[s, 0], E[s, pl.ds(0, 48)]], axis=0)
            else:
                left = E[s, pl.ds(part * 64 - 16, 64)]
            if part == 3:
                right = jnp.concatenate([E[s, pl.ds(208, 48)], EX[s, 1]], axis=0)
            else:
                right = E[s, pl.ds(part * 64 + 16, 64)]
            a = [AE[n, rows].reshape(shape) for n in range(7)]
            m = FA[rows].reshape(shape)
            new = (
                (KEEP * e + a[6])
                + (a[0] * left.reshape(shape) + a[1] * right.reshape(shape))
                + (
                    a[2] * jnp.where(y == 0, each_y(EY.at[s, 0], part), pltpu.roll(e, 1, 1))
                    + a[3] * jnp.where(y == 15, each_y(EY.at[s, 1], part), pltpu.roll(e, 15, 1))
                )
                + (
                    a[4] * jnp.where(z == 0, pltpu.roll(m, 1, 2), pltpu.roll(e, 1, 2))
                    + a[5] * jnp.where(z == 127, pltpu.roll(m, 127, 2), pltpu.roll(e, 127, 2))
                )
            )
            E[s + 1, rows] = new.reshape(64, 128)
        EYS[s + 1, 0] = E2[pl.ds((s + 1) * 256, 16, stride=16), :]
        EYS[s + 1, 1] = E2[pl.ds((s + 1) * 256 + 15, 16, stride=16), :]

    gy_lo, gy_hi = {"gy": lax.max(j - 1, 0)}, {"gy": lax.min(j + 1, 3)}

    def planes_of(s):
        ss, rs = sws.at[s], swr.at[s]
        return (
            [
                rdma(D.at[s, 1, inner], D.at[s, 17, inner], ss.at[2], rs.at[2], {"gx": i_lo}),
                rdma(D.at[s, 16, inner], D.at[s, 0, inner], ss.at[3], rs.at[3], {"gx": i_hi}),
            ],
            rdma(D.at[s, inner, 1], D.at[s, inner, 17], ss.at[0], rs.at[0], gy_lo),
            rdma(D.at[s, inner, 16], D.at[s, inner, 0], ss.at[1], rs.at[1], gy_hi),
        )

    def e_of(s):
        ss, rs = sws.at[s], swr.at[s]
        return (
            [
                rdma(E.at[s, pl.ds(0, 16)], EX.at[s, 1], ss.at[4], rs.at[4], {"gx": i_lo}),
                rdma(E.at[s, pl.ds(240, 16)], EX.at[s, 0], ss.at[5], rs.at[5], {"gx": i_hi}),
            ],
            rdma(EYS.at[s, 0], EY.at[s, 1], ss.at[6], rs.at[6], gy_lo),
            rdma(EYS.at[s, 1], EY.at[s, 0], ss.at[7], rs.at[7], gy_hi),
        )

    def put_d(s):
        def put(x, y, new, along_x=False):
            n = new.shape[0]
            if along_x:
                D[s, pl.ds(x + 1, n), y + 1] = new
            else:
                D[s, x + 1, pl.ds(y + 1, n)] = new

        return put

    OUT2 = OUT.reshape(2048, 128)

    def put_out(x, y, new, along_x=False):
        for u in range(new.shape[0]):
            xu, yu = (x + u, y) if along_x else (x, y + u)
            row = xu * 128 + yu // 8 * 64 + yu % 8
            OUT2[pl.ds(row, 8, stride=8), :] = new[u]

    def inside(s, put):
        def body(x, _):
            for y in (1, 8):
                put(x, y, columns(s, x, y, 7))
            return 0

        lax.fori_loop(1, 15, body, 0)

    def y_planes(s, put):
        def body(g, _):
            for y in (0, 15):
                put(g * 4, y, columns(s, g * 4, y, 4, True), True)
            return 0

        lax.fori_loop(0, 4, body, 0)

    def x_planes(s, put):
        for x in (0, 15):
            for y in (1, 8):
                put(x, y, columns(s, x, y, 7))

    faces(0)
    inside(0, put_d(1))
    vx_lo.wait_recv()
    vx_hi.wait_recv()
    for n, big, at in ((0, 3, 0), (1, 0, 17)):
        tile = VX[n]
        for row in range(1, 5):
            t = cell(tile, big, row)
            for y in range(row * 4 - 3, row * 4 + 1):
                D[0, at, y] = t

    def e_send(s):
        x_e, down_e, up_e = e_of(s)
        for c in x_e:
            c.start()

        @pl.when(j > 0)
        def _():
            down_e.start()

        @pl.when(j < NGY - 1)
        def _():
            up_e.start()

    def e_wait(s):
        x_e, down_e, up_e = e_of(s)
        for c in x_e:
            c.wait()

        @pl.when(j > 0)
        def _():
            down_e.wait_send()
            up_e.wait_recv()

        @pl.when(j < NGY - 1)
        def _():
            up_e.wait_send()
            down_e.wait_recv()

    def planes(s):
        x_d, down_d, up_d = planes_of(s + 1)
        y_planes(s, put_d(s + 1))

        @pl.when(j > 0)
        def _():
            down_d.start()

        @pl.when(j < NGY - 1)
        def _():
            up_d.start()

        x_planes(s, put_d(s + 1))
        for c in x_d:
            c.start()

    def planes_wait(s):
        x_d, down_d, up_d = planes_of(s + 1)

        @pl.when(j > 0)
        def _():
            down_d.wait_send()
            up_d.wait_recv()

        @pl.when(j < NGY - 1)
        def _():
            up_d.wait_send()
            down_d.wait_recv()

        for c in x_d:
            c.wait()

    def ends_wait():
        for c in ends_s:
            c.wait_recv()
        for part in range(4):
            for n in range(6):
                at = part * 32 + n * 4
                AE[n, pl.ds(part * 64, 64)] = jnp.where(
                    lane64 < 4,
                    pltpu.roll(RA[1], (128 - at) % 128, 1) if at else RA[1],
                    jnp.where(lane64 >= 124, pltpu.roll(RA[0], 124 - at, 1), 0.0),
                )
        for g in range(32):
            up = pltpu.roll(RB[1], (128 - g * 4) % 128, 1) if g else RB[1]
            down = pltpu.roll(RB[0], 124 - g * 4, 1) if g < 31 else RB[0]
            AE[6, pl.ds(g * 8, 8)] = jnp.where(
                lane < 4, up, jnp.where(lane >= 124, down, 0.0)
            )

    planes(0)
    ends_wait()
    for c in (ex_lo, ex_hi):
        c.wait_recv()
    beyond(0)
    e_send(1)
    faces(1)
    inside(1, put_d(2))
    planes_wait(0)
    planes(1)
    e_wait(1)
    beyond(1)
    e_send(2)
    faces(2)
    inside(2, put_d(3))
    planes_wait(1)
    planes(2)
    e_wait(2)
    beyond(2)
    faces(3)
    inside(3, put_out)
    some = pl.ds(1, 14)
    first_out = pltpu.make_async_copy(OUT.at[some], out_hbm.at[some], lsem.at[0])
    first_out.start()
    planes_wait(2)
    first_out.wait()
    y_planes(3, put_out)
    last_out = [
        pltpu.make_async_copy(OUT.at[at], out_hbm.at[at], lsem.at[n])
        for n, at in ((1, (some, 0, slice(None), 0)), (2, (some, 1, slice(None), 7)), (3, 0), (4, 15))
    ]
    for c in last_out[:2]:
        c.start()
    x_planes(3, put_out)
    for c in last_out[2:]:
        c.start()

    for c in last_out + [bhp_copy]:
        c.wait()
    for c in sends + xs + ends_s + [zc_lo, zc_hi, vx_lo, vx_hi, ex_lo, ex_hi]:
        c.wait_send()

    @pl.when(j > 0)
    def _():
        for c in y_down:
            c.wait_send()

    @pl.when(j < NGY - 1)
    def _():
        for c in y_up:
            c.wait_send()


def tiles(a):
    return a.reshape(16, 2, 8, 8, 128).transpose(0, 1, 3, 2, 4)


def per_device(
    pressure,
    pressure_old,
    accumulation,
    permeability,
    comp_block,
    comp_owner,
    comp_well,
    comp_wi,
    well_rate,
    well_storage,
    well_bhp_old,
):
    perm = permeability.reshape(3, 16, 2, 8, 8, 128).transpose(0, 1, 2, 4, 3, 5)
    hbm = pl.BlockSpec(memory_space=pltpu.HBM)
    grid = (16, 16, 8, 128)
    dma = pltpu.SemaphoreType.DMA

    def vm(*shape):
        return pltpu.VMEM(shape, F32)

    out, bhp = pl.pallas_call(
        kernel,
        out_shape=(
            jax.ShapeDtypeStruct((16, 2, 8, 8, 128), F32),
            jax.ShapeDtypeStruct((1, 8), F32),
        ),
        in_specs=[hbm] * 11,
        out_specs=(hbm, hbm),
        scratch_shapes=[
            pltpu.SMEM((1, 128), jnp.int32),
            pltpu.VMEM((1, 128), jnp.int32),
            pltpu.VMEM((1, 128), jnp.int32),
            pltpu.VMEM((1, 128), jnp.int32),
            vm(128, 128),
            vm(1, 8),
            vm(1, 8),
            vm(1, 8),
            vm(1, 8),
            vm(16, 2, 8, 8, 128),
            vm(18, 18, 8, 128),
            vm(*grid),
            vm(*grid),
            vm(18, 16, 8, 128),
            vm(16, 18, 8, 128),
            vm(*grid),
            vm(17, 16, 8, 128),
            vm(16, 17, 8, 128),
            vm(*grid),
            vm(*grid),
            vm(*grid),
            vm(*grid),
            vm(*grid),
            vm(*grid),
            vm(*grid),
            vm(*grid),
            vm(*grid),
            vm(*grid),
            vm(4, 18, 18, 8, 128),
            vm(16, 2, 8, 8, 128),
            pltpu.VMEM((16, 128, 128), jnp.bfloat16),
            vm(128, 128),
            vm(8, 128),
            vm(8, 8, 128),
            vm(8, 8, 128),
            vm(256, 128),
            vm(256, 128),
            vm(2, 8, 128),
            vm(2, 8, 128),
            vm(2, 64, 128),
            vm(2, 64, 128),
            vm(2, 8, 128),
            vm(2, 8, 128),
            vm(7, 256, 128),
            vm(4, 256, 128),
            vm(4, 2, 16, 128),
            vm(4, 2, 16, 128),
            vm(4, 2, 16, 128),
            vm(256, 128),
            vm(256, 128),
            vm(256, 128),
            vm(16, 8, 128),
            vm(8, 16, 8, 128),
            vm(8, 128),
            vm(8, 128),
            vm(3, 4, 8, 128),
            vm(3, 4, 8, 128),
            vm(8, 128),
            vm(2, 8, 128),
            dma((16,)),
            dma((8,)),
            dma((8,)),
            dma((8,)),
            dma((8,)),
            dma((10,)),
            dma((10,)),
            dma((11,)),
            dma((3, 4)),
            dma((11,)),
            dma((3, 4)),
            dma((2,)),
            dma((2,)),
            dma((4,)),
            dma((4,)),
            dma((4, 8)),
            dma((4, 8)),
        ],
        compiler_params=pltpu.CompilerParams(
            collective_id=0, has_side_effects=True, vmem_limit_bytes=60 * 1024 * 1024
        ),
    )(
        tiles(pressure),
        tiles(pressure_old),
        tiles(accumulation),
        perm,
        comp_block.reshape(1, 128),
        comp_owner.reshape(1, 128),
        comp_well.reshape(1, 128),
        comp_wi.reshape(128, 128),
        well_rate.reshape(1, 8),
        well_storage.reshape(1, 8),
        well_bhp_old.reshape(1, 8),
    )
    delta = out.transpose(0, 1, 3, 2, 4).reshape(16, 16, 1024)
    return pressure + delta, bhp.reshape(1, 1, 1, 8)


def solution(mesh):
    return jax.shard_map(
        per_device,
        mesh=mesh,
        in_specs=(
            P("gx", "gy", "grp"),
            P("gx", "gy", "grp"),
            P("gx", "gy", "grp"),
            P(None, "gx", "gy", "grp"),
            P("gx", "gy", "grp", None),
            P("gx", "gy", "grp", None, None),
            P("gx", "gy", "grp", None),
            P("gx", "gy", "grp", None, None),
            P("gx", "gy", "grp", None),
            P("gx", "gy", "grp", None),
            P("gx", "gy", "grp", None),
        ),
        out_specs=(P("gx", "gy", "grp"), P("gx", "gy", "grp", None)),
        check_vma=False,
    )
```

```python
import jax
import jax.numpy as jnp
from jax import lax
from jax.experimental import pallas as pl
from jax.experimental.pallas import tpu as pltpu
from jax.sharding import PartitionSpec as P

MESH = pl.DeviceIdType.MESH
F32 = jnp.float32
RELAX = 0.7
KEEP = 1.0 - RELAX
NGX, NGY, NGRP = 8, 4, 8
FAR_FIRST = (3, 5, 1, 7, 4, 2, 6)
HIGH = lax.Precision.HIGHEST


def iota(shape, dim):
    return lax.broadcasted_iota(jnp.int32, shape, dim)


def nt(a, b):
    return lax.dot_general(
        a, b, (((1,), (1,)), ((), ())), precision=HIGH, preferred_element_type=F32
    )


def exact(a, onehot, dim):
    hi = a.astype(jnp.bfloat16).astype(F32)
    mid = (a - hi).astype(jnp.bfloat16).astype(F32)
    parts = jnp.concatenate([hi, mid, a - hi - mid], axis=0).astype(jnp.bfloat16)
    out = lax.dot_general(
        parts, onehot, (((1,), (dim,)), ((), ())), preferred_element_type=F32
    )
    return (out[0:8] + out[8:16]) + out[16:24]


def rcp(x):
    r = pl.reciprocal(x, approx=True)
    return r * (2.0 - x * r)


def harm(a, b):
    return 2.0 * a * b * rcp(a + b)


def z_below(v):
    r = pltpu.roll(v, 1, 2)
    return jnp.where(iota(v.shape, 2) == 0, pltpu.roll(r, 1, 1), r)


def z_above(v):
    r = pltpu.roll(v, 127, 2)
    return jnp.where(iota(v.shape, 2) == 127, pltpu.roll(r, 7, 1), r)


def kernel(
    p_hbm,
    po_hbm,
    ac_hbm,
    k_hbm,
    cb_hbm,
    ow_hbm,
    cw_hbm,
    wi_hbm,
    rate_hbm,
    stor_hbm,
    old_hbm,
    out_hbm,
    bhp_hbm,
    cb_s,
    cb_v,
    ow_v,
    cw_v,
    wi_v,
    rate_v,
    stor_v,
    old_v,
    bhp_out,
    PG,
    PP,
    PO,
    AC,
    KX,
    KY,
    KZ,
    TX,
    TY,
    TZL,
    TZH,
    AXL,
    AXH,
    AYL,
    AYH,
    AZL,
    AZH,
    CC,
    BB,
    D,
    OUT,
    OH,
    PR,
    OWN,
    W1,
    W2,
    HZP,
    HZK,
    ZS0,
    ZI,
    SA,
    RA,
    SB,
    RB,
    AE,
    E,
    EX,
    EY,
    EYS,
    FA,
    AR,
    FR,
    UU,
    CQ,
    CSO,
    CBO,
    CS,
    CB,
    VO,
    VX,
    lsem,
    a1s,
    a1r,
    a2s,
    a2r,
    ihs,
    ihr,
    css,
    csr,
    cbs,
    cbr,
    vxs,
    vxr,
    ras,
    rar,
    sws,
    swr,
):
    i = lax.axis_index("gx")
    j = lax.axis_index("gy")
    l = lax.axis_index("grp")
    i_lo, i_hi = lax.rem(i + NGX - 1, NGX), lax.rem(i + 1, NGX)
    l_lo, l_hi = lax.rem(l + NGRP - 1, NGRP), lax.rem(l + 1, NGRP)

    def rdma(src, dst, ss, rs, dev):
        return pltpu.make_async_remote_copy(
            src_ref=src, dst_ref=dst, send_sem=ss, recv_sem=rs, device_id=dev, device_id_type=MESH
        )

    bar = pltpu.get_barrier_semaphore()

    def greet(dev):
        pl.semaphore_signal(bar, inc=1, device_id=dev, device_id_type=MESH)

    for dz in (0, 2, 1):
        for dj in range(1, NGY):
            greet({"gy": lax.rem(j + dj, NGY), "grp": lax.rem(l + dz + NGRP - 1, NGRP)})
    for d in FAR_FIRST:
        greet({"grp": lax.rem(l + d, NGRP)})
    for d in range(1, NGX):
        greet({"gx": lax.rem(i + d, NGX)})

    load_g = pltpu.make_async_copy(p_hbm, PG, lsem.at[0])
    load_g.start()
    small = [
        pltpu.make_async_copy(src, dst, lsem.at[7 + n])
        for n, (src, dst) in enumerate(
            (
                (cb_hbm, cb_s),
                (wi_hbm, wi_v),
                (cb_hbm, cb_v),
                (ow_hbm, ow_v),
                (cw_hbm, cw_v),
                (rate_hbm, rate_v),
                (stor_hbm, stor_v),
                (old_hbm, old_v),
            )
        )
    ]
    for c in small:
        c.start()

    def load_kz(ys, _):
        for yt in range(2):
            pltpu.make_async_copy(
                k_hbm.at[2, :, yt, :, ys, :], KZ.at[:, yt * 8 + ys], lsem.at[4]
            ).start()
        return 0

    lax.fori_loop(0, 8, load_kz, 0)

    def load(ys, _):
        for yt in range(2):
            y = yt * 8 + ys
            pltpu.make_async_copy(
                p_hbm.at[:, yt, :, ys, :], PP.at[pl.ds(1, 16), 1 + y], lsem.at[1]
            ).start()
            pltpu.make_async_copy(
                k_hbm.at[0, :, yt, :, ys, :], KX.at[pl.ds(1, 16), y], lsem.at[2]
            ).start()
            pltpu.make_async_copy(
                k_hbm.at[1, :, yt, :, ys, :], KY.at[:, 1 + y], lsem.at[3]
            ).start()
            pltpu.make_async_copy(po_hbm.at[:, yt, :, ys, :], PO.at[:, y], lsem.at[5]).start()
            pltpu.make_async_copy(ac_hbm.at[:, yt, :, ys, :], AC.at[:, y], lsem.at[6]).start()
        return 0

    lax.fori_loop(0, 8, load, 0)

    for c in small:
        c.wait()
    load_g.wait()

    def gather(g, _):
        for u in range(8):
            b = cb_s[0, g * 8 + u]
            x, y, k = b // 128, lax.rem(b // 8, 16), lax.rem(b, 8)
            PR[pl.ds(g * 8 + u, 1), :] = PG[x, y // 8, k, pl.ds(lax.rem(y, 8), 1), :]
        return 0

    lax.fori_loop(0, 16, gather, 0)
    wi = wi_v[...]
    sub = iota((8, 128), 0)
    lane = iota((8, 128), 1)
    sub128 = iota((128, 128), 0)
    lane128 = iota((128, 128), 1)
    ones8 = jnp.ones((8, 128), F32)
    weighted = nt(ones8, wi * PR[...])
    total = nt(ones8, wi)
    cb = cb_v[...]
    q = ow_v[...] * 8 + cw_v[...]
    q_hi, q_lo = q // 128, lax.rem(q, 128)
    pick = (sub128 == q_lo).astype(F32).astype(jnp.bfloat16)
    share = exact(
        jnp.where(sub == q_hi, weighted, 0.0) + jnp.where(sub == q_hi + 4, total, 0.0), pick, 1
    )
    own = i * NGRP + l
    own_row, shift = own // 16, lax.rem(own, 16) * 8
    OWN[...] = jnp.zeros((8, 128), F32)
    OWN[0:1, 0:8] = stor_v[...] * old_v[...] - rate_v[...]
    OWN[1:2, 0:8] = stor_v[...]
    placed = pltpu.roll(OWN[...], shift, 1)
    share = (
        share
        + jnp.where(sub == own_row, placed[0:1], 0.0)
        + jnp.where(sub == own_row + 4, placed[1:2], 0.0)
    )
    W1[i] = share

    lane64 = iota((64, 128), 1)

    def end_rows(ref, part, k, base, width):
        return jnp.concatenate(
            [
                ref[pl.ds(base + (part * 4 + u) * width * 8 + k, 16, stride=8), :]
                for u in range(4)
            ],
            axis=0,
        )

    KZ2 = KZ.reshape(2048, 128)

    def flat(ref):
        ref2 = ref.reshape(2048, 128)
        return (
            lambda part: end_rows(ref2, part, 0, 0, 16),
            lambda part: end_rows(ref2, part, 7, 0, 16),
        )

    def raw_rows(k):
        def rows(part):
            return jnp.concatenate(
                [PG[part * 4 + u, yt, k] for u in range(4) for yt in range(2)], axis=0
            )

        return rows

    def pack_tile(refs, lo_ref, hi_ref):
        keep = 4 if len(refs) == 1 else 1
        lo = hi = jnp.zeros((8, 128), F32)
        for part in range(4):
            for n, ends in enumerate(refs):
                a, b = ends[0](part), ends[1](part)
                for u in range(8):
                    to = part * 32 + u * 4 + n
                    at = slice(u * 8, u * 8 + 8)
                    a8 = jnp.where(lane < keep, a[at], 0.0)
                    b8 = jnp.where(lane >= 128 - keep, b[at], 0.0)
                    lo = lo + (pltpu.roll(a8, to, 1) if to else a8)
                    hi = hi + pltpu.roll(b8, (to + keep) % 128, 1)
        lo_ref[...] = lo
        hi_ref[...] = hi

    def pack_ends(refs, lo_ref, hi_ref):
        lo = hi = jnp.zeros((64, 128), F32)
        for part in range(4):
            for n, ends in enumerate(refs):
                to = part * 32 + n * 4
                a = jnp.where(lane64 < 4, ends[0](part), 0.0)
                b = jnp.where(lane64 >= 124, ends[1](part), 0.0)
                lo = lo + (pltpu.roll(a, to, 1) if to else a)
                hi = hi + pltpu.roll(b, to + 4, 1)
        lo_ref[...] = lo
        hi_ref[...] = hi

    pltpu.make_async_copy(KZ, KZ, lsem.at[4]).wait()
    pack_tile([(raw_rows(0), raw_rows(7)), flat(KZ)], ZS0.at[0], ZS0.at[1])


    pl.semaphore_wait(bar, 23)

    sends = []
    for d in range(1, NGX):
        c = rdma(W1.at[i], W1.at[i], a1s.at[d], a1r.at[i], {"gx": lax.rem(i + d, NGX)})
        c.start()
        sends.append(c)

    zc_lo = rdma(ZS0.at[0], ZI.at[1], ihs.at[0], ihr.at[0], {"grp": l_lo})
    zc_hi = rdma(ZS0.at[1], ZI.at[0], ihs.at[1], ihr.at[1], {"grp": l_hi})
    zc_lo.start()
    zc_hi.start()

    zplane = jnp.zeros((16, 8, 128), F32)

    @pl.when(j == 0)
    def _():
        PP[pl.ds(1, 16), 0] = zplane
        for s in range(1, 4):
            D[s, pl.ds(1, 16), 0] = zplane
            EY[s, 0] = jnp.zeros((16, 128), F32)

    @pl.when(j == NGY - 1)
    def _():
        PP[pl.ds(1, 16), 17] = zplane
        for s in range(1, 4):
            D[s, pl.ds(1, 16), 17] = zplane
            EY[s, 1] = jnp.zeros((16, 128), F32)

    inner = pl.ds(1, 16)
    pltpu.make_async_copy(KZ, KX.at[pl.ds(1, 16)], lsem.at[2]).wait()
    pltpu.make_async_copy(KZ, KY.at[:, pl.ds(1, 16)], lsem.at[3]).wait()
    pltpu.make_async_copy(KZ, PP.at[pl.ds(1, 16), pl.ds(1, 16)], lsem.at[1]).wait()
    xs = [
        rdma(KX.at[1], KX.at[17], ihs.at[2], ihr.at[2], {"gx": i_lo}),
        rdma(KX.at[16], KX.at[0], ihs.at[3], ihr.at[3], {"gx": i_hi}),
        rdma(PP.at[1, inner], PP.at[17, inner], ihs.at[4], ihr.at[4], {"gx": i_lo}),
        rdma(PP.at[16, inner], PP.at[0, inner], ihs.at[5], ihr.at[5], {"gx": i_hi}),
    ]
    for c in xs:
        c.start()
    y_down = [
        rdma(KY.at[:, 1], KY.at[:, 17], ihs.at[6], ihr.at[6], {"gy": lax.max(j - 1, 0)}),
        rdma(PP.at[inner, 1], PP.at[inner, 17], ihs.at[7], ihr.at[7], {"gy": lax.max(j - 1, 0)}),
    ]
    y_up = [
        rdma(KY.at[:, 16], KY.at[:, 0], ihs.at[8], ihr.at[8], {"gy": lax.min(j + 1, 3)}),
        rdma(PP.at[inner, 16], PP.at[inner, 0], ihs.at[9], ihr.at[9], {"gy": lax.min(j + 1, 3)}),
    ]

    @pl.when(j > 0)
    def _():
        for c in y_down:
            c.start()

    @pl.when(j < NGY - 1)
    def _():
        for c in y_up:
            c.start()

    def onehot(x, _):
        OH[x] = (sub128 + x * 128 == cb).astype(F32).astype(jnp.bfloat16)
        return 0

    lax.fori_loop(0, 16, onehot, 0)

    def halves(v):
        hi = v.astype(jnp.bfloat16)
        lo = (v - hi.astype(F32)).astype(jnp.bfloat16)
        return jnp.concatenate([hi, lo], axis=1)

    def blocks(x, n, parts):
        rows = OH[pl.ds(x, n)].reshape(n * 128, 128)
        r = jnp.dot(rows, parts, preferred_element_type=F32)
        return (r[:, :128] + r[:, 128:]).reshape(n, 16, 8, 128)

    wi_parts = halves(wi)

    CQ[...] = jnp.zeros((8, 16, 8, 128), F32)
    pltpu.make_async_copy(KZ, PO, lsem.at[5]).wait()
    pltpu.make_async_copy(KZ, AC, lsem.at[6]).wait()

    def prepare(x, _):
        w16 = blocks(x, 1, wi_parts)[0]
        for yt in range(2):
            y0 = yt * 8
            c8 = pl.ds(y0, 8)
            p = PP[x + 1, pl.ds(y0 + 1, 8)]
            acc = AC[x, c8]
            w = w16[y0 : y0 + 8]
            PO[x, c8] = acc * (p - PO[x, c8]) + w * p
            accw = acc + w
            AC[x, c8] = accw
            for yl in range(2):
                CQ[1, x // 4 * 4 + yt * 2 + yl] += accw[yl * 4 : yl * 4 + 4].sum(0)
            kz = KZ[x, c8]
            tzl = harm(z_below(kz), kz)
            TZL[x, c8] = tzl
            TZH[x, c8] = z_above(tzl)
            n = 8 - yt
            lower, upper = KY[x, pl.ds(y0 + 1, n)], KY[x, pl.ds(y0 + 2, n)]
            TY[x, pl.ds(y0 + 1, n)] = harm(lower, upper)
        return 0

    lax.fori_loop(0, 3, prepare, 0)

    for d in range(1, NGX):
        s = lax.rem(i + d, NGX)
        rdma(W1.at[i], W1.at[s], a1s.at[d], a1r.at[s], {"gx": s}).wait_recv()
    acc8 = W1[0]
    for s in range(1, NGX):
        acc8 = acc8 + W1[s]
    W2[l] = acc8
    for d in FAR_FIRST:
        c = rdma(W2.at[l], W2.at[l], a2s.at[d], a2r.at[l], {"grp": lax.rem(l + d, NGRP)})
        c.start()
        sends.append(c)

    lax.fori_loop(3, 16, prepare, 0)

    def faces_x(x, _):
        for yt in range(2):
            c8 = pl.ds(yt * 8, 8)
            TX[x, c8] = harm(KX[x, c8], KX[x + 1, c8])
        return 0

    lax.fori_loop(1, 16, faces_x, 0)

    for c in xs:
        c.wait_recv()

    @pl.when(j > 0)
    def _():
        for c in y_up:
            c.wait_recv()

    @pl.when(j < NGY - 1)
    def _():
        for c in y_down:
            c.wait_recv()

    @pl.when(i == 0)
    def _():
        KX[0] = zplane

    @pl.when(i == NGX - 1)
    def _():
        KX[17] = zplane

    @pl.when(j == 0)
    def _():
        KY[:, 0] = zplane

    @pl.when(j == NGY - 1)
    def _():
        KY[:, 17] = zplane

    for x in (0, 16):
        TX[x] = harm(KX[x], KX[x + 1])
    for y in (0, 16):
        TY[:, y] = harm(KY[:, y], KY[:, y + 1])
    zc_lo.wait_recv()
    zc_hi.wait_recv()
    has_lo = (l > 0).astype(F32)
    has_hi = (l < NGRP - 1).astype(F32)
    for g in range(32):
        for n, ref in enumerate((HZP, HZK)):
            lo = pltpu.roll(ZI[0], (128 - g * 4 - n) % 128, 1) if g + n else ZI[0]
            hi = pltpu.roll(ZI[1], 127 - g * 4 - n, 1)
            if n:
                lo, hi = lo * has_lo, hi * has_hi
            ref[pl.ds(g * 8, 8)] = jnp.where(lane == 0, lo, hi)

    for part in range(4):
        rows = pl.ds(part * 64, 64)
        k_end = jnp.where(
            lane64 < 64, end_rows(KZ2, part, 0, 0, 16), end_rows(KZ2, part, 7, 0, 16)
        )
        HZK[rows] = harm(k_end, HZK[rows])
    sh3 = (8, 8, 128)
    first = (iota(sh3, 2) == 0) & (iota(sh3, 1) == 0)
    last = (iota(sh3, 2) == 127) & (iota(sh3, 1) == 7)

    def column(ref, n):
        return jnp.concatenate(
            [jnp.broadcast_to(ref[pl.ds(n + u, 1), :], (8, 128))[None] for u in range(8)], axis=0
        )

    def operator(x, _):
        big = x // 4
        f_lo = (lax.rem(x, 4) == 0).astype(F32)
        f_hi = (lax.rem(x, 4) == 3).astype(F32)
        for yt in range(2):
            y0 = yt * 8
            c8 = pl.ds(y0, 8)
            txl, txh = TX[x, c8], TX[x + 1, c8]
            tyl, tyh = TY[x, c8], TY[x, pl.ds(y0 + 1, 8)]
            tk = column(HZK, x * 16 + y0)
            tzl = jnp.where(first, tk, TZL[x, c8])
            tzh = jnp.where(last, tk, TZH[x, c8])
            tsum = ((txl + txh) + (tyl + tyh)) + (tzl + tzh)
            p = PP[x + 1, pl.ds(y0 + 1, 8)]
            hp = column(HZP, x * 16 + y0)
            nb = (
                (txl * PP[x, pl.ds(y0 + 1, 8)] + txh * PP[x + 2, pl.ds(y0 + 1, 8)])
                + (tyl * PP[x + 1, c8] + tyh * PP[x + 1, pl.ds(y0 + 2, 8)])
                + (
                    tzl * jnp.where(first, hp, z_below(p))
                    + tzh * jnp.where(last, hp, z_above(p))
                )
            )
            r0 = PO[x, c8] + tsum * p - nb
            c = RELAX * rcp(AC[x, c8] + tsum)
            AXL[x, c8] = c * txl
            AXH[x, c8] = c * txh
            AYL[x, c8] = c * tyl
            AYH[x, c8] = c * tyh
            AZL[x, c8] = c * tzl
            AZH[x, c8] = c * tzh
            CC[x, c8] = c
            BB[x, c8] = -c * r0
            for yl in range(2):
                n = big * 4 + yt * 2 + yl
                part = slice(yl * 4, yl * 4 + 4)
                CQ[0, n] += r0[part].sum(0)
                CQ[2, n] += txl[part].sum(0) * f_lo
                CQ[3, n] += txh[part].sum(0) * f_hi
                CQ[4, n] += tyl[yl * 4]
                CQ[5, n] += tyh[yl * 4 + 3]
                CQ[6, n] += tzl[part].sum(0)
                CQ[7, n] += tzh[part].sum(0)
        return 0

    lax.fori_loop(0, 16, operator, 0)

    sh4 = (16, 8, 128)
    lane4 = iota(sh4, 2)
    place4 = lane4 == iota(sh4, 0) * 8 + iota(sh4, 1)

    def coarse_of(n):
        v = CQ[n]
        if n == 6:
            v = jnp.where(lane4 == 0, v, 0.0)
        if n == 7:
            v = jnp.where(lane4 == 127, v, 0.0)
        v = jnp.where(place4, jnp.sum(v, axis=2, keepdims=True), 0.0)
        return jnp.sum(v.sum(0), axis=0, keepdims=True)

    r_c, a_c, xl, xh, yl, yh, zl, zh = [coarse_of(n) for n in range(8)]
    scale = RELAX / (a_c + ((xl + xh) + (yl + yh)) + (zl + zh))
    lane1 = iota((1, 128), 1)
    CSO[...] = jnp.concatenate(
        [
            jnp.where(lane1 >= 32, scale * xl, 0.0),
            jnp.where(lane1 < 96, scale * xh, 0.0),
            scale * yl,
            scale * yh,
            scale * zl,
            scale * zh,
            scale,
            scale,
        ],
        axis=0,
    )
    peers = [(dj, dz) for dz in (0, 2, 1) for dj in range(NGY) if (dj, dz) != (0, 1)]

    def to_peers(own_ref, all_ref, ss, rs, count):
        rows = pl.ds(0, count)
        for n, (dj, dz) in enumerate(peers):
            dev = {"gy": lax.rem(j + dj, NGY), "grp": lax.rem(l + dz + NGRP - 1, NGRP)}
            to = all_ref.at[2 - dz, j, rows]
            c = rdma(own_ref.at[rows], to, ss.at[n], rs.at[2 - dz, j], dev)
            c.start()
            sends.append(c)

    def from_peers(own_ref, all_ref, ss, rs, count):
        rows = pl.ds(0, count)
        for n, (dj, dz) in enumerate(peers):
            s = lax.rem(j + dj, NGY)
            dev = {"gy": s, "grp": lax.rem(l + dz + NGRP - 1, NGRP)}
            to = all_ref.at[dz, s, rows]
            rdma(own_ref.at[rows], to, ss.at[n], rs.at[dz, s], dev).wait_recv()

    to_peers(CSO, CS, css, csr, 8)
    CS[1, j] = CSO[...]

    cx, cy, ck = cb // 128, lax.rem(cb // 8, 16), lax.rem(cb, 8)
    spot = (sub128 == (cx // 4) * 32 + (cy // 4) * 8 + ck).astype(F32).astype(jnp.bfloat16)

    for d in range(1, NGRP):
        s = lax.rem(l + d, NGRP)
        rdma(W2.at[l], W2.at[s], a2s.at[d], a2r.at[s], {"grp": s}).wait_recv()
    acc8 = W2[0]
    for s in range(1, NGRP):
        acc8 = acc8 + W2[s]
    bhp = jnp.where(sub < 4, acc8 / jnp.where(sub < 4, pltpu.roll(acc8, 4, 0), 1.0), 0.0)
    bhp_c = jnp.sum(
        jnp.where(sub == q_hi, exact(bhp, pick, 0), 0.0), axis=0, keepdims=True
    )

    CBO[...] = scale * (exact(total * bhp_c, spot, 1) - r_c)
    to_peers(CBO, CB, cbs, cbr, 1)
    CB[1, j] = CBO[...]
    mine = pltpu.roll(jnp.where(sub == own_row, bhp, 0.0), lax.rem(128 - shift, 128), 1)
    bhp_out[...] = jnp.sum(mine, axis=0, keepdims=True)[:, 0:8]
    bhp_copy = pltpu.make_async_copy(bhp_out, bhp_hbm, lsem.at[15])
    bhp_copy.start()

    ends_s = [
        rdma(SA.at[0], RA.at[1], ras.at[0], rar.at[0], {"grp": l_lo}),
        rdma(SA.at[1], RA.at[0], ras.at[1], rar.at[1], {"grp": l_hi}),
        rdma(SB.at[0], RB.at[1], ras.at[2], rar.at[2], {"grp": l_lo}),
        rdma(SB.at[1], RB.at[0], ras.at[3], rar.at[3], {"grp": l_hi}),
    ]
    pack_ends([flat(r) for r in (AXL, AXH, AYL, AYH, AZL, AZH)], SA.at[0], SA.at[1])
    ends_s[0].start()
    ends_s[1].start()
    AZL2, AZH2 = AZL.reshape(2048, 128), AZH.reshape(2048, 128)
    for part in range(4):
        AR[pl.ds(part * 64, 64)] = jnp.where(
            lane64 < 64, end_rows(AZL2, part, 0, 0, 16), end_rows(AZH2, part, 7, 0, 16)
        )

    bhp_col = jnp.sum(jnp.where(sub128 == lane128, bhp_c, 0.0), axis=1, keepdims=True)
    wb_parts = halves(wi * bhp_col)

    def finish(g, _):
        at = pl.ds(g * 4, 4)
        BB[at] = BB[at] + CC[at] * blocks(g * 4, 4, wb_parts)
        return 0

    lax.fori_loop(0, 4, finish, 0)
    pack_tile([flat(BB)], SB.at[0], SB.at[1])
    ends_s[2].start()
    ends_s[3].start()

    def joined(tile):
        block = lax.rem(lane, 32) // 8
        for g in range(NGY):
            for y in range(4):
                u = None
                for dz in range(3):
                    t = tile(dz, g)
                    to = (8 * (dz - y)) % 128
                    t = pltpu.roll(t, to, 1) if to else t
                    u = jnp.where(block == dz, t, 0.0 if u is None else u)
                UU[g * 4 + y] = u

    UU2 = UU.reshape(128, 128)
    from_peers(CSO, CS, css, csr, 8)
    joined(lambda dz, g: CS[dz, g])
    coef = [UU2[pl.ds(n, 16, stride=8), :] for n in range(6)]
    from_peers(CBO, CB, cbs, cbr, 1)
    joined(lambda dz, g: jnp.broadcast_to(CB[dz, g, 0:1], (8, 128)))
    rhs = UU2[pl.ds(0, 16, stride=8), :]

    def coarse_step(_, v):
        return (
            (KEEP * v + rhs)
            + (coef[0] * pltpu.roll(v, 32, 1) + coef[1] * pltpu.roll(v, 96, 1))
            + (coef[2] * pltpu.roll(v, 1, 0) + coef[3] * pltpu.roll(v, 15, 0))
            + (coef[4] * pltpu.roll(v, 1, 1) + coef[5] * pltpu.roll(v, 127, 1))
        )

    v = lax.fori_loop(0, 7, coarse_step, rhs)
    mine = jnp.zeros((8, 128), F32)
    for g in range(NGY):
        mine = jnp.where(j == g, pltpu.roll(v, (17 - 4 * g) % 16, 0)[0:8], mine)
    VO[...] = mine
    vx_lo = rdma(VO, VX.at[1], vxs.at[0], vxr.at[0], {"gx": i_lo})
    vx_hi = rdma(VO, VX.at[0], vxs.at[1], vxr.at[1], {"gx": i_hi})
    vx_lo.start()
    vx_hi.start()

    def cell(tile, big, row):
        t = jnp.where(lane == big * 32 + 8 + sub, tile[row : row + 1], 0.0)
        return jnp.broadcast_to(jnp.sum(t, axis=1, keepdims=True), (8, 128))

    for big in range(4):
        for row in range(6):
            t = cell(mine, big, row)
            ys = (0,) if row == 0 else (17,) if row == 5 else range(row * 4 - 3, row * 4 + 1)
            for x in range(4):
                for y in ys:
                    D[0, 1 + big * 4 + x, y] = t
    sub16 = iota((16, 128), 0)
    y_lo = y_hi = jnp.zeros((16, 128), F32)
    for big in range(4):
        lo, hi = [
            jnp.sum(jnp.where(lane == big * 32 + at, mine, 0.0), axis=1, keepdims=True)
            for at in (7, 16)
        ]
        e = jnp.where(lane < 64, hi, lo)
        rows = jnp.zeros((16, 128), F32)
        for y in range(4):
            rows = jnp.where(sub16 // 4 == y, e[y + 1 : y + 2], rows)
        for u in range(4):
            E[0, pl.ds((big * 4 + u) * 16, 16)] = rows
        y_lo = jnp.where(sub16 // 4 == big, e[0:1], y_lo)
        y_hi = jnp.where(sub16 // 4 == big, e[5:6], y_hi)
    EY[0, 0] = y_lo
    EY[0, 1] = y_hi
    ex_lo = rdma(E.at[0, pl.ds(0, 16)], EX.at[0, 1], sws.at[0, 4], swr.at[0, 4], {"gx": i_lo})
    ex_hi = rdma(E.at[0, pl.ds(240, 16)], EX.at[0, 0], sws.at[0, 5], swr.at[0, 5], {"gx": i_hi})
    ex_lo.start()
    ex_hi.start()
    D2 = D.reshape(4 * 18 * 18 * 8, 128)
    E2 = E.reshape(4 * 256, 128)

    def faces(s):
        for part in range(4):
            base = (s * 18 * 18 + 19) * 8
            rows = pl.ds(part * 64, 64)
            m = jnp.where(
                lane64 < 64, end_rows(D2, part, 0, base, 18), end_rows(D2, part, 7, base, 18)
            )
            FA[rows] = m
            d = E[s, rows] - m
            FR[rows] = AR[rows] * jnp.where(
                lane64 < 64, pltpu.roll(d, 1, 1), pltpu.roll(d, 127, 1)
            )

    def columns(s, x, y, n, along_x=False):
        at = (pl.ds(x, n), y) if along_x else (x, pl.ds(y, n))

        def near(dx, dy):
            if along_x:
                return D[s, pl.ds(x + 1 + dx, n), y + 1 + dy]
            return D[s, x + 1 + dx, pl.ds(y + 1 + dy, n)]

        v = near(0, 0)
        shape = (n, 8, 128)
        k, z = iota(shape, 1), iota(shape, 2)
        ends = ((k == 0) & (z == 0)) | ((k == 7) & (z == 127))
        fix = jnp.concatenate(
            [
                jnp.broadcast_to(
                    FR[pl.ds(x * 16 + y + u * (16 if along_x else 1), 1), :], (8, 128)
                )[None]
                for u in range(n)
            ],
            axis=0,
        )
        return (
            (KEEP * v + BB[at])
            + (AXL[at] * near(-1, 0) + AXH[at] * near(1, 0))
            + (AYL[at] * near(0, -1) + AYH[at] * near(0, 1))
            + (AZL[at] * z_below(v) + AZH[at] * z_above(v))
            + jnp.where(ends, fix, 0.0)
        )

    def beyond(s):
        shape = (4, 16, 128)
        y, z = iota(shape, 1), iota(shape, 2)

        def each_y(ref, part):
            return jnp.concatenate(
                [
                    jnp.broadcast_to(ref[pl.ds(part * 4 + u, 1), :], (16, 128))[None]
                    for u in range(4)
                ],
                axis=0,
            )

        for part in range(4):
            rows = pl.ds(part * 64, 64)
            e = E[s, rows].reshape(shape)
            if part == 0:
                left = jnp.concatenate([EX[s, 0], E[s, pl.ds(0, 48)]], axis=0)
            else:
                left = E[s, pl.ds(part * 64 - 16, 64)]
            if part == 3:
                right = jnp.concatenate([E[s, pl.ds(208, 48)], EX[s, 1]], axis=0)
            else:
                right = E[s, pl.ds(part * 64 + 16, 64)]
            a = [AE[n, rows].reshape(shape) for n in range(7)]
            m = FA[rows].reshape(shape)
            new = (
                (KEEP * e + a[6])
                + (a[0] * left.reshape(shape) + a[1] * right.reshape(shape))
                + (
                    a[2] * jnp.where(y == 0, each_y(EY.at[s, 0], part), pltpu.roll(e, 1, 1))
                    + a[3] * jnp.where(y == 15, each_y(EY.at[s, 1], part), pltpu.roll(e, 15, 1))
                )
                + (
                    a[4] * jnp.where(z == 0, pltpu.roll(m, 1, 2), pltpu.roll(e, 1, 2))
                    + a[5] * jnp.where(z == 127, pltpu.roll(m, 127, 2), pltpu.roll(e, 127, 2))
                )
            )
            E[s + 1, rows] = new.reshape(64, 128)
        EYS[s + 1, 0] = E2[pl.ds((s + 1) * 256, 16, stride=16), :]
        EYS[s + 1, 1] = E2[pl.ds((s + 1) * 256 + 15, 16, stride=16), :]

    gy_lo, gy_hi = {"gy": lax.max(j - 1, 0)}, {"gy": lax.min(j + 1, 3)}

    def planes_of(s):
        ss, rs = sws.at[s], swr.at[s]
        return (
            [
                rdma(D.at[s, 1, inner], D.at[s, 17, inner], ss.at[2], rs.at[2], {"gx": i_lo}),
                rdma(D.at[s, 16, inner], D.at[s, 0, inner], ss.at[3], rs.at[3], {"gx": i_hi}),
            ],
            rdma(D.at[s, inner, 1], D.at[s, inner, 17], ss.at[0], rs.at[0], gy_lo),
            rdma(D.at[s, inner, 16], D.at[s, inner, 0], ss.at[1], rs.at[1], gy_hi),
        )

    def e_of(s):
        ss, rs = sws.at[s], swr.at[s]
        return (
            [
                rdma(E.at[s, pl.ds(0, 16)], EX.at[s, 1], ss.at[4], rs.at[4], {"gx": i_lo}),
                rdma(E.at[s, pl.ds(240, 16)], EX.at[s, 0], ss.at[5], rs.at[5], {"gx": i_hi}),
            ],
            rdma(EYS.at[s, 0], EY.at[s, 1], ss.at[6], rs.at[6], gy_lo),
            rdma(EYS.at[s, 1], EY.at[s, 0], ss.at[7], rs.at[7], gy_hi),
        )

    def put_d(s):
        def put(x, y, new, along_x=False):
            n = new.shape[0]
            if along_x:
                D[s, pl.ds(x + 1, n), y + 1] = new
            else:
                D[s, x + 1, pl.ds(y + 1, n)] = new

        return put

    OUT2 = OUT.reshape(2048, 128)

    def put_out(x, y, new, along_x=False):
        for u in range(new.shape[0]):
            xu, yu = (x + u, y) if along_x else (x, y + u)
            row = xu * 128 + yu // 8 * 64 + yu % 8
            OUT2[pl.ds(row, 8, stride=8), :] = new[u]

    def inside(s, put):
        def body(x, _):
            for y in (1, 8):
                put(x, y, columns(s, x, y, 7))
            return 0

        lax.fori_loop(1, 15, body, 0)

    def y_planes(s, put):
        def body(g, _):
            for y in (0, 15):
                put(g * 8, y, columns(s, g * 8, y, 8, True), True)
            return 0

        lax.fori_loop(0, 2, body, 0)

    def x_planes(s, put):
        for x in (0, 15):
            for y in (1, 8):
                put(x, y, columns(s, x, y, 7))

    faces(0)
    inside(0, put_d(1))
    vx_lo.wait_recv()
    vx_hi.wait_recv()
    for n, big, at in ((0, 3, 0), (1, 0, 17)):
        tile = VX[n]
        for row in range(1, 5):
            t = cell(tile, big, row)
            for y in range(row * 4 - 3, row * 4 + 1):
                D[0, at, y] = t

    def e_send(s):
        x_e, down_e, up_e = e_of(s)
        for c in x_e:
            c.start()

        @pl.when(j > 0)
        def _():
            down_e.start()

        @pl.when(j < NGY - 1)
        def _():
            up_e.start()

    def e_wait(s):
        x_e, down_e, up_e = e_of(s)
        for c in x_e:
            c.wait()

        @pl.when(j > 0)
        def _():
            down_e.wait_send()
            up_e.wait_recv()

        @pl.when(j < NGY - 1)
        def _():
            up_e.wait_send()
            down_e.wait_recv()

    def planes(s):
        x_d, down_d, up_d = planes_of(s + 1)
        y_planes(s, put_d(s + 1))

        @pl.when(j > 0)
        def _():
            down_d.start()

        @pl.when(j < NGY - 1)
        def _():
            up_d.start()

        x_planes(s, put_d(s + 1))
        for c in x_d:
            c.start()

    def planes_wait(s):
        x_d, down_d, up_d = planes_of(s + 1)

        @pl.when(j > 0)
        def _():
            down_d.wait_send()
            up_d.wait_recv()

        @pl.when(j < NGY - 1)
        def _():
            up_d.wait_send()
            down_d.wait_recv()

        for c in x_d:
            c.wait()

    def ends_wait():
        for c in ends_s:
            c.wait_recv()
        for part in range(4):
            for n in range(6):
                at = part * 32 + n * 4
                AE[n, pl.ds(part * 64, 64)] = jnp.where(
                    lane64 < 4,
                    pltpu.roll(RA[1], (128 - at) % 128, 1) if at else RA[1],
                    jnp.where(lane64 >= 124, pltpu.roll(RA[0], 124 - at, 1), 0.0),
                )
        for g in range(32):
            up = pltpu.roll(RB[1], (128 - g * 4) % 128, 1) if g else RB[1]
            down = pltpu.roll(RB[0], 124 - g * 4, 1) if g < 31 else RB[0]
            AE[6, pl.ds(g * 8, 8)] = jnp.where(
                lane < 4, up, jnp.where(lane >= 124, down, 0.0)
            )

    planes(0)
    ends_wait()
    for c in (ex_lo, ex_hi):
        c.wait_recv()
    beyond(0)
    e_send(1)
    faces(1)
    inside(1, put_d(2))
    planes_wait(0)
    planes(1)
    e_wait(1)
    beyond(1)
    e_send(2)
    faces(2)
    inside(2, put_d(3))
    planes_wait(1)
    planes(2)
    e_wait(2)
    beyond(2)
    faces(3)
    inside(3, put_out)
    some = pl.ds(1, 14)
    first_out = pltpu.make_async_copy(OUT.at[some], out_hbm.at[some], lsem.at[0])
    first_out.start()
    planes_wait(2)
    first_out.wait()
    y_planes(3, put_out)
    last_out = [
        pltpu.make_async_copy(OUT.at[at], out_hbm.at[at], lsem.at[n])
        for n, at in ((1, (some, 0, slice(None), 0)), (2, (some, 1, slice(None), 7)), (3, 0), (4, 15))
    ]
    for c in last_out[:2]:
        c.start()
    x_planes(3, put_out)
    for c in last_out[2:]:
        c.start()

    for c in last_out + [bhp_copy]:
        c.wait()
    for c in sends + xs + ends_s + [zc_lo, zc_hi, vx_lo, vx_hi, ex_lo, ex_hi]:
        c.wait_send()

    @pl.when(j > 0)
    def _():
        for c in y_down:
            c.wait_send()

    @pl.when(j < NGY - 1)
    def _():
        for c in y_up:
            c.wait_send()


def tiles(a):
    return a.reshape(16, 2, 8, 8, 128).transpose(0, 1, 3, 2, 4)


def per_device(
    pressure,
    pressure_old,
    accumulation,
    permeability,
    comp_block,
    comp_owner,
    comp_well,
    comp_wi,
    well_rate,
    well_storage,
    well_bhp_old,
):
    perm = permeability.reshape(3, 16, 2, 8, 8, 128).transpose(0, 1, 2, 4, 3, 5)
    hbm = pl.BlockSpec(memory_space=pltpu.HBM)
    grid = (16, 16, 8, 128)
    dma = pltpu.SemaphoreType.DMA

    def vm(*shape):
        return pltpu.VMEM(shape, F32)

    out, bhp = pl.pallas_call(
        kernel,
        out_shape=(
            jax.ShapeDtypeStruct((16, 2, 8, 8, 128), F32),
            jax.ShapeDtypeStruct((1, 8), F32),
        ),
        in_specs=[hbm] * 11,
        out_specs=(hbm, hbm),
        scratch_shapes=[
            pltpu.SMEM((1, 128), jnp.int32),
            pltpu.VMEM((1, 128), jnp.int32),
            pltpu.VMEM((1, 128), jnp.int32),
            pltpu.VMEM((1, 128), jnp.int32),
            vm(128, 128),
            vm(1, 8),
            vm(1, 8),
            vm(1, 8),
            vm(1, 8),
            vm(16, 2, 8, 8, 128),
            vm(18, 18, 8, 128),
            vm(*grid),
            vm(*grid),
            vm(18, 16, 8, 128),
            vm(16, 18, 8, 128),
            vm(*grid),
            vm(17, 16, 8, 128),
            vm(16, 17, 8, 128),
            vm(*grid),
            vm(*grid),
            vm(*grid),
            vm(*grid),
            vm(*grid),
            vm(*grid),
            vm(*grid),
            vm(*grid),
            vm(*grid),
            vm(*grid),
            vm(4, 18, 18, 8, 128),
            vm(16, 2, 8, 8, 128),
            pltpu.VMEM((16, 128, 128), jnp.bfloat16),
            vm(128, 128),
            vm(8, 128),
            vm(8, 8, 128),
            vm(8, 8, 128),
            vm(256, 128),
            vm(256, 128),
            vm(2, 8, 128),
            vm(2, 8, 128),
            vm(2, 64, 128),
            vm(2, 64, 128),
            vm(2, 8, 128),
            vm(2, 8, 128),
            vm(7, 256, 128),
            vm(4, 256, 128),
            vm(4, 2, 16, 128),
            vm(4, 2, 16, 128),
            vm(4, 2, 16, 128),
            vm(256, 128),
            vm(256, 128),
            vm(256, 128),
            vm(16, 8, 128),
            vm(8, 16, 8, 128),
            vm(8, 128),
            vm(8, 128),
            vm(3, 4, 8, 128),
            vm(3, 4, 8, 128),
            vm(8, 128),
            vm(2, 8, 128),
            dma((16,)),
            dma((8,)),
            dma((8,)),
            dma((8,)),
            dma((8,)),
            dma((10,)),
            dma((10,)),
            dma((11,)),
            dma((3, 4)),
            dma((11,)),
            dma((3, 4)),
            dma((2,)),
            dma((2,)),
            dma((4,)),
            dma((4,)),
            dma((4, 8)),
            dma((4, 8)),
        ],
        compiler_params=pltpu.CompilerParams(
            collective_id=0, has_side_effects=True, vmem_limit_bytes=60 * 1024 * 1024
        ),
    )(
        tiles(pressure),
        tiles(pressure_old),
        tiles(accumulation),
        perm,
        comp_block.reshape(1, 128),
        comp_owner.reshape(1, 128),
        comp_well.reshape(1, 128),
        comp_wi.reshape(128, 128),
        well_rate.reshape(1, 8),
        well_storage.reshape(1, 8),
        well_bhp_old.reshape(1, 8),
    )
    delta = out.transpose(0, 1, 3, 2, 4).reshape(16, 16, 1024)
    return pressure + delta, bhp.reshape(1, 1, 1, 8)


def solution(mesh):
    return jax.shard_map(
        per_device,
        mesh=mesh,
        in_specs=(
            P("gx", "gy", "grp"),
            P("gx", "gy", "grp"),
            P("gx", "gy", "grp"),
            P(None, "gx", "gy", "grp"),
            P("gx", "gy", "grp", None),
            P("gx", "gy", "grp", None, None),
            P("gx", "gy", "grp", None),
            P("gx", "gy", "grp", None, None),
            P("gx", "gy", "grp", None),
            P("gx", "gy", "grp", None),
            P("gx", "gy", "grp", None),
        ),
        out_specs=(P("gx", "gy", "grp"), P("gx", "gy", "grp", None)),
        check_vma=False,
    )
```
